32 devices in a mesh: section: 4 (over y, core), dp: 8 (over z, x).
Axes of the slice: x: 2, y: 2, z: 4, core: 2. Of those that a mesh axis runs over, the one named last changes fastest.
Arguments:
- tokens: bfloat16 [32, 4, 512, 512], P('dp', 'section'), may hold values from -6 to 6
- doc_ids: int32 [32, 4, 512], P('dp', 'section'), may hold values from 0 to 3, never falling along the last dimension, each value on 1 to 256 neighbouring positions
- reset_flags: int32 [32, 4], P('dp', 'section'), may hold values from 0 to 1, as said below
- attn_gain: bfloat16 [512], replicated, may hold values from 0.5 to 1.5
- w_qkv: bfloat16 [512, 1536], replicated, may hold values from -0.25 to 0.25
- w_attn_out: bfloat16 [512, 512], replicated, may hold values from -0.75 to 0.75
- ffn_gain: bfloat16 [512], replicated, may hold values from 0.5 to 1.5
- w_in: bfloat16 [512, 2048], replicated, may hold values from -0.25 to 0.25
- w_out: bfloat16 [2048, 512], replicated, may hold values from -0.1875 to 0.1875
- write_gain: bfloat16 [512], replicated, may hold values from 0.5 to 1.5
- w_write: bfloat16 [512, 1536], replicated, may hold values from -0.25 to 0.25
- w_write_out: bfloat16 [512, 512], replicated, may hold values from -1 to 1
- init_memory: bfloat16 [64, 512], replicated, may hold values from -6 to 6
- out_grad: bfloat16 [32, 4, 512, 512], P('dp', 'section'), may hold values from -6 to 6
- memory_grad: bfloat16 [32, 4, 64, 512], P('dp', 'section'), may hold values from -6 to 6
Outputs:
- encoded: bfloat16 [32, 4, 512, 512], P('dp', 'section')
- memories: bfloat16 [32, 4, 64, 512], P('dp', 'section')
- tokens_grad: float32 [32, 4, 512, 512], P('dp', 'section')
- attn_gain_grad: float32 [512], replicated
- w_qkv_grad: float32 [512, 1536], replicated
- w_attn_out_grad: float32 [512, 512], replicated
- ffn_gain_grad: float32 [512], replicated
- w_in_grad: float32 [512, 2048], replicated
- w_out_grad: float32 [2048, 512], replicated
- write_gain_grad: float32 [512], replicated
- w_write_grad: float32 [512, 1536], replicated
- w_write_out_grad: float32 [512, 512], replicated
- init_memory_grad: float32 [64, 512], replicated
The draws below stay inside these ranges and needn't reach their ends.
Inputs may be any that keep to these rules, and one draw needn't show every extreme that they name: `reset_flags`: the first segment of every stream has flag 1; among the 4 streams of each index of dp one has no other flag.
All inputs are finite; a program needn't handle non-finite values.
Results may differ from the reference program's by a relative error of at most 0.014.
Values may be sent and summed in bfloat16 or wider, within the bound.
No kernel may reach another device: no remote copies, remote signals or barrier semaphores. Data moves between devices by JAX's collectives and lax.ppermute only.
A program may use at most 256 MiB of HBM per device.

```python
import math
import jax
import jax.numpy as jnp
import numpy as np
from jax import lax

D = 512
HEADS = 8
FF = 2048
SLOTS = 64
HEAD_DIM = 64
SEG = 512
MB = 4
STREAMS = 32
SEGS = 4


def draw_reset_flags(key, part):
    key = jax.random.fold_in(key, 11)
    first_key, second_key = jax.random.split(key)
    flags = (jax.random.randint(first_key, (STREAMS, SEGS), 0, 4) == 0).astype(jnp.int32)
    chosen = jax.random.randint(second_key, (STREAMS // MB,), 0, MB)
    position = jnp.arange(STREAMS) % MB
    cleared = position == jnp.repeat(chosen, MB)
    flags = jnp.where(cleared[:, None], 0, flags)
    flags = flags.at[:, 0].set(1)
    return flags.astype(jnp.int32)


def block_levels(stream_key, shape, shards, smallest, top_value):
    def one(axis_at, blocks):
        steps = jax.random.uniform(jax.random.fold_in(jax.random.fold_in(stream_key, 6), axis_at), (blocks,), jnp.float32, smallest / len(shards), top_value / len(shards))
        return jnp.repeat(jnp.exp(steps), shape[axis_at] // blocks).reshape((-1,) + (1,) * (len(shape) - axis_at - 1))

    level = one(*shards[0])
    for cut in shards[1:]:
        level = level * one(*cut)
    return level


def split_up(count, total, most, slope):
    weights = [(1 << 20) // math.isqrt(grade ** slope) + 1 for grade in range(2, count + 1)]
    rest, holding = total - most - (count - 1), [1] * (count - 1)
    while rest > 0:
        movable = [i for i in range(count - 1) if holding[i] < most]
        pool, left = sum([weights[i] for i in movable]), rest
        for i in movable:
            more = min(most - holding[i], max(1, left * weights[i] // pool), rest)
            holding[i] = holding[i] + more
            rest = rest - more
    return np.array([most] + holding)


def ragged_sizes(own_key, number_of, total, most, slope):
    if number_of == 2:
        one = jax.random.randint(own_key, (), max(1, total - most), min(most, total - 1) + 1)
        return jnp.stack([one, total - one])
    sizes = jnp.asarray(split_up(number_of, total, most, slope), jnp.int32)
    couples = (number_of - 1) // 2
    giver, sink = sizes[1:1 + 2 * couples:2], sizes[2:2 + 2 * couples:2]
    room = jnp.minimum(giver - 1, most - sink)
    shifted = jax.random.randint(jax.random.fold_in(own_key, 1), (couples,), 0, 1 << 20) % (room + 1)
    sizes = sizes.at[1:1 + 2 * couples:2].set(giver - shifted).at[2:2 + 2 * couples:2].set(sink + shifted)
    return sizes[jax.random.permutation(jax.random.fold_in(own_key, 2), number_of)]


def noise(key, dims, scale, bound, pieces=(), kind=jnp.bfloat16):
    values = scale * jax.random.normal(key, dims, jnp.float32)
    if pieces:
        values = values * block_levels(key, dims, pieces, -0.22, 0.18)
    return jnp.clip(values, -bound, bound).astype(kind)


def setup_inputs(seed: int = 0) -> dict:
    streams_of = jax.random.split(jax.random.key(seed), 16)
    tokens = noise(streams_of[0], (STREAMS, SEGS, SEG, D), 1.0, 6.0, ((0, 8), (1, 4)))
    doc_ids = jax.vmap(lambda own: jnp.searchsorted(jnp.cumsum(ragged_sizes(own, 4, SEG, SEG // 2, 0)), jnp.arange(SEG), side="right"))(jax.random.split(streams_of[1], STREAMS * SEGS)).reshape((STREAMS, SEGS, SEG)).astype(jnp.int32)
    reset_flags = draw_reset_flags(jax.random.fold_in(streams_of[15], 71), 0)
    attn_gain = jnp.clip(1.0 + 0.1 * jax.random.normal(streams_of[3], (D,), jnp.float32), 0.5, 1.5).astype(jnp.bfloat16)
    w_qkv = noise(streams_of[4], (D, 3 * D), D ** -0.5, 0.25)
    w_attn_out = noise(streams_of[5], (D, D), (D // 8) ** -0.5, 0.75)
    ffn_gain = jnp.clip(1.0 + 0.1 * jax.random.normal(streams_of[6], (D,), jnp.float32), 0.5, 1.5).astype(jnp.bfloat16)
    w_in = noise(streams_of[7], (D, FF), D ** -0.5, 0.25)
    w_out = noise(streams_of[8], (FF, D), (FF // 2) ** -0.5, 0.1875)
    write_gain = jnp.clip(1.0 + 0.1 * jax.random.normal(streams_of[9], (D,), jnp.float32), 0.5, 1.5).astype(jnp.bfloat16)
    w_write = noise(streams_of[10], (D, 3 * D), D ** -0.5, 0.25)
    w_write_out = noise(streams_of[11], (D, D), (D // 16) ** -0.5, 1.0)
    init_memory = noise(streams_of[12], (SLOTS, D), 1.0, 6.0)
    out_grad = noise(streams_of[13], (STREAMS, SEGS, SEG, D), 1.0, 6.0, ((0, 8), (1, 4)))
    memory_grad = noise(streams_of[14], (STREAMS, SEGS, SLOTS, D), 1.0, 6.0, ((0, 8), (1, 4)))
    return dict(tokens=tokens, doc_ids=doc_ids, reset_flags=reset_flags, attn_gain=attn_gain, w_qkv=w_qkv, w_attn_out=w_attn_out, ffn_gain=ffn_gain, w_in=w_in, w_out=w_out, write_gain=write_gain, w_write=w_write, w_write_out=w_write_out, init_memory=init_memory, out_grad=out_grad, memory_grad=memory_grad)


EPS = 1e-06
MASKED = -1000000000.0
HIGH = lax.Precision.HIGHEST

@jax.custom_vjp
def low(v):
    return lax.optimization_barrier(v.astype(jnp.bfloat16)).astype(jnp.float32)

@jax.custom_vjp
def low_back(v):
    return v

def low_keep(v):
    return (low(v), None)

def low_pass(kept, grad):
    return (grad,)

def back_keep(v):
    return (v, None)

def back_low(kept, grad):
    return (low(grad),)
low.defvjp(low_keep, low_pass)
low_back.defvjp(back_keep, back_low)

def norm_rows(values, gain):
    return values * lax.rsqrt(lax.optimization_barrier(jnp.mean(values * values, axis=-1, keepdims=True)) + EPS) * gain

def product(left, right):
    return jnp.dot(left, right, precision=HIGH)

def attend(queries, keys, values, allowed):
    scale = HEAD_DIM ** (-0.5)
    q_heads = queries.reshape(queries.shape[0], HEADS, HEAD_DIM)
    k_heads = keys.reshape(keys.shape[0], HEADS, HEAD_DIM)
    v_heads = values.reshape(values.shape[0], HEADS, HEAD_DIM)
    scores = low_back(jnp.einsum('qhd,khd->hqk', q_heads, k_heads, precision=HIGH) * scale)
    attn_probs = low(jax.nn.softmax(jnp.where(allowed[None], scores, MASKED), axis=-1))
    mixed = jnp.einsum('hqk,khd->qhd', attn_probs, v_heads, precision=HIGH)
    return low(low_back(mixed.reshape(queries.shape[0], D)))

def segment(token_rows, memory_rows, docs, params):
    attn_gain, w_qkv, w_attn_out, ffn_gain, w_in, w_out, write_gain, w_write, w_write_out, init_memory = params
    normed = low(norm_rows(token_rows, attn_gain))
    mem_normed = low(norm_rows(memory_rows, attn_gain))
    proj_all = low(low_back(product(normed, w_qkv)))
    mem_kv = low(low_back(product(mem_normed, w_qkv[:, D:])))
    keys = jnp.concatenate([mem_kv[:, :D], proj_all[:, D:2 * D]], axis=0)
    values = jnp.concatenate([mem_kv[:, D:], proj_all[:, 2 * D:]], axis=0)
    allowed = jnp.concatenate([jnp.ones((SEG, SLOTS), bool), docs[:, None] == docs[None, :]], axis=1)
    mixed = attend(proj_all[:, :D], keys, values, allowed)
    hidden_one = token_rows + low_back(product(mixed, w_attn_out))
    upper = low_back(product(low(norm_rows(hidden_one, ffn_gain)), w_in))
    hidden_two = hidden_one + low_back(product(low(jax.nn.gelu(upper)), w_out))
    write_proj = low(low_back(product(low(norm_rows(memory_rows, write_gain)), w_write)))
    write_kv = low(low_back(product(low(norm_rows(hidden_two, write_gain)), w_write[:, D:])))
    wkeys = jnp.concatenate([write_proj[:, D:2 * D], write_kv[:, :D]], axis=0)
    wvalues = jnp.concatenate([write_proj[:, 2 * D:], write_kv[:, D:]], axis=0)
    wallowed = jnp.concatenate([jnp.eye(SLOTS, dtype=bool), jnp.ones((SLOTS, SEG), bool)], axis=1)
    written = attend(write_proj[:, :D], wkeys, wvalues, wallowed)
    new_memory = memory_rows + low_back(product(written, w_write_out))
    return (hidden_two, new_memory)

def stream(token_rows, docs, resets, params):
    init_memory = params[9]
    carried = init_memory
    encs = []
    mems = []
    for index in range(SEGS):
        start = jnp.where(resets[index] > 0, init_memory, low_back(carried))
        hidden_two, new_memory = segment(token_rows[index], start, docs[index], params)
        rounded = low(new_memory)
        encs.append(hidden_two)
        mems.append(rounded)
        carried = rounded
    return (jnp.stack(encs), jnp.stack(mems))

def reference(tokens, doc_ids, reset_flags, attn_gain, w_qkv, w_attn_out, ffn_gain, w_in, w_out, write_gain, w_write, w_write_out, init_memory, out_grad, memory_grad):
    params = tuple((p.astype(jnp.float32) for p in (attn_gain, w_qkv, w_attn_out, ffn_gain, w_in, w_out, write_gain, w_write, w_write_out, init_memory)))
    zero = tuple((jnp.zeros_like(p) for p in params))

    def one_stream(total, items):
        token_rows, docs, resets, enc_cot, mem_cot = items

        def forward(rows_in, weights):
            return stream(rows_in, docs, resets, weights)
        (encs, mems), backward = jax.vjp(forward, token_rows.astype(jnp.float32), params)
        grad_rows, grad_params = backward((enc_cot.astype(jnp.float32), mem_cot.astype(jnp.float32)))
        total = tuple((a + b for a, b in zip(total, grad_params)))
        return (total, (encs.astype(jnp.bfloat16), mems.astype(jnp.bfloat16), grad_rows))
    total, (encoded, memories, tokens_grad) = lax.scan(one_stream, zero, (tokens, doc_ids, reset_flags, out_grad, memory_grad))
    return (encoded, memories, tokens_grad, total[0], total[1], total[2], total[3], total[4], total[5], total[6], total[7], total[8], total[9])
```

```python
import jax
import jax.numpy as jnp
from jax import lax
from jax.experimental import pallas as pl
from jax.experimental.pallas import tpu as pltpu
from jax.sharding import PartitionSpec as P

HEADS = 8
HEAD_DIM = 64
EPS = 1e-06
MASKED = -1000000000.0
F32 = jnp.float32
BF16 = jnp.bfloat16
SQRT_2_PI = 0.7978845608028654
CUBIC = 0.044715
VMEM_LIMIT = 60 * 1024 * 1024


def nn(left, right):
    return lax.dot_general(left, right, (((1,), (0,)), ((), ())), preferred_element_type=F32)


def nt(left, right):
    return lax.dot_general(left, right, (((1,), (1,)), ((), ())), preferred_element_type=F32)


def wide(column_tile, width):
    copies = max(1, width // 128)
    if width < 128:
        return column_tile[:, :width]
    return jnp.concatenate([column_tile] * copies, axis=1)


def inverse_rms(values):
    return lax.rsqrt(jnp.mean(values * values, axis=0, keepdims=True) + EPS)


def lane_sums(values):
    total = values[:, :128]
    for at in range(128, values.shape[1], 128):
        total = total + values[:, at : at + 128]
    return total


def head_mask(rows, columns):
    row_head = lax.broadcasted_iota(jnp.int32, (rows, columns), 0) // HEAD_DIM
    column_head = lax.broadcasted_iota(jnp.int32, (rows, columns), 1) // HEAD_DIM
    return row_head == column_head


def norm_back(grad_normed, normed, scale, gain, gain_inverse):
    weighed = grad_normed * normed
    mean = jnp.mean(weighed, axis=0, keepdims=True)
    return scale * (grad_normed * gain - normed * gain_inverse * mean), weighed


def forward_kernel(
    flags,
    docs_ref,
    tok_ref,
    mem0_ref,
    init_ref,
    ga_ref,
    gf_ref,
    gw_ref,
    spread_ref,
    fold_ref,
    wqkv_ref,
    wao_ref,
    win_ref,
    wout_ref,
    ww_ref,
    wwo_ref,
    enc_ref,
    a1_ref,
    a1m_ref,
    q_ref,
    kt_ref,
    ktm_ref,
    v_ref,
    vm_ref,
    e_ref,
    em_ref,
    att_ref,
    a2_ref,
    z_ref,
    gp_ref,
    a3_ref,
    a3m_ref,
    qw_ref,
    kwt_ref,
    kwtm_ref,
    vw_ref,
    vwm_ref,
    ew_ref,
    ewm_ref,
    watt_ref,
    stat_ref,
    carry,
    bias,
    k_nat,
    km_nat,
    vt,
    vtm,
    hidden,
):
    step = pl.program_id(0)
    width = wao_ref.shape[0]
    seg = tok_ref.shape[1]
    slots = init_ref.shape[1]
    ff = win_ref.shape[0]

    @pl.when(step == 0)
    def _():
        carry[...] = mem0_ref[...].astype(F32)

    mem = jnp.where(flags[step] > 0, init_ref[...].astype(F32), carry[...])
    ga, gf, gw = ga_ref[...], gf_ref[...], gw_ref[...]

    docs = docs_ref[0].astype(F32)
    doc_rows = jnp.broadcast_to(docs, (128, seg)).T
    for at in range(0, seg, 128):
        bias[:, at : at + 128] = jnp.where(doc_rows == docs[:, at : at + 128], 0.0, MASKED)

    tokens = tok_ref[0].astype(F32).T
    r1 = inverse_rms(tokens)
    a1_ref[...] = (tokens * r1 * wide(ga, seg)).astype(BF16)
    rm = inverse_rms(mem)
    a1m_ref[0] = (mem * rm * ga[:, :slots]).astype(BF16)
    stat_ref[0, 0:1, :] = r1
    stat_ref[0, 4:5, :slots] = rm

    a1 = a1_ref[...]
    a1m = a1m_ref[0]
    q_ref[0] = (nn(wqkv_ref[:width, :], a1) * HEAD_DIM**-0.5).astype(BF16)
    kt = nn(wqkv_ref[width : 2 * width, :], a1).astype(BF16)
    kt_ref[0] = kt
    k_nat[...] = kt.T
    vt[...] = nn(wqkv_ref[2 * width :, :], a1).astype(BF16)
    v_ref[0] = vt[...].T
    ktm = nn(wqkv_ref[width : 2 * width, :], a1m).astype(BF16)
    ktm_ref[0] = ktm
    km_nat[...] = ktm.T
    vtm[...] = nn(wqkv_ref[2 * width :, :], a1m).astype(BF16)
    vm_ref[0] = vtm[...].T

    def pair(index, unused):
        lanes = pl.ds(pl.multiple_of(index * 128, 128), 128)
        keys = k_nat[:, lanes]
        mem_keys = km_nat[:, lanes]
        for half in range(2):
            head = index * 2 + half
            rows = pl.ds(pl.multiple_of(head * HEAD_DIM, HEAD_DIM), HEAD_DIM)
            queries = q_ref[0, rows, :]
            blank = jnp.zeros_like(queries)
            queries = jnp.concatenate([queries, blank] if half == 0 else [blank, queries], axis=0)
            for at in range(0, seg, 256):
                cols = slice(at, at + 256)
                scores = nn(keys, queries[:, cols]) + bias[:, cols]
                mem_scores = nn(mem_keys, queries[:, cols])
                top = jnp.maximum(
                    jnp.max(scores, axis=0, keepdims=True),
                    jnp.max(mem_scores, axis=0, keepdims=True),
                )
                raised = jnp.exp(scores - top)
                mem_raised = jnp.exp(mem_scores - top)
                inverse = 1.0 / (
                    jnp.sum(raised, axis=0, keepdims=True)
                    + jnp.sum(mem_raised, axis=0, keepdims=True)
                )
                raised = raised.astype(BF16)
                mem_raised = mem_raised.astype(BF16)
                e_ref[0, head, :, cols] = raised
                em_ref[0, rows, cols] = mem_raised
                mixed = nn(vt[rows, :], raised) + nn(vtm[rows, :], mem_raised)
                att_ref[rows, cols] = (mixed * inverse).astype(BF16)
                stat_ref[0, pl.ds(8 + head, 1), cols] = inverse
        return unused

    lax.fori_loop(0, HEADS // 2, pair, 0)

    h1 = tok_ref[0].astype(F32).T + nn(wao_ref[...], att_ref[...])
    r2 = inverse_rms(h1)
    stat_ref[0, 1:2, :] = r2
    a2_ref[...] = (h1 * r2 * wide(gf, seg)).astype(BF16)
    hidden[...] = h1
    a2 = a2_ref[...]
    for at in range(0, ff, 512):
        upper = nn(win_ref[at : at + 512, :], a2)
        square = upper * upper
        bent = jnp.tanh(upper * (SQRT_2_PI + (SQRT_2_PI * CUBIC) * square))
        cdf = 0.5 + 0.5 * bent
        z_ref[at : at + 512, :] = (upper * cdf).astype(BF16)
        slope = (0.5 * SQRT_2_PI) + (1.5 * SQRT_2_PI * CUBIC) * square
        gp_ref[0, at : at + 512, :] = (cdf + upper * (1.0 - bent * bent) * slope).astype(BF16)
    enc = hidden[...] + nn(wout_ref[...], z_ref[...])
    enc_ref[0, :seg, :] = enc.T.astype(BF16)
    r3 = inverse_rms(enc)
    stat_ref[0, 2:3, :] = r3
    a3_ref[...] = (enc * r3 * wide(gw, seg)).astype(BF16)
    a3m_ref[0] = (mem * rm * gw[:, :slots]).astype(BF16)
    a3 = a3_ref[...]
    a3m = a3m_ref[0]

    kwt = nn(ww_ref[width : 2 * width, :], a3).astype(BF16)
    kwt_ref[0] = kwt
    kw = kwt.T
    vwt = nn(ww_ref[2 * width :, :], a3).astype(BF16)
    vw_ref[0] = vwt.T
    kwtm = nn(ww_ref[width : 2 * width, :], a3m).astype(BF16)
    kwtm_ref[0] = kwtm
    vwtm = nn(ww_ref[2 * width :, :], a3m).astype(BF16)
    vwm_ref[0] = vwtm.T
    qwt = (nn(ww_ref[:width, :], a3m) * HEAD_DIM**-0.5).astype(BF16)
    own = head_mask(width, HEADS * slots)
    qw = jnp.where(own, nn(qwt, spread_ref[...]), 0.0).astype(BF16)
    qw_ref[0] = qw
    scores = nn(kw, qw)
    mem_scores = nn(kwtm.T, qw)
    slot_row = lax.broadcasted_iota(jnp.int32, mem_scores.shape, 0)
    slot_col = lax.broadcasted_iota(jnp.int32, mem_scores.shape, 1) % slots
    mem_scores = jnp.where(slot_row == slot_col, mem_scores, MASKED)
    top = jnp.maximum(
        jnp.max(scores, axis=0, keepdims=True), jnp.max(mem_scores, axis=0, keepdims=True)
    )
    raised = jnp.exp(scores - top)
    mem_raised = jnp.exp(mem_scores - top)
    inverse = 1.0 / (
        jnp.sum(raised, axis=0, keepdims=True) + jnp.sum(mem_raised, axis=0, keepdims=True)
    )
    stat_ref[0, 3:4, :] = inverse
    raised = raised.astype(BF16)
    mem_raised = mem_raised.astype(BF16)
    ew_ref[0] = raised
    ewm_ref[0] = mem_raised
    mixed = (nn(vwt, raised) + nn(vwtm, mem_raised)) * inverse
    watt = nn(jnp.where(own, mixed, 0.0).astype(BF16), fold_ref[...]).astype(BF16)
    watt_ref[0] = watt
    new_mem = (mem + nn(wwo_ref[...], watt)).astype(BF16).astype(F32)
    carry[...] = new_mem
    enc_ref[0, seg:, :] = new_mem.T.astype(BF16)


def chain_kernel(
    flags,
    gout_ref,
    carry0_ref,
    ga_ref,
    gf_ref,
    gw_ref,
    gai_ref,
    gfi_ref,
    gwi_ref,
    spread_ref,
    fold_ref,
    wqkv_ref,
    wao_ref,
    win_ref,
    wout_ref,
    ww_ref,
    wwo_ref,
    a1m_ref,
    q_ref,
    vm_ref,
    em_ref,
    att_ref,
    a2_ref,
    gp_ref,
    a3_ref,
    a3m_ref,
    qw_ref,
    kwt_ref,
    kwtm_ref,
    vw_ref,
    vwm_ref,
    ew_ref,
    ewm_ref,
    stat_ref,
    bm_ref,
    gwkv_ref,
    gwm_ref,
    bf_ref,
    gu_ref,
    ba_ref,
    gh_ref,
    do_ref,
    dd_ref,
    dsm_ref,
    gkvm_ref,
    init_ref,
    gains_ref,
    sent_ref,
    carry,
):
    step = pl.program_id(0)
    steps = pl.num_programs(0)
    place = steps - 1 - step
    width = wao_ref.shape[0]
    ff = wout_ref.shape[0]
    seg = q_ref.shape[2]
    slots = a1m_ref.shape[2]
    reset = flags[place] > 0

    @pl.when(step == 0)
    def _():
        carry[...] = carry0_ref[...].astype(F32)
        init_ref[...] = jnp.zeros_like(init_ref)
        gains_ref[...] = jnp.zeros_like(gains_ref)

    ga, gf, gw = ga_ref[...], gf_ref[...], gw_ref[...]
    gai, gfi, gwi = gai_ref[...], gfi_ref[...], gwi_ref[...]
    own = head_mask(width, HEADS * slots)
    rm = stat_ref[0, 4:5, :slots]

    grad_mem = gout_ref[0, seg:, :].astype(F32).T + carry[...]
    branch_mem = grad_mem.astype(BF16)
    bm_ref[0] = branch_mem
    grad_watt = nn(wwo_ref[...], branch_mem).astype(BF16)
    inverse = stat_ref[0, 3:4, :]
    scaled = (jnp.where(own, nn(grad_watt, spread_ref[...]), 0.0) * inverse).astype(BF16)
    raised = ew_ref[0].astype(F32)
    mem_raised = ewm_ref[0].astype(F32)
    grad_probs = nn(vw_ref[0], scaled)
    mem_grad_probs = nn(vwm_ref[0], scaled)
    dots = (
        jnp.sum(raised * grad_probs, axis=0, keepdims=True)
        + jnp.sum(mem_raised * mem_grad_probs, axis=0, keepdims=True)
    ) * inverse
    grad_scores = (raised * (grad_probs - dots)).astype(BF16)
    mem_grad_scores = (mem_raised * (mem_grad_probs - dots)).astype(BF16)
    gwkv_ref[:width, :] = nt(qw_ref[0], grad_scores).astype(BF16)
    gwkv_ref[width:, :] = nt(scaled, ew_ref[0]).astype(BF16)
    grad_q = (nn(kwt_ref[0], grad_scores) + nn(kwtm_ref[0], mem_grad_scores)) * HEAD_DIM**-0.5
    gwm_ref[0, :width, :] = nn(jnp.where(own, grad_q, 0.0).astype(BF16), fold_ref[...]).astype(BF16)
    gwm_ref[0, width : 2 * width, :] = nt(qw_ref[0], mem_grad_scores).astype(BF16)
    gwm_ref[0, 2 * width :, :] = nt(scaled, ewm_ref[0]).astype(BF16)

    grad_a3 = nn(ww_ref[:, width:], gwkv_ref[...])
    grad_a3m = nn(ww_ref[...], gwm_ref[0])
    part, weighed = norm_back(
        grad_a3, a3_ref[...].astype(F32), stat_ref[0, 2:3, :], wide(gw, seg), wide(gwi, seg)
    )
    mem_part, mem_weighed = norm_back(
        grad_a3m, a3m_ref[0].astype(F32), rm, gw[:, :slots], gwi[:, :slots]
    )
    gains_ref[2] += lane_sums(weighed)
    gains_ref[2, :, :slots] += mem_weighed
    grad_mem_in = grad_mem + mem_part
    gh_ref[0] = gout_ref[0, :seg, :].astype(F32).T + part

    bf_ref[...] = gh_ref[0].astype(BF16)
    branch = bf_ref[...]
    for at in range(0, ff, 512):
        grad_z = nn(wout_ref[at : at + 512, :], branch)
        gu_ref[at : at + 512, :] = (grad_z * gp_ref[0, at : at + 512, :].astype(F32)).astype(BF16)
    grad_a2 = nn(win_ref[...], gu_ref[...])
    part, weighed = norm_back(
        grad_a2, a2_ref[...].astype(F32), stat_ref[0, 1:2, :], wide(gf, seg), wide(gfi, seg)
    )
    gains_ref[1] += lane_sums(weighed)
    gh_ref[0] += part

    ba_ref[...] = gh_ref[0].astype(BF16)
    grad_att = nn(wao_ref[...], ba_ref[...]).astype(BF16)
    products = grad_att.astype(F32) * att_ref[...].astype(F32)
    rows = []
    dots = []
    for head in range(HEADS):
        span = slice(head * HEAD_DIM, (head + 1) * HEAD_DIM)
        inverse = stat_ref[0, 8 + head : 9 + head, :]
        dots.append(jnp.sum(products[span, :], axis=0, keepdims=True) * inverse)
        rows.append((grad_att[span, :].astype(F32) * inverse).astype(BF16))
    scaled = jnp.concatenate(rows, axis=0)
    do_ref[0] = scaled
    dd_ref[0] = jnp.concatenate(dots, axis=0)
    mem_values = jnp.concatenate([vm_ref[0].astype(F32)] * HEADS, axis=0)
    mem_values = jnp.where(own, mem_values, 0.0).astype(BF16)
    grad_probs = nn(mem_values, scaled)
    parts = []
    for head in range(HEADS):
        span = slice(head * slots, (head + 1) * slots)
        parts.append(
            (em_ref[0, span, :].astype(F32) * (grad_probs[span, :] - dots[head])).astype(BF16)
        )
    grad_scores = jnp.concatenate(parts, axis=0)
    dsm_ref[0] = grad_scores
    grad_k = jnp.where(own, nt(q_ref[0], grad_scores), 0.0).astype(BF16)
    grad_v = jnp.where(own, nt(scaled, em_ref[0]), 0.0).astype(BF16)
    gkvm_ref[0, :width, :] = nn(grad_k, fold_ref[...]).astype(BF16)
    gkvm_ref[0, width:, :] = nn(grad_v, fold_ref[...]).astype(BF16)
    grad_a1m = nn(wqkv_ref[:, width:], gkvm_ref[0])
    mem_part, mem_weighed = norm_back(
        grad_a1m, a1m_ref[0].astype(F32), rm, ga[:, :slots], gai[:, :slots]
    )
    gains_ref[0, :, :slots] += mem_weighed
    grad_mem_in = grad_mem_in + mem_part
    init_ref[...] += jnp.where(reset, grad_mem_in, 0.0)
    carry[...] = jnp.where(reset, 0.0, grad_mem_in).astype(BF16).astype(F32)
    sent_ref[...] = carry[...].astype(BF16)


def attention_kernel(
    do_ref,
    dd_ref,
    dsm_ref,
    gh_ref,
    q_ref,
    kt_ref,
    ktm_ref,
    v_ref,
    e_ref,
    a1_ref,
    stat_ref,
    ga_ref,
    gai_ref,
    wqkv_ref,
    gqkv_ref,
    gtok_ref,
    gain_ref,
    grad_scores,
):
    step = pl.program_id(0)
    width = wqkv_ref.shape[0]
    seg = q_ref.shape[2]

    @pl.when(step == 0)
    def _():
        gain_ref[...] = jnp.zeros_like(gain_ref)

    def pair(index, unused):
        lanes = pl.ds(pl.multiple_of(index * 128, 128), 128)
        values = v_ref[0, :, lanes]
        for half in range(2):
            head = index * 2 + half
            base = pl.multiple_of(head * HEAD_DIM, HEAD_DIM)
            rows = pl.ds(base, HEAD_DIM)
            key_rows = pl.ds(width + base, HEAD_DIM)
            value_rows = pl.ds(2 * width + base, HEAD_DIM)
            grads = do_ref[0, rows, :]
            blank = jnp.zeros_like(grads)
            padded = jnp.concatenate([grads, blank] if half == 0 else [blank, grads], axis=0)
            dots = dd_ref[0, pl.ds(head, 1), :]
            for at in range(0, seg, 256):
                cols = slice(at, at + 256)
                grad_probs = nn(values, padded[:, cols])
                raised = e_ref[0, head, :, cols].astype(F32)
                inner = (raised * (grad_probs - dots[:, cols])).astype(BF16)
                grad_scores[half, :, cols] = inner
                grad_q = nn(kt_ref[0, rows, :], inner) + nn(ktm_ref[0, rows, :], dsm_ref[0, rows, cols])
                gqkv_ref[rows, cols] = (grad_q * HEAD_DIM**-0.5).astype(BF16)
            gqkv_ref[key_rows, :] = nt(q_ref[0, rows, :], grad_scores[half]).astype(BF16)
            gqkv_ref[value_rows, :] = nt(grads, e_ref[0, head]).astype(BF16)
        return unused

    lax.fori_loop(0, HEADS // 2, pair, 0)
    grad_a1 = nn(wqkv_ref[...], gqkv_ref[...])
    part, weighed = norm_back(
        grad_a1,
        a1_ref[...].astype(F32),
        stat_ref[0, 0:1, :],
        wide(ga_ref[...], seg),
        wide(gai_ref[...], seg),
    )
    gain_ref[...] += lane_sums(weighed)
    gtok_ref[0] = (gh_ref[0] + part).T.astype(BF16)


def whole(array):
    zeros = (0,) * array.ndim
    return pl.BlockSpec(array.shape, lambda *unused: zeros, pipeline_mode=pl.Buffered(1))


def params():
    return pltpu.CompilerParams(
        dimension_semantics=("arbitrary",), vmem_limit_bytes=VMEM_LIMIT
    )


def forward_chain(rows, docs, flags, mem0, consts, w):
    segs, seg, width = rows.shape[0], rows.shape[1], rows.shape[2]
    slots = mem0.shape[1]
    ff = w["in_t"].shape[0]
    flat = lambda height: (jax.ShapeDtypeStruct((height, segs * seg), BF16), pl.BlockSpec((height, seg), lambda s, f: (0, s)))

    def stack(*shape, dtype=BF16):
        tail = (0,) * len(shape)
        return (
            jax.ShapeDtypeStruct((segs,) + shape, dtype),
            pl.BlockSpec((1,) + shape, lambda s, f: (s,) + tail),
        )

    outs = dict(
        enc=stack(seg + slots, width),
        a1=flat(width),
        a1m=stack(width, slots),
        q=stack(width, seg),
        kt=stack(width, seg),
        ktm=stack(width, slots),
        v=stack(seg, width),
        vm=stack(slots, width),
        e=stack(HEADS, seg, seg),
        em=stack(HEADS * slots, seg),
        att=flat(width),
        a2=flat(width),
        z=flat(ff),
        gp=stack(ff, seg),
        a3=flat(width),
        a3m=stack(width, slots),
        qw=stack(width, HEADS * slots),
        kwt=stack(width, seg),
        kwtm=stack(width, slots),
        vw=stack(seg, width),
        vwm=stack(slots, width),
        ew=stack(seg, HEADS * slots),
        ewm=stack(slots, HEADS * slots),
        watt=stack(width, slots),
        stat=stack(16, seg, dtype=F32),
    )
    fixed = [
        mem0,
        consts["init_t"],
        consts["ga"],
        consts["gf"],
        consts["gw"],
        consts["spread"],
        consts["fold"],
        w["qkv_t"],
        w["ao_t"],
        w["in_t"],
        w["out_t"],
        w["write_t"],
        w["wo_t"],
    ]
    results = pl.pallas_call(
        forward_kernel,
        grid_spec=pltpu.PrefetchScalarGridSpec(
            num_scalar_prefetch=1,
            grid=(segs,),
            in_specs=[
                pl.BlockSpec((1, 1, seg), lambda s, f: (s, 0, 0)),
                pl.BlockSpec((1, seg, width), lambda s, f: (s, 0, 0)),
            ]
            + [whole(a) for a in fixed],
            out_specs=[spec for _, spec in outs.values()],
            scratch_shapes=[
                pltpu.VMEM((width, slots), F32),
                pltpu.VMEM((seg, seg), F32),
                pltpu.VMEM((seg, width), BF16),
                pltpu.VMEM((slots, width), BF16),
                pltpu.VMEM((width, seg), BF16),
                pltpu.VMEM((width, slots), BF16),
                pltpu.VMEM((width, seg), F32),
            ],
        ),
        out_shape=[shape for shape, _ in outs.values()],
        compiler_params=params(),
        name="forward_chain",
    )(flags, docs, rows, *fixed)
    return dict(zip(outs, results))


def backward_chain(kept, gout, flags, carry0, consts, w):
    segs = gout.shape[0]
    width, slots = kept["a1m"].shape[1:]
    seg = kept["q"].shape[2]
    ff = kept["gp"].shape[1]
    last = segs - 1

    def flat(height):
        return (
            jax.ShapeDtypeStruct((height, segs * seg), BF16),
            pl.BlockSpec((height, seg), lambda s, f: (0, last - s)),
        )

    def stack(*shape, dtype=BF16):
        tail = (0,) * len(shape)
        return (
            jax.ShapeDtypeStruct((segs,) + shape, dtype),
            pl.BlockSpec((1,) + shape, lambda s, f: (last - s,) + tail),
        )

    def single(*shape, dtype=F32):
        tail = (0,) * len(shape)
        return (jax.ShapeDtypeStruct(shape, dtype), pl.BlockSpec(shape, lambda s, f: tail))

    outs = dict(
        bm=stack(width, slots),
        gwkv=flat(2 * width),
        gwm=stack(3 * width, slots),
        bf=flat(width),
        gu=flat(ff),
        ba=flat(width),
        gh=stack(width, seg, dtype=F32),
        do=stack(width, seg),
        dd=stack(HEADS, seg, dtype=F32),
        dsm=stack(HEADS * slots, seg),
        gkvm=stack(2 * width, slots),
        init=single(width, slots),
        gains=single(3, width, 128),
        sent=single(width, slots, dtype=BF16),
    )
    fixed = [
        carry0,
        consts["ga"],
        consts["gf"],
        consts["gw"],
        consts["gai"],
        consts["gfi"],
        consts["gwi"],
        consts["spread"],
        consts["fold"],
        w["qkv"],
        w["ao"],
        w["in"],
        w["out"],
        w["write"],
        w["wo"],
    ]
    blocked = ["a1m", "q", "vm", "em", "att", "a2", "gp", "a3", "a3m", "qw", "kwt", "kwtm", "vw", "vwm", "ew", "ewm", "stat"]

    def spec_of(array):
        if array.ndim == 2:
            return pl.BlockSpec((array.shape[0], seg), lambda s, f: (0, last - s))
        tail = (0,) * (array.ndim - 1)
        return pl.BlockSpec((1,) + array.shape[1:], lambda s, f: (last - s,) + tail)

    results = pl.pallas_call(
        chain_kernel,
        grid_spec=pltpu.PrefetchScalarGridSpec(
            num_scalar_prefetch=1,
            grid=(segs,),
            in_specs=[spec_of(gout)]
            + [whole(a) for a in fixed]
            + [spec_of(kept[name]) for name in blocked],
            out_specs=[spec for _, spec in outs.values()],
            scratch_shapes=[pltpu.VMEM((width, slots), F32)],
        ),
        out_shape=[shape for shape, _ in outs.values()],
        compiler_params=params(),
        name="backward_chain",
    )(flags, gout, *fixed, *[kept[name] for name in blocked])
    return dict(zip(outs, results))


def attention_back(kept, grads, consts, w):
    segs, width, seg = kept["q"].shape

    def spec_of(array):
        if array.ndim == 2:
            return pl.BlockSpec((array.shape[0], seg), lambda s: (0, s))
        tail = (0,) * (array.ndim - 1)
        return pl.BlockSpec((1,) + array.shape[1:], lambda s: (s,) + tail)

    blocked = [grads["do"], grads["dd"], grads["dsm"], grads["gh"]] + [
        kept[name] for name in ("q", "kt", "ktm", "v", "e", "a1", "stat")
    ]
    fixed = [consts["ga"], consts["gai"], w["qkv"]]
    return pl.pallas_call(
        attention_kernel,
        grid=(segs,),
        in_specs=[spec_of(a) for a in blocked] + [whole(a) for a in fixed],
        out_specs=[
            pl.BlockSpec((3 * width, seg), lambda s: (0, s)),
            pl.BlockSpec((1, seg, width), lambda s: (s, 0, 0)),
            pl.BlockSpec((width, 128), lambda s: (0, 0)),
        ],
        out_shape=[
            jax.ShapeDtypeStruct((3 * width, segs * seg), BF16),
            jax.ShapeDtypeStruct((segs, seg, width), BF16),
            jax.ShapeDtypeStruct((width, 128), F32),
        ],
        scratch_shapes=[pltpu.VMEM((2, seg, seg), BF16)],
        compiler_params=params(),
        name="attention_back",
    )(*blocked, *fixed)


def swap_pairs(value, axis, mask):
    size = lax.axis_size(axis)
    return lax.ppermute(value, axis, [(i, i ^ mask) for i in range(size)])


def bits_of(axis):
    size = lax.axis_size(axis)
    return [(axis, 1 << at) for at in range(size.bit_length() - 1)]


def summed(value, order):
    for axis, mask in order:
        half = value.shape[0] // 2
        high = (lax.axis_index(axis) // mask) % 2
        sent = lax.dynamic_slice_in_dim(value, (1 - high) * half, half, 0)
        held = lax.dynamic_slice_in_dim(value, high * half, half, 0)
        value = held + swap_pairs(sent, axis, mask)
    for axis, mask in reversed(order):
        high = (lax.axis_index(axis) // mask) % 2
        other = swap_pairs(value, axis, mask)
        low_part = jnp.where(high == 0, value, other)
        high_part = jnp.where(high == 0, other, value)
        value = jnp.concatenate([low_part, high_part], axis=0)
    return value


def to_streams(value, chunks):
    place = lax.axis_index("section")
    if chunks == 1:
        sections = lax.axis_size("section")
        parts = [lax.dynamic_index_in_dim(value, place, 0, keepdims=False)]
        for mask in range(1, sections):
            sent = lax.dynamic_index_in_dim(value, place ^ mask, 0, keepdims=False)
            parts.append(swap_pairs(sent, "section", mask))
        stacked = jnp.stack(parts)
        return jnp.stack(
            [lax.dynamic_index_in_dim(stacked, place ^ at, 0, keepdims=False) for at in range(sections)]
        )
    gathered = lax.all_gather(value, "section")
    own = lax.dynamic_index_in_dim(gathered, place // chunks, 1, keepdims=False)
    count = gathered.shape[0] // chunks
    return lax.dynamic_slice_in_dim(own, (place % chunks) * count, count, 0)


def to_segments(value, chunks):
    if chunks == 1:
        return to_streams(value, 1)
    place = lax.axis_index("section")
    gathered = lax.all_gather(value, "section")
    sections = gathered.shape[0]
    count = value.shape[0]
    by_stream = gathered.reshape((sections // chunks, chunks * count) + value.shape[1:])
    return lax.dynamic_index_in_dim(by_stream, place, 1, keepdims=False)


def body(
    tokens,
    doc_ids,
    reset_flags,
    attn_gain,
    w_qkv,
    w_attn_out,
    ffn_gain,
    w_in,
    w_out,
    write_gain,
    w_write,
    w_write_out,
    init_memory,
    out_grad,
    memory_grad,
):
    streams, _, seg, width = tokens.shape
    slots = init_memory.shape[0]
    ff = w_in.shape[1]
    sections = lax.axis_size("section")
    chunks = sections // streams
    place = lax.axis_index("section")

    def lanes_of(gain):
        return jnp.broadcast_to(gain.astype(F32)[:, None], (width, 128))

    spread = (jnp.arange(slots)[:, None] == jnp.arange(HEADS * slots)[None, :] % slots).astype(BF16)
    consts = dict(
        init_t=init_memory.T,
        ga=lanes_of(attn_gain),
        gf=lanes_of(ffn_gain),
        gw=lanes_of(write_gain),
        spread=spread,
        fold=spread.T,
    )
    for name in ("ga", "gf", "gw"):
        consts[name + "i"] = 1.0 / consts[name]
    w = dict(
        qkv=w_qkv,
        ao=w_attn_out,
        out=w_out,
        write=w_write,
        wo=w_write_out,
        qkv_t=w_qkv.T,
        ao_t=w_attn_out.T,
        in_t=w_in.T,
        out_t=w_out.T,
        write_t=w_write.T,
        wo_t=w_write_out.T,
    )
    w["in"] = w_in

    marks = jnp.concatenate(
        [doc_ids[:, 0], jnp.broadcast_to(reset_flags, (streams, seg))], axis=1
    ).reshape(streams, 2, seg)
    marks = jnp.pad(marks, ((0, 0), (0, 14), (0, 0))).astype(BF16)
    own = to_streams(jnp.concatenate([tokens[:, 0], marks], axis=1), chunks)
    rows = own[:, :seg]
    docs = own[:, seg : seg + 1]
    flags = own[:, seg + 1, 0].astype(jnp.int32)
    gout = to_streams(jnp.concatenate([out_grad[:, 0], memory_grad[:, 0]], axis=1), chunks)

    arriving = jnp.zeros((width, slots), BF16)
    for turn in range(chunks):
        kept = forward_chain(rows, docs, flags, arriving, consts, w)
        if turn < chunks - 1:
            last = kept["enc"][-1, seg:, :].T
            arriving = lax.ppermute(last, "section", [(i, i + 1) for i in range(sections - 1)])

    returned = to_segments(kept["enc"], chunks)

    returning = jnp.zeros((width, slots), BF16)
    for turn in range(chunks):
        grads = backward_chain(kept, gout, flags, returning, consts, w)
        if turn < chunks - 1:
            returning = lax.ppermute(grads["sent"], "section", [(i + 1, i) for i in range(sections - 1)])

    gqkv, gtok, gain_attn = attention_back(kept, grads, consts, w)
    token_grads = to_segments(gtok, chunks)

    def weight(left, right):
        return lax.dot_general(left, right, (((1,), (1,)), ((), ())), preferred_element_type=F32)

    def weight_mem(left, right):
        return jnp.einsum("sft,sgt->fg", left, right, preferred_element_type=F32)

    grad_out = weight(kept["z"], grads["bf"]).astype(BF16)
    grad_in = weight(kept["a2"], grads["gu"]).astype(BF16)
    grad_write = weight_mem(kept["a3m"], grads["gwm"])
    grad_write = jnp.concatenate(
        [grad_write[:, :width], grad_write[:, width:] + weight(kept["a3"], grads["gwkv"])], axis=1
    )
    grad_wo = weight_mem(kept["watt"], grads["bm"])
    grad_ao = weight(kept["att"], grads["ba"])
    grad_qkv = weight(kept["a1"], gqkv)
    grad_qkv = jnp.concatenate(
        [grad_qkv[:, :width], grad_qkv[:, width:] + weight_mem(kept["a1m"], grads["gkvm"])], axis=1
    )
    gains = jnp.sum(grads["gains"], axis=2)
    gains = gains + jnp.stack([jnp.sum(gain_attn, axis=1), jnp.zeros(width), jnp.zeros(width)])
    gains = gains / jnp.stack([attn_gain, ffn_gain, write_gain]).astype(F32)
    extras = jnp.concatenate([grads["init"].T.reshape(-1), gains.reshape(-1)])
    pad = (-extras.shape[0]) % (width * 128)
    extras = jnp.pad(extras, (0, pad)).reshape(width, -1)

    section_bits = bits_of("section")
    dp_bits = bits_of("dp")
    order = section_bits[:1] + dp_bits[:1] + section_bits[1:] + dp_bits[1:]
    other = section_bits + dp_bits
    group_out = summed(grad_out, order)
    group_in = summed(grad_in, other)
    group_write = summed(jnp.concatenate([grad_write, grad_wo], axis=1).astype(BF16), order)
    group_qkv = summed(jnp.concatenate([grad_qkv, grad_ao, extras], axis=1).astype(BF16), other)

    extras = group_qkv[:, 4 * width :].astype(F32).reshape(-1)
    cut = slots * width
    init_grad = extras[:cut].reshape(slots, width)
    gains = extras[cut : cut + 3 * width].reshape(3, width)
    return (
        returned[:, None, :seg],
        returned[:, None, seg:],
        token_grads[:, None].astype(F32),
        gains[0],
        group_qkv[:, : 3 * width].astype(F32),
        group_qkv[:, 3 * width : 4 * width].astype(F32),
        gains[1],
        group_in.astype(F32),
        group_out.astype(F32),
        gains[2],
        group_write[:, : 3 * width].astype(F32),
        group_write[:, 3 * width :].astype(F32),
        init_grad,
    )


def solution(mesh):
    local = P("dp", "section")
    return jax.shard_map(
        body,
        mesh=mesh,
        in_specs=(local,) * 3 + (P(),) * 10 + (local,) * 2,
        out_specs=(local,) * 3 + (P(),) * 10,
        check_vma=False,
    )
```

```python
import jax
import jax.numpy as jnp
import numpy as np
from jax import lax
from jax.experimental import pallas as pl
from jax.experimental.pallas import tpu as pltpu
from jax.sharding import PartitionSpec as P

HEADS = 8
HEAD_DIM = 64
EPS = 1e-06
MASKED = -1000000000.0
F32 = jnp.float32
BF16 = jnp.bfloat16
SQRT_2_PI = 0.7978845608028654
CUBIC = 0.044715
VMEM_LIMIT = 60 * 1024 * 1024


def nn(left, right):
    return lax.dot_general(left, right, (((1,), (0,)), ((), ())), preferred_element_type=F32)


def tn(left, right):
    return lax.dot_general(left, right, (((0,), (0,)), ((), ())), preferred_element_type=F32)


def nt(left, right):
    return lax.dot_general(left, right, (((1,), (1,)), ((), ())), preferred_element_type=F32)


def wide(column_tile, width):
    copies = max(1, width // 128)
    if width < 128:
        return column_tile[:, :width]
    return jnp.concatenate([column_tile] * copies, axis=1)


def inverse_rms(values):
    return lax.rsqrt(jnp.mean(values * values, axis=0, keepdims=True) + EPS)


def lane_sums(values):
    total = values[:, :128]
    for at in range(128, values.shape[1], 128):
        total = total + values[:, at : at + 128]
    return total


def head_mask(rows, columns):
    row_head = lax.broadcasted_iota(jnp.int32, (rows, columns), 0) // HEAD_DIM
    column_head = lax.broadcasted_iota(jnp.int32, (rows, columns), 1) // HEAD_DIM
    return row_head == column_head


def norm_back(grad_normed, normed, scale, gain, gain_inverse):
    weighed = grad_normed * normed
    mean = jnp.mean(weighed, axis=0, keepdims=True)
    return scale * (grad_normed * gain - normed * gain_inverse * mean), weighed


def gain_tiles(gains_ref, count=3):
    tiles = []
    for at in range(count):
        row = gains_ref[at : at + 1, :]
        tiles.append(jnp.broadcast_to(row, (128, row.shape[1])).T)
    return tiles


class Sources:
    def __init__(self, arrays, choices):
        self.arrays = arrays
        self.choices = choices

    def start(self, refs, at, place, buffer, sem):
        for condition, parts in self.choices(at, place):

            @pl.when(condition)
            def _():
                top = 0
                for number, index in parts:
                    source = refs[number].at[index]
                    target = buffer.at[pl.ds(top, source.shape[0]), :]
                    pltpu.make_async_copy(source, target, sem).start()
                    top += source.shape[0]

    def wait(self, buffer, sem):
        pltpu.make_async_copy(buffer, buffer, sem).wait()

    def rows_of(self, refs, steps, segment, place, buffer, sems):
        step = pl.program_id(0)
        slot = lax.rem(step, 2)

        @pl.when(step == 0)
        def _():
            self.start(refs, segment(0), place, buffer.at[0], sems.at[0])

        if steps > 1:

            @pl.when(step + 1 < steps)
            def _():
                self.start(refs, segment(step + 1), place, buffer.at[1 - slot], sems.at[1 - slot])

        self.wait(buffer.at[slot], sems.at[slot])
        return buffer.at[slot]


def forward_kernel(
    sources,
    first,
    count,
    place_ref,
    mem0_ref,
    init_ref,
    gains_ref,
    spread_ref,
    fold_ref,
    wqkv_ref,
    wao_ref,
    win_ref,
    wout_ref,
    ww_ref,
    wwo_ref,
    *refs,
):
    (
        enc_ref,
        a1_ref,
        a1m_ref,
        q_ref,
        kt_ref,
        ktm_ref,
        v_ref,
        vm_ref,
        e_ref,
        em_ref,
        att_ref,
        a2_ref,
        z_ref,
        gp_ref,
        a3_ref,
        a3m_ref,
        qw_ref,
        kwt_ref,
        kwtm_ref,
        vw_ref,
        vwm_ref,
        ew_ref,
        ewm_ref,
        watt_ref,
        stat_ref,
        last_ref,
        carry,
        bias,
        k_nat,
        km_nat,
        vt,
        vtm,
        hidden,
        row_buffer,
        row_sems,
    ) = refs[-35:]
    step = pl.program_id(0)
    rows_ref = sources.rows_of(
        refs[: len(sources.arrays)], count, lambda s: s + first, place_ref[0], row_buffer, row_sems
    )
    width = wao_ref.shape[0]
    seg = q_ref.shape[2]
    slots = init_ref.shape[0]
    ff = win_ref.shape[0]

    @pl.when(step == 0)
    def _():
        carry[...] = mem0_ref[...].astype(F32)

    docs = rows_ref[seg : seg + 1, :].astype(F32)
    flag = rows_ref[seg + 1 : seg + 2, :].astype(F32)
    stat_ref[0, 5:6, :] = flag
    mem = jnp.where(flag[:, :slots] > 0.0, init_ref[...].astype(F32).T, carry[...])
    ga, gf, gw = gain_tiles(gains_ref)

    doc_rows = jnp.broadcast_to(docs, (128, seg)).T
    for at in range(0, seg, 128):
        bias[:, at : at + 128] = jnp.where(doc_rows == docs[:, at : at + 128], 0.0, MASKED)

    tokens = rows_ref[:seg, :].astype(F32).T
    r1 = inverse_rms(tokens)
    a1_ref[...] = (tokens * r1 * wide(ga, seg)).astype(BF16)
    rm = inverse_rms(mem)
    a1m_ref[0] = (mem * rm * ga[:, :slots]).astype(BF16)
    stat_ref[0, 0:1, :] = r1
    stat_ref[0, 4:5, :slots] = rm

    a1 = a1_ref[...]
    a1m = a1m_ref[0]
    q_ref[0] = (nn(wqkv_ref[:width, :], a1) * HEAD_DIM**-0.5).astype(BF16)
    kt = nn(wqkv_ref[width : 2 * width, :], a1).astype(BF16)
    kt_ref[0] = kt
    k_nat[...] = kt.T
    vt[...] = nn(wqkv_ref[2 * width :, :], a1).astype(BF16)
    v_ref[0] = vt[...].T
    ktm = nn(wqkv_ref[width : 2 * width, :], a1m).astype(BF16)
    ktm_ref[0] = ktm
    km_nat[...] = ktm.T
    vtm[...] = nn(wqkv_ref[2 * width :, :], a1m).astype(BF16)
    vm_ref[0] = vtm[...].T

    def pair(index, unused):
        lanes = pl.ds(pl.multiple_of(index * 128, 128), 128)
        keys = k_nat[:, lanes]
        mem_keys = km_nat[:, lanes]
        for half in range(2):
            head = index * 2 + half
            rows = pl.ds(pl.multiple_of(head * HEAD_DIM, HEAD_DIM), HEAD_DIM)
            queries = q_ref[0, rows, :]
            blank = jnp.zeros_like(queries)
            queries = jnp.concatenate([queries, blank] if half == 0 else [blank, queries], axis=0)
            scores = nn(keys, queries) + bias[...]
            mem_scores = nn(mem_keys, queries)
            top = jnp.maximum(
                jnp.max(scores, axis=0, keepdims=True), jnp.max(mem_scores, axis=0, keepdims=True)
            )
            raised = jnp.exp(scores - top)
            mem_raised = jnp.exp(mem_scores - top)
            inverse = 1.0 / (
                jnp.sum(raised, axis=0, keepdims=True) + jnp.sum(mem_raised, axis=0, keepdims=True)
            )
            raised = raised.astype(BF16)
            mem_raised = mem_raised.astype(BF16)
            e_ref[0, head] = raised
            em_ref[0, rows, :] = mem_raised
            mixed = nn(vt[rows, :], raised) + nn(vtm[rows, :], mem_raised)
            att_ref[rows, :] = (mixed * inverse).astype(BF16)
            stat_ref[0, pl.ds(8 + head, 1), :] = inverse
        return unused

    lax.fori_loop(0, HEADS // 2, pair, 0, unroll=HEADS // 2)

    h1 = rows_ref[:seg, :].astype(F32).T + nn(wao_ref[...], att_ref[...])
    r2 = inverse_rms(h1)
    stat_ref[0, 1:2, :] = r2
    a2_ref[...] = (h1 * r2 * wide(gf, seg)).astype(BF16)
    hidden[...] = h1
    a2 = a2_ref[...]
    for at in range(0, ff, 512):
        upper = nn(win_ref[at : at + 512, :], a2)
        square = upper * upper
        bent = jnp.tanh(upper * (SQRT_2_PI + (SQRT_2_PI * CUBIC) * square))
        cdf = 0.5 + 0.5 * bent
        z_ref[at : at + 512, :] = (upper * cdf).astype(BF16)
        slope = (0.5 * SQRT_2_PI) + (1.5 * SQRT_2_PI * CUBIC) * square
        gp_ref[0, at : at + 512, :] = (cdf + upper * (1.0 - bent * bent) * slope).astype(BF16)
    enc = hidden[...] + tn(wout_ref[...], z_ref[...])
    enc_ref[0, :seg, :] = enc.T.astype(BF16)
    r3 = inverse_rms(enc)
    stat_ref[0, 2:3, :] = r3
    a3_ref[...] = (enc * r3 * wide(gw, seg)).astype(BF16)
    a3m_ref[0] = (mem * rm * gw[:, :slots]).astype(BF16)
    a3 = a3_ref[...]
    a3m = a3m_ref[0]

    kwt = nn(ww_ref[width : 2 * width, :], a3).astype(BF16)
    kwt_ref[0] = kwt
    kw = kwt.T
    vwt = nn(ww_ref[2 * width :, :], a3).astype(BF16)
    vw_ref[0] = vwt.T
    kwtm = nn(ww_ref[width : 2 * width, :], a3m).astype(BF16)
    kwtm_ref[0] = kwtm
    vwtm = nn(ww_ref[2 * width :, :], a3m).astype(BF16)
    vwm_ref[0] = vwtm.T
    qwt = (nn(ww_ref[:width, :], a3m) * HEAD_DIM**-0.5).astype(BF16)
    own = head_mask(width, HEADS * slots)
    qw = jnp.where(own, nn(qwt, spread_ref[...]), 0.0).astype(BF16)
    qw_ref[0] = qw
    scores = nn(kw, qw)
    mem_scores = nn(kwtm.T, qw)
    slot_row = lax.broadcasted_iota(jnp.int32, mem_scores.shape, 0)
    slot_col = lax.broadcasted_iota(jnp.int32, mem_scores.shape, 1) % slots
    mem_scores = jnp.where(slot_row == slot_col, mem_scores, MASKED)
    top = jnp.maximum(
        jnp.max(scores, axis=0, keepdims=True), jnp.max(mem_scores, axis=0, keepdims=True)
    )
    raised = jnp.exp(scores - top)
    mem_raised = jnp.exp(mem_scores - top)
    inverse = 1.0 / (
        jnp.sum(raised, axis=0, keepdims=True) + jnp.sum(mem_raised, axis=0, keepdims=True)
    )
    stat_ref[0, 3:4, :] = inverse
    raised = raised.astype(BF16)
    mem_raised = mem_raised.astype(BF16)
    ew_ref[0] = raised
    ewm_ref[0] = mem_raised
    mixed = (nn(vwt, raised) + nn(vwtm, mem_raised)) * inverse
    watt = nn(jnp.where(own, mixed, 0.0).astype(BF16), fold_ref[...]).astype(BF16)
    watt_ref[0] = watt
    new_mem = (mem + nn(wwo_ref[...], watt)).astype(BF16).astype(F32)
    carry[...] = new_mem
    enc_ref[0, seg:, :] = new_mem.T.astype(BF16)
    last_ref[...] = new_mem.astype(BF16)


def chain_kernel(
    sources,
    segs,
    place_ref,
    carry0_ref,
    weights_gains_ref,
    spread_ref,
    fold_ref,
    wqkv_ref,
    wao_ref,
    win_ref,
    wout_ref,
    ww_ref,
    wwo_ref,
    a1m_ref,
    q_ref,
    vm_ref,
    em_ref,
    att_ref,
    a2_ref,
    gp_ref,
    a3_ref,
    a3m_ref,
    qw_ref,
    kwt_ref,
    kwtm_ref,
    vw_ref,
    vwm_ref,
    ew_ref,
    ewm_ref,
    stat_ref,
    *refs,
):
    source_refs, refs = refs[: len(sources.arrays)], refs[len(sources.arrays) :]
    bm_ref, gwkv_ref, gwm_ref, bf_ref, gu_ref, ba_ref, gh_ref, do_ref, dd_ref, dsm_ref = refs[:10]
    gkvm_ref, init_ref, gains_ref, sent_ref, carry, grad_buffer, grad_sems = refs[10:]
    gout_ref = sources.rows_of(
        source_refs, segs, lambda s: segs - 1 - s, place_ref[0], grad_buffer, grad_sems
    )
    step = pl.program_id(0)
    width = wao_ref.shape[0]
    ff = wout_ref.shape[0]
    seg = q_ref.shape[2]
    slots = a1m_ref.shape[2]
    reset = stat_ref[0, 5:6, :slots] > 0.0

    @pl.when(step == 0)
    def _():
        carry[...] = carry0_ref[...].astype(F32)
        init_ref[...] = jnp.zeros_like(init_ref)
        gains_ref[...] = jnp.zeros_like(gains_ref)

    ga, gf, gw = gain_tiles(weights_gains_ref)
    gai, gfi, gwi = 1.0 / ga, 1.0 / gf, 1.0 / gw
    own = head_mask(width, HEADS * slots)
    rm = stat_ref[0, 4:5, :slots]

    grad_mem = gout_ref[seg:, :].astype(F32).T + carry[...]
    branch_mem = grad_mem.astype(BF16)
    bm_ref[0] = branch_mem
    grad_watt = nn(wwo_ref[...], branch_mem).astype(BF16)
    inverse = stat_ref[0, 3:4, :]
    scaled = (jnp.where(own, nn(grad_watt, spread_ref[...]), 0.0) * inverse).astype(BF16)
    raised = ew_ref[0].astype(F32)
    mem_raised = ewm_ref[0].astype(F32)
    grad_probs = nn(vw_ref[0], scaled)
    mem_grad_probs = nn(vwm_ref[0], scaled)
    dots = (
        jnp.sum(raised * grad_probs, axis=0, keepdims=True)
        + jnp.sum(mem_raised * mem_grad_probs, axis=0, keepdims=True)
    ) * inverse
    grad_scores = (raised * (grad_probs - dots)).astype(BF16)
    mem_grad_scores = (mem_raised * (mem_grad_probs - dots)).astype(BF16)
    gwkv_ref[:width, :] = nt(qw_ref[0], grad_scores).astype(BF16)
    gwkv_ref[width:, :] = nt(scaled, ew_ref[0]).astype(BF16)
    grad_q = (nn(kwt_ref[0], grad_scores) + nn(kwtm_ref[0], mem_grad_scores)) * HEAD_DIM**-0.5
    gwm_ref[0, :width, :] = nn(jnp.where(own, grad_q, 0.0).astype(BF16), fold_ref[...]).astype(BF16)
    gwm_ref[0, width : 2 * width, :] = nt(qw_ref[0], mem_grad_scores).astype(BF16)
    gwm_ref[0, 2 * width :, :] = nt(scaled, ewm_ref[0]).astype(BF16)

    grad_a3 = nn(ww_ref[:, width:], gwkv_ref[...])
    grad_a3m = nn(ww_ref[...], gwm_ref[0])
    part, weighed = norm_back(
        grad_a3, a3_ref[...].astype(F32), stat_ref[0, 2:3, :], wide(gw, seg), wide(gwi, seg)
    )
    mem_part, mem_weighed = norm_back(
        grad_a3m, a3m_ref[0].astype(F32), rm, gw[:, :slots], gwi[:, :slots]
    )
    gains_ref[2] += lane_sums(weighed)
    gains_ref[2, :, :slots] += mem_weighed
    grad_mem_in = grad_mem + mem_part
    gh_ref[0] = gout_ref[:seg, :].astype(F32).T + part

    bf_ref[...] = gh_ref[0].astype(BF16)
    branch = bf_ref[...]
    for at in range(0, ff, 512):
        grad_z = nn(wout_ref[at : at + 512, :], branch)
        gu_ref[at : at + 512, :] = (grad_z * gp_ref[0, at : at + 512, :].astype(F32)).astype(BF16)
    grad_a2 = nn(win_ref[...], gu_ref[...])
    part, weighed = norm_back(
        grad_a2, a2_ref[...].astype(F32), stat_ref[0, 1:2, :], wide(gf, seg), wide(gfi, seg)
    )
    gains_ref[1] += lane_sums(weighed)
    gh_ref[0] += part

    ba_ref[...] = gh_ref[0].astype(BF16)
    grad_att = nn(wao_ref[...], ba_ref[...]).astype(BF16)
    products = grad_att.astype(F32) * att_ref[...].astype(F32)
    rows = []
    dots = []
    for head in range(HEADS):
        span = slice(head * HEAD_DIM, (head + 1) * HEAD_DIM)
        inverse = stat_ref[0, 8 + head : 9 + head, :]
        dots.append(jnp.sum(products[span, :], axis=0, keepdims=True) * inverse)
        rows.append((grad_att[span, :].astype(F32) * inverse).astype(BF16))
    scaled = jnp.concatenate(rows, axis=0)
    do_ref[0] = scaled
    dd_ref[0] = jnp.concatenate(dots, axis=0)
    mem_values = jnp.concatenate([vm_ref[0].astype(F32)] * HEADS, axis=0)
    mem_values = jnp.where(own, mem_values, 0.0).astype(BF16)
    grad_probs = nn(mem_values, scaled)
    parts = []
    for head in range(HEADS):
        span = slice(head * slots, (head + 1) * slots)
        parts.append(
            (em_ref[0, span, :].astype(F32) * (grad_probs[span, :] - dots[head])).astype(BF16)
        )
    grad_scores = jnp.concatenate(parts, axis=0)
    dsm_ref[0] = grad_scores
    grad_k = jnp.where(own, nt(q_ref[0], grad_scores), 0.0).astype(BF16)
    grad_v = jnp.where(own, nt(scaled, em_ref[0]), 0.0).astype(BF16)
    gkvm_ref[0, :width, :] = nn(grad_k, fold_ref[...]).astype(BF16)
    gkvm_ref[0, width:, :] = nn(grad_v, fold_ref[...]).astype(BF16)
    grad_a1m = nn(wqkv_ref[:, width:], gkvm_ref[0])
    mem_part, mem_weighed = norm_back(
        grad_a1m, a1m_ref[0].astype(F32), rm, ga[:, :slots], gai[:, :slots]
    )
    gains_ref[0, :, :slots] += mem_weighed
    grad_mem_in = grad_mem_in + mem_part
    init_ref[...] += jnp.where(reset, grad_mem_in, 0.0)
    carry[...] = jnp.where(reset, 0.0, grad_mem_in).astype(BF16).astype(F32)
    sent_ref[...] = carry[...].astype(BF16)


def attention_kernel(
    place_ref,
    do_ref,
    dd_ref,
    dsm_ref,
    gh_ref,
    q_ref,
    kt_ref,
    ktm_ref,
    v_ref,
    e_ref,
    a1_ref,
    stat_ref,
    gains_ref,
    wqkv_ref,
    *refs,
):
    gqkv_ref, out_ref, gain_ref = refs[-3:]
    pair = pl.program_id(1)
    width = wqkv_ref.shape[0]
    seg = q_ref.shape[2]
    for half in range(2):
        head = pair * 2 + half
        base = pl.multiple_of(head * HEAD_DIM, HEAD_DIM)
        span = slice(half * HEAD_DIM, (half + 1) * HEAD_DIM)
        grads = do_ref[0, span, :]
        blank = jnp.zeros_like(grads)
        padded = jnp.concatenate([grads, blank] if half == 0 else [blank, grads], axis=0)
        dots = dd_ref[0, pl.ds(head, 1), :]
        grad_probs = nn(v_ref[0], padded)
        inner = (e_ref[0, half].astype(F32) * (grad_probs - dots)).astype(BF16)
        grad_q = nn(kt_ref[0, span, :], inner) + nn(ktm_ref[0, span, :], dsm_ref[0, span, :])
        gqkv_ref[pl.ds(base, HEAD_DIM), :] = (grad_q * HEAD_DIM**-0.5).astype(BF16)
        gqkv_ref[pl.ds(width + base, HEAD_DIM), :] = nt(q_ref[0, span, :], inner).astype(BF16)
        gqkv_ref[pl.ds(2 * width + base, HEAD_DIM), :] = nt(grads, e_ref[0, half]).astype(BF16)

    @pl.when((pl.program_id(0) == 0) & (pair == 0))
    def _():
        gain_ref[...] = jnp.zeros_like(gain_ref)

    @pl.when(pair == pl.num_programs(1) - 1)
    def _():
        grad_a1 = nn(wqkv_ref[...], gqkv_ref[...])
        (ga,) = gain_tiles(gains_ref, 1)
        part, weighed = norm_back(
            grad_a1,
            a1_ref[...].astype(F32),
            stat_ref[0, 0:1, :],
            wide(ga, seg),
            wide(1.0 / ga, seg),
        )
        gain_ref[...] += lane_sums(weighed)
        out_ref[0] = (gh_ref[0] + part).T.astype(BF16)


def whole(array):
    zeros = (0,) * array.ndim
    return pl.BlockSpec(array.shape, lambda *unused: zeros, pipeline_mode=pl.Buffered(1))


def params():
    return pltpu.CompilerParams(dimension_semantics=("arbitrary",), vmem_limit_bytes=VMEM_LIMIT)


def cost(microseconds):
    return pl.CostEstimate(
        flops=int(microseconds * 1e9), bytes_accessed=1 << 20, transcendentals=0
    )


def forward_chain(sources, place, first, count, mem0, consts, w, before=None):
    segs = consts["segs"]
    seg = consts["seg"]
    width, slots = mem0.shape
    ff = w["in_t"].shape[0]

    def flat(height):
        return (
            jax.ShapeDtypeStruct((height, segs * seg), BF16),
            pl.BlockSpec((height, seg), lambda s, f: (0, s + first)),
        )

    def stack(*shape, dtype=BF16):
        tail = (0,) * len(shape)
        return (
            jax.ShapeDtypeStruct((segs,) + shape, dtype),
            pl.BlockSpec((1,) + shape, lambda s, f: (s + first,) + tail),
        )

    outs = dict(
        enc=stack(seg + slots, width),
        a1=flat(width),
        a1m=stack(width, slots),
        q=stack(width, seg),
        kt=stack(width, seg),
        ktm=stack(width, slots),
        v=stack(seg, width),
        vm=stack(slots, width),
        e=stack(HEADS, seg, seg),
        em=stack(HEADS * slots, seg),
        att=flat(width),
        a2=flat(width),
        z=flat(ff),
        gp=stack(ff, seg),
        a3=flat(width),
        a3m=stack(width, slots),
        qw=stack(width, HEADS * slots),
        kwt=stack(width, seg),
        kwtm=stack(width, slots),
        vw=stack(seg, width),
        vwm=stack(slots, width),
        ew=stack(seg, HEADS * slots),
        ewm=stack(slots, HEADS * slots),
        watt=stack(width, slots),
        stat=stack(16, seg, dtype=F32),
        last=(
            jax.ShapeDtypeStruct((width, slots), BF16),
            pl.BlockSpec((width, slots), lambda s, f: (0, 0)),
        ),
    )
    fixed = [
        mem0,
        consts["init"],
        consts["gains"],
        consts["spread"],
        consts["fold"],
        w["qkv_t"],
        w["ao_t"],
        w["in_t"],
        w["out"],
        w["write_t"],
        w["wo_t"],
    ]
    passed = [] if before is None else [before[name] for name in outs if name != "last"]
    in_count = 1 + len(fixed) + len(sources.arrays)
    results = pl.pallas_call(
        lambda *refs: forward_kernel(sources, first, count, *refs),
        grid_spec=pltpu.PrefetchScalarGridSpec(
            num_scalar_prefetch=1,
            grid=(count,),
            in_specs=[whole(a) for a in fixed]
            + [pl.BlockSpec(memory_space=pl.ANY)] * (len(sources.arrays) + len(passed)),
            out_specs=[spec for _, spec in outs.values()],
            scratch_shapes=[
                pltpu.VMEM((width, slots), F32),
                pltpu.VMEM((seg, seg), F32),
                pltpu.VMEM((seg, width), BF16),
                pltpu.VMEM((slots, width), BF16),
                pltpu.VMEM((width, seg), BF16),
                pltpu.VMEM((width, slots), BF16),
                pltpu.VMEM((width, seg), F32),
                pltpu.VMEM((2, seg + 16, width), BF16),
                pltpu.SemaphoreType.DMA((2,)),
            ],
        ),
        out_shape=[shape for shape, _ in outs.values()],
        input_output_aliases={in_count + at: at for at in range(len(passed))},
        compiler_params=params(),
        cost_estimate=cost(18 * count),
        name="forward_chain",
    )(place, *fixed, *sources.arrays, *passed)
    return dict(zip(outs, results))


def backward_chain(kept, sources, place, carry0, consts, w):
    segs = consts["segs"]
    width, slots = kept["a1m"].shape[1:]
    seg = kept["q"].shape[2]
    ff = kept["gp"].shape[1]
    last = segs - 1

    def flat(height):
        return (
            jax.ShapeDtypeStruct((height, segs * seg), BF16),
            pl.BlockSpec((height, seg), lambda s, f: (0, last - s)),
        )

    def stack(*shape, dtype=BF16):
        tail = (0,) * len(shape)
        return (
            jax.ShapeDtypeStruct((segs,) + shape, dtype),
            pl.BlockSpec((1,) + shape, lambda s, f: (last - s,) + tail),
        )

    def single(*shape, dtype=F32):
        tail = (0,) * len(shape)
        return (jax.ShapeDtypeStruct(shape, dtype), pl.BlockSpec(shape, lambda s, f: tail))

    outs = dict(
        bm=stack(width, slots),
        gwkv=flat(2 * width),
        gwm=stack(3 * width, slots),
        bf=flat(width),
        gu=flat(ff),
        ba=flat(width),
        gh=stack(width, seg, dtype=F32),
        do=stack(width, seg),
        dd=stack(HEADS, seg, dtype=F32),
        dsm=stack(HEADS * slots, seg),
        gkvm=stack(2 * width, slots),
        init=single(width, slots),
        gains=single(3, width, 128),
        sent=single(width, slots, dtype=BF16),
    )
    fixed = [
        carry0,
        consts["gains"],
        consts["spread"],
        consts["fold"],
        w["qkv"],
        w["ao"],
        w["in"],
        w["out"],
        w["write"],
        w["wo"],
    ]
    blocked = ["a1m", "q", "vm", "em", "att", "a2", "gp", "a3", "a3m", "qw"]
    blocked += ["kwt", "kwtm", "vw", "vwm", "ew", "ewm", "stat"]

    def spec_of(array):
        if array.ndim == 2:
            return pl.BlockSpec((array.shape[0], seg), lambda s, f: (0, last - s))
        tail = (0,) * (array.ndim - 1)
        return pl.BlockSpec((1,) + array.shape[1:], lambda s, f: (last - s,) + tail)

    results = pl.pallas_call(
        lambda *refs: chain_kernel(sources, segs, *refs),
        grid_spec=pltpu.PrefetchScalarGridSpec(
            num_scalar_prefetch=1,
            grid=(segs,),
            in_specs=[whole(a) for a in fixed]
            + [spec_of(kept[name]) for name in blocked]
            + [pl.BlockSpec(memory_space=pl.ANY)] * len(sources.arrays),
            out_specs=[spec for _, spec in outs.values()],
            scratch_shapes=[
                pltpu.VMEM((width, slots), F32),
                pltpu.VMEM((2, seg + slots, width), BF16),
                pltpu.SemaphoreType.DMA((2,)),
            ],
        ),
        out_shape=[shape for shape, _ in outs.values()],
        compiler_params=params(),
        cost_estimate=cost(11 * segs),
        name="backward_chain",
    )(place, *fixed, *[kept[name] for name in blocked], *sources.arrays)
    return dict(zip(outs, results))


def attention_back(kept, grads, which, consts, w, before):
    segs, width, seg = kept["q"].shape
    count = which.shape[0]
    pair = 2 * HEAD_DIM

    def by_pair(rows, lanes):
        return pl.BlockSpec((1, rows, lanes), lambda s, h, f: (f[s], h, 0))

    def by_seg(array):
        tail = (0,) * (array.ndim - 1)
        return pl.BlockSpec((1,) + array.shape[1:], lambda s, h, f: (f[s],) + tail)

    inputs = [
        (grads["do"], by_pair(pair, seg)),
        (grads["dd"], by_seg(grads["dd"])),
        (grads["dsm"], by_pair(pair, seg)),
        (grads["gh"], by_seg(grads["gh"])),
        (kept["q"], by_pair(pair, seg)),
        (kept["kt"], by_pair(pair, seg)),
        (kept["ktm"], by_pair(pair, kept["ktm"].shape[2])),
        (kept["v"], pl.BlockSpec((1, seg, pair), lambda s, h, f: (f[s], 0, h))),
        (kept["e"], pl.BlockSpec((1, 2, seg, seg), lambda s, h, f: (f[s], h, 0, 0))),
        (kept["a1"], pl.BlockSpec((width, seg), lambda s, h, f: (0, f[s]))),
        (kept["stat"], by_seg(kept["stat"])),
        (consts["gains"], whole(consts["gains"])),
        (w["qkv"], whole(w["qkv"])),
    ]
    passed = [] if before is None else [before]
    return pl.pallas_call(
        attention_kernel,
        grid_spec=pltpu.PrefetchScalarGridSpec(
            num_scalar_prefetch=1,
            grid=(count, HEADS // 2),
            in_specs=[spec for _, spec in inputs]
            + [pl.BlockSpec(memory_space=pl.ANY)] * len(passed),
            out_specs=[
                pl.BlockSpec((3 * width, seg), lambda s, h, f: (0, f[s])),
                pl.BlockSpec((1, seg, width), lambda s, h, f: (s, 0, 0)),
                pl.BlockSpec((width, 128), lambda s, h, f: (0, 0)),
            ],
        ),
        out_shape=[
            jax.ShapeDtypeStruct((3 * width, segs * seg), BF16),
            jax.ShapeDtypeStruct((count, seg, width), BF16),
            jax.ShapeDtypeStruct((width, 128), F32),
        ],
        input_output_aliases={1 + len(inputs): 0} if passed else {},
        compiler_params=pltpu.CompilerParams(
            dimension_semantics=("arbitrary", "arbitrary"), vmem_limit_bytes=VMEM_LIMIT
        ),
        cost_estimate=cost(10 * count),
        name="attention_back",
    )(which, *[array for array, _ in inputs], *passed)


def swap_pairs(value, axis, mask):
    size = lax.axis_size(axis)
    return lax.ppermute(value, axis, [(i, i ^ mask) for i in range(size)])


def sum_phases(dp_first):
    section = [("section", 1 << at) for at in range(lax.axis_size("section").bit_length() - 1)]
    dp = [("dp", 1 << at) for at in range(lax.axis_size("dp").bit_length() - 1)]
    phases = [(step, step) for step in section[:1]]
    crossed = []
    if len(section) > 1 and dp:
        crossed = [(dp[0], section[1]), (section[1], dp[0])]
        section, dp = section[2:], dp[1:]
    else:
        section = section[1:]
    straight = [(step, step) for step in dp + section]
    return phases + (straight + crossed if dp_first else crossed + straight)


def phase_swap(value, phase):
    sections, dps = lax.axis_size("section"), lax.axis_size("dp")
    route = []
    for section in range(sections):
        axis, mask = phase[section % 2]
        for dp in range(dps):
            to = ((section ^ mask) * dps + dp) if axis == "section" else (section * dps + (dp ^ mask))
            route.append((section * dps + dp, to))
    return lax.ppermute(value, ("section", "dp"), route)


def phase_bit(phase):
    bits = [(lax.axis_index(axis) // mask) % 2 for axis, mask in phase]
    return jnp.where(lax.axis_index("section") % 2 == 0, bits[0], bits[1])


def half_of(value, side):
    half = value.shape[0] // 2
    return lax.dynamic_slice_in_dim(value, side * half, half, 0)


def fetch(source, target, sem):
    copy = pltpu.make_async_copy(source, target, sem)
    copy.start()
    return copy


def slot_sum(left, right):
    join = lambda ref: jnp.concatenate([ref[at] for at in range(ref.shape[0])], axis=1)
    return nt(join(left), join(right))


def early_weights_kernel(
    side_ref, a2_ref, gu_ref, bf_ref, z_ref, a3_ref, gwkv_ref, a3m_ref, gwm_ref, watt_ref, bm_ref, *refs
):
    out_ref, a2, gu, z, bf, a3, gw, a3m, gwm, left, right, staged, in_sems, out_sems = refs
    side = side_ref[0]
    width = a2.shape[0]
    folds = gu.shape[0]
    base = side * (folds * width)
    loads = []

    def load(source, target):
        loads.append(fetch(source, target, in_sems.at[len(loads)]))

    def wait(count):
        for _ in range(count):
            loads[wait.done].wait()
            wait.done += 1

    wait.done = 0
    load(a2_ref, a2)
    for at in range(folds):
        rows = pl.ds(pl.multiple_of(base + at * width, width), width)
        load(gu_ref.at[rows, :], gu.at[at])
    load(bf_ref, bf)
    for at in range(folds):
        rows = pl.ds(pl.multiple_of(base + at * width, width), width)
        load(z_ref.at[rows, :], z.at[at])
    load(a3_ref, a3)
    load(gwkv_ref.at[pl.ds(pl.multiple_of(side * width, width), width), :], gw)
    load(a3m_ref, a3m)
    load(gwm_ref.at[:, pl.ds(pl.multiple_of((1 + side) * width, width), width), :], gwm)
    last = in_sems.at[len(loads)]

    @pl.when(side == 0)
    def _():
        pltpu.make_async_copy(a3m_ref, left, last).start()
        pltpu.make_async_copy(gwm_ref.at[:, pl.ds(0, width), :], right, last).start()

    @pl.when(side == 1)
    def _():
        pltpu.make_async_copy(watt_ref, left, last).start()
        pltpu.make_async_copy(bm_ref, right, last).start()

    stores = []

    def put(tile, value):
        columns = slice(tile * width, (tile + 1) * width)
        staged[:, columns] = value.astype(BF16)
        stores.append(fetch(staged.at[:, columns], out_ref.at[:, columns], out_sems.at[tile]))

    wait(1)
    for at in range(folds):
        wait(1)
        put(at, nt(a2[...], gu[at]))
    wait(1)
    for at in range(folds):
        wait(1)
        put(folds + at, nt(z[at], bf[...]))
    wait(4)
    put(2 * folds, nt(a3[...], gw[...]) + slot_sum(a3m, gwm))
    pltpu.make_async_copy(watt_ref, left, last).wait()
    pltpu.make_async_copy(bm_ref, right, last).wait()
    put(2 * folds + 1, slot_sum(left, right))
    for store in stores:
        store.wait()


def early_weights(kept, grads, side):
    width, tokens = kept["a2"].shape
    folds = kept["z"].shape[0] // 2 // width
    inputs = [kept["a2"], grads["gu"], grads["bf"], kept["z"], kept["a3"], grads["gwkv"]]
    inputs += [kept["a3m"], grads["gwm"], kept["watt"], grads["bm"]]
    anywhere = pl.BlockSpec(memory_space=pl.ANY)
    full = pltpu.VMEM((width, tokens), BF16)
    several = pltpu.VMEM((folds, width, tokens), BF16)
    slots = pltpu.VMEM(kept["a3m"].shape, BF16)
    out = jax.ShapeDtypeStruct((width, (2 * folds + 2) * width), BF16)
    return pl.pallas_call(
        early_weights_kernel,
        grid_spec=pltpu.PrefetchScalarGridSpec(
            num_scalar_prefetch=1,
            grid=(1,),
            in_specs=[anywhere] * len(inputs),
            out_specs=anywhere,
            scratch_shapes=[full, several, several, full, full, full]
            + [slots] * 4
            + [
                pltpu.VMEM(out.shape, BF16),
                pltpu.SemaphoreType.DMA((7 + 2 * folds,)),
                pltpu.SemaphoreType.DMA((2 * folds + 2,)),
            ],
        ),
        out_shape=out,
        compiler_params=params(),
        cost_estimate=cost(9),
        name="early_weights",
    )(side, *inputs)


def late_weights_kernel(count, side_ref, a1_ref, gqkv_ref, att_ref, ba_ref, a1m_ref, gkvm_ref, *refs):
    init_ref, gains_ref, refs = refs[0], refs[1], refs[2:]
    part_refs, refs = refs[:count], refs[count:]
    out_ref, a1, main, left, right, a1m, gkvm, init, gains, parts, staged, in_sems, out_sems = refs
    side = side_ref[0]
    width = a1.shape[0]
    slots = init.shape[1]
    rows = pl.ds(pl.multiple_of((1 + side) * width, width), width)
    kv_rows = pl.ds(pl.multiple_of(side * width, width), width)
    loads = [
        fetch(a1_ref, a1, in_sems.at[0]),
        fetch(gqkv_ref.at[rows, :], main, in_sems.at[1]),
        fetch(a1m_ref, a1m, in_sems.at[2]),
        fetch(gkvm_ref.at[:, kv_rows, :], gkvm, in_sems.at[3]),
    ]

    @pl.when(side == 0)
    def _():
        pltpu.make_async_copy(a1_ref, left, in_sems.at[4]).start()
        pltpu.make_async_copy(gqkv_ref.at[pl.ds(0, width), :], right, in_sems.at[5]).start()

    @pl.when(side == 1)
    def _():
        pltpu.make_async_copy(att_ref, left, in_sems.at[4]).start()
        pltpu.make_async_copy(ba_ref, right, in_sems.at[5]).start()

    others = [fetch(init_ref, init, in_sems.at[6]), fetch(gains_ref, gains, in_sems.at[7])]
    others += [fetch(ref, parts.at[at], in_sems.at[8 + at]) for at, ref in enumerate(part_refs)]
    stores = []

    def put(columns, value):
        staged[:, columns] = value.astype(BF16)
        stores.append(fetch(staged.at[:, columns], out_ref.at[:, columns], out_sems.at[len(stores)]))

    for load in loads:
        load.wait()
    put(slice(0, width), nt(a1[...], main[...]) + slot_sum(a1m, gkvm))
    pltpu.make_async_copy(att_ref, left, in_sems.at[4]).wait()
    pltpu.make_async_copy(ba_ref, right, in_sems.at[5]).wait()
    put(slice(width, 2 * width), nt(left[...], right[...]))
    for load in others:
        load.wait()
    columns = [gains[0], gains[1], gains[2]]
    for at in range(count):
        columns[0] = columns[0] + parts[at]
    lane = lax.broadcasted_iota(jnp.int32, init.shape, 1)
    extras = jnp.zeros(init.shape, F32)
    for at, column in enumerate(columns):
        extras = jnp.where(lane == at, jnp.sum(column, axis=1, keepdims=True), extras)
    extras = jnp.where(side == 0, init[...], extras)
    extras = jnp.concatenate([extras, jnp.zeros_like(extras)], axis=1)
    put(slice(2 * width, 2 * width + 2 * slots), extras)
    for store in stores:
        store.wait()


def late_weights(kept, grads, gqkv, gain_parts, side):
    width, tokens = kept["a1"].shape
    count = len(gain_parts)
    inputs = [kept["a1"], gqkv, kept["att"], grads["ba"], kept["a1m"], grads["gkvm"]]
    inputs += [grads["init"], grads["gains"]] + list(gain_parts)
    slots = grads["init"].shape[1]
    anywhere = pl.BlockSpec(memory_space=pl.ANY)
    full = pltpu.VMEM((width, tokens), BF16)
    small = pltpu.VMEM(kept["a1m"].shape, BF16)
    out = jax.ShapeDtypeStruct((width, 2 * width + 2 * slots), BF16)
    return pl.pallas_call(
        lambda *refs: late_weights_kernel(count, *refs),
        grid_spec=pltpu.PrefetchScalarGridSpec(
            num_scalar_prefetch=1,
            grid=(1,),
            in_specs=[anywhere] * len(inputs),
            out_specs=anywhere,
            scratch_shapes=[full] * 4
            + [small] * 2
            + [
                pltpu.VMEM(grads["init"].shape, F32),
                pltpu.VMEM(grads["gains"].shape, F32),
                pltpu.VMEM((count,) + gain_parts[0].shape, F32),
                pltpu.VMEM(out.shape, BF16),
                pltpu.SemaphoreType.DMA((8 + count,)),
                pltpu.SemaphoreType.DMA((3,)),
            ],
        ),
        out_shape=out,
        compiler_params=params(),
        cost_estimate=cost(4),
        name="late_weights",
    )(side, *inputs)


class Sum:
    def __init__(self, value, share, dp_first=False):
        self.phases = sum_phases(dp_first)
        inner = self.phases[1:]
        self.value = value
        self.share = share
        halvings = 0
        while halvings < len(inner) - 1 and value.shape[0] >> (halvings + 1) >= 16:
            halvings += 1
        self.halved = inner[:halvings]
        self.steps = [("halve", phase) for phase in self.halved]
        self.steps += [("add", phase) for phase in inner[halvings:]]
        self.steps += [("double", phase) for phase in reversed(self.halved)]
        self.steps += [("last", self.phases[0])]
        self.started = None

    def prepare(self):
        kind, phase = self.steps.pop(0)
        if kind == "halve":
            bit = phase_bit(phase)
            value = self.value
            self.sent, self.value = half_of(value, 1 - bit), half_of(value, bit)
            if self.share is not None:
                self.sent = self.sent + half_of(self.share, 1 - bit)
                self.value = self.value + half_of(self.share, bit)
        else:
            if self.share is not None:
                self.value = self.value + self.share
            self.sent = self.value
        self.share = None
        self.ready = (kind, phase)

    def launch(self):
        kind, phase = self.ready
        self.started = (kind, phase_swap(self.sent, phase))

    def finish(self, *after):
        kind, other = self.started
        self.started = None
        if after:
            other = tied(other, *after)
        if kind in ("halve", "add"):
            self.value = self.value + other
        elif kind == "double":
            self.value = jnp.concatenate([self.value, other], axis=0)
        else:
            self.value = (self.value, other)

    def places(self):
        own = sum(phase_bit(phase) << at for at, phase in enumerate(reversed(self.halved)))
        swapped = [(late, early) for early, late in self.halved]
        other = sum(phase_bit(phase) << at for at, phase in enumerate(reversed(swapped)))
        numbers = jnp.stack([phase_bit(self.phases[0]), jnp.int32(own), jnp.int32(other)])
        return numbers.astype(jnp.int32), 1 << len(self.halved)


def advance(totals, *after, extra=()):
    going = []
    for total in totals:
        if total.started is not None:
            total.finish(*after)
        if total.steps:
            total.prepare()
            going.append(total)
    joined = lax.optimization_barrier(tuple(total.sent for total in going) + tuple(extra))
    for total, sent in zip(going, joined):
        if total.value is total.sent:
            total.value = sent
        total.sent = sent
        total.launch()
    return list(joined[: len(going)]), list(joined[len(going) :])


def unpack_kernel(count, regions, place_ref, own_ref, other_ref, *refs):
    outs = len(refs) // 2
    out_refs, staged, sems = refs[:outs], refs[outs : 2 * outs], refs[2 * outs]
    rows = own_ref.shape[0] // count

    def take(ref, side, number, sem):
        copies = []
        for start, stop, at, top, left in regions[side]:
            for block in range(count):
                target = pl.multiple_of(top + (block ^ place_ref[number]) * rows, rows)
                value = ref[block * rows : (block + 1) * rows, start:stop].astype(F32)
                staged[at][pl.ds(target, rows), left : left + stop - start] = value
            slab = (pl.ds(top, own_ref.shape[0]), pl.ds(left, stop - start))
            copies.append((staged[at].at[slab], out_refs[at].at[slab], sems.at[sem + len(copies)]))
            pltpu.make_async_copy(*copies[-1]).start()
        return copies

    for side in range(2):

        @pl.when(place_ref[0] == side)
        def _():
            copies = take(own_ref, side, 1, 0)
            copies += take(other_ref, 1 - side, 2, len(copies))
            for copy in copies:
                pltpu.make_async_copy(*copy).wait()


def unpacked(total, regions, shapes):
    own, other = total.value
    places, count = total.places()
    vmem = pl.BlockSpec(memory_space=pltpu.VMEM)
    return pl.pallas_call(
        lambda *refs: unpack_kernel(count, regions, *refs),
        in_specs=[pl.BlockSpec(memory_space=pltpu.SMEM), vmem, vmem],
        out_specs=[pl.BlockSpec(memory_space=pl.ANY)] * len(shapes),
        out_shape=[jax.ShapeDtypeStruct(shape, F32) for shape in shapes],
        scratch_shapes=[pltpu.VMEM(shape, F32) for shape in shapes]
        + [pltpu.SemaphoreType.DMA((len(regions[0]) + len(regions[1]),))],
        compiler_params=pltpu.CompilerParams(vmem_limit_bytes=VMEM_LIMIT),
        cost_estimate=cost(4),
        name="unpack",
    )(places, own, other)


def pieces_in(value, place):
    parts = [lax.dynamic_index_in_dim(value, place, 0, keepdims=True)]
    sent = []
    for mask in range(1, lax.axis_size("section")):
        sent.append(lax.dynamic_index_in_dim(value, place ^ mask, 0, keepdims=True))
        parts.append(swap_pairs(sent[-1], "section", mask))
    return in_rank_order(jnp.concatenate(parts, axis=0), place), sent, parts[1:]


def in_rank_order(pieces, place):
    count = pieces.shape[0]
    return jnp.stack(
        [lax.dynamic_index_in_dim(pieces, at ^ place, 0, keepdims=False) for at in range(count)]
    )


def rank_sources(arrays, place, after):
    sections = lax.axis_size("section")
    payload = []
    for mask in range(1, sections):
        picked = [lax.dynamic_index_in_dim(a, place ^ mask, 0, keepdims=True) for a in arrays]
        payload.append(jnp.concatenate(picked, axis=1))
    payload[1:] = lax.optimization_barrier(tuple(payload[1:]))
    payload[0] = tied(payload[0], *payload[1:])
    early = []
    for mask in range(1, sections):
        route = [(i, i ^ mask) for i in range(sections) if mask == 1 or i != 1]
        early.append(lax.ppermute(payload[mask - 1], "section", route))
    late = [
        lax.ppermute(tied(payload[mask - 1], *after), "section", [(1, 1 ^ mask)])
        for mask in range(2, sections)
    ]
    own = len(arrays)

    def choose(at, here):
        mask = at ^ here
        yield mask == 0, [(number, here) for number in range(own)]
        for other in range(1, sections):
            yield (mask == other) & ((at != 1) | (other == 1)), [(own + other - 1, 0)]

    def choose_late(at, here):
        yield from choose(at, here)
        for other in range(2, sections):
            yield (at == 1) & ((at ^ here) == other), [(own + sections - 1 + other - 2, 0)]

    return Sources(list(arrays) + early, choose), Sources(list(arrays) + early + late, choose_late)


def sources_in(arrays, place):
    sections = lax.axis_size("section")
    sent, pieces = [], []
    for mask in range(1, sections):
        picked = [lax.dynamic_index_in_dim(a, place ^ mask, 0, keepdims=True) for a in arrays]
        sent.append(jnp.concatenate(picked, axis=1))
        pieces.append(swap_pairs(sent[-1], "section", mask))
    own = len(arrays)

    def choose(at, here):
        yield (at ^ here) == 0, [(number, here) for number in range(own)]
        for other in range(1, sections):
            yield (at ^ here) == other, [(own + other - 1, 0)]

    return Sources(list(arrays) + pieces, choose), sent


def gathered_sources(arrays, chunks):
    rows = gathered_in(jnp.concatenate(arrays, axis=1), chunks)
    return Sources([rows], lambda at, here: [(at >= 0, [(0, at)])])


def gathered_in(value, chunks):
    place = lax.axis_index("section")
    gathered = lax.all_gather(value, "section")
    own = lax.dynamic_index_in_dim(gathered, place // chunks, 1, keepdims=False)
    count = gathered.shape[0] // chunks
    return lax.dynamic_slice_in_dim(own, (place % chunks) * count, count, 0)


def gathered_out(value, chunks):
    place = lax.axis_index("section")
    gathered = lax.all_gather(value, "section")
    sections = gathered.shape[0]
    by_stream = gathered.reshape((sections // chunks, chunks * value.shape[0]) + value.shape[1:])
    return lax.dynamic_index_in_dim(by_stream, place, 1, keepdims=False)


def tied(value, *others):
    return lax.optimization_barrier((value,) + others)[0]


def body(
    tokens,
    doc_ids,
    reset_flags,
    attn_gain,
    w_qkv,
    w_attn_out,
    ffn_gain,
    w_in,
    w_out,
    write_gain,
    w_write,
    w_write_out,
    init_memory,
    out_grad,
    memory_grad,
):
    streams, _, seg, width = tokens.shape
    slots = init_memory.shape[0]
    sections = lax.axis_size("section")
    chunks = sections // streams
    segs = sections // chunks
    place = lax.axis_index("section")

    spread = np.tile(np.eye(slots, dtype=np.float32), (1, HEADS))
    consts = dict(
        segs=segs,
        seg=seg,
        init=init_memory,
        gains=jnp.stack([attn_gain, ffn_gain, write_gain]).astype(F32),
        spread=jnp.asarray(spread, BF16),
        fold=jnp.asarray(spread.T, BF16),
    )
    w = dict(
        qkv=w_qkv,
        ao=w_attn_out,
        out=w_out,
        write=w_write,
        wo=w_write_out,
        qkv_t=w_qkv.T,
        ao_t=w_attn_out.T,
        in_t=w_in.T,
        write_t=w_write.T,
        wo_t=w_write_out.T,
    )
    w["in"] = w_in

    marks = jnp.concatenate(
        [doc_ids[:, 0], jnp.broadcast_to(reset_flags, (streams, seg))], axis=1
    ).reshape(streams, 2, seg)
    marks = jnp.pad(marks, ((0, 0), (0, 14), (0, 0))).astype(BF16)
    parts_in = [tokens[:, 0], marks]
    grads_in = [out_grad[:, 0], memory_grad[:, 0]]
    empty = jnp.zeros((width, slots), BF16)
    if chunks == 1:
        after = [w[name] for name in ("qkv_t", "in_t", "write_t")]
        first, rows = rank_sources(parts_in, place, after)
        xor = place
    else:
        first = rows = gathered_sources(parts_in, chunks)
        xor = 0
    xor = jnp.full((1,), xor, jnp.int32)

    arriving = empty
    for turn in range(chunks):
        start = forward_chain(first, xor, 0, 1, arriving, consts, w)
        if turn == 0 and chunks == 1:
            gout, sent = sources_in([tied(value, start["last"]) for value in grads_in], place)
            then = tied(xor, *sent)
        elif turn == 0:
            gout = gathered_sources(grads_in, chunks)
            then = xor
        kept = forward_chain(rows, then, 1, segs - 1, start["last"], consts, w, start)
        if turn < chunks - 1:
            arriving = lax.ppermute(
                kept["last"], "section", [(i, i + 1) for i in range(sections - 1)]
            )
    if chunks == 1:
        done, sent, pieces = pieces_in(kept["enc"], place)
        then = tied(xor, *sent)
    else:
        done = gathered_out(kept["enc"], chunks)
        pieces = []
        then = xor

    returning = empty
    for turn in range(chunks):
        grads = backward_chain(kept, gout, then, returning, consts, w)
        if turn < chunks - 1:
            returning = lax.ppermute(
                grads["sent"], "section", [(i + 1, i) for i in range(sections - 1)]
            )

    ff = w_in.shape[1]
    folds = ff // width
    cores = sum_phases(False)[0]
    side = phase_bit(cores).reshape(1)
    grads = dict(grads, gu=tied(grads['gu'], *pieces))
    sent = early_weights(kept, grads, 1 - side)
    share = phase_swap(sent, cores)
    early = Sum(early_weights(kept, grads, tied(side, sent)), share)
    after, _ = advance([early])
    order = [1, 2, 3, 0] if segs == 4 else list(range(segs - 1, -1, -1))
    gqkv = None
    gain_parts = []
    outgoing, incoming, arrived = {}, {}, []
    for at in order:
        which = tied(xor ^ at, *after, *arrived)
        gqkv, out, part = attention_back(kept, grads, which, consts, w, gqkv)
        gain_parts.append(part)
        after, (outgoing[at],) = advance([early], part, extra=[out])
        if chunks == 1:
            arrived = list(incoming.values())[-1:]
            incoming[at] = swap_pairs(outgoing[at], "section", at) if at else outgoing[at]

    sent = late_weights(kept, grads, gqkv, gain_parts, tied(1 - side, *after, *arrived))
    after, (sent,) = advance([early], sent, extra=[sent])
    share = phase_swap(sent, cores)
    mine = tied(side, sent, *after)
    late = Sum(late_weights(kept, grads, gqkv, gain_parts, mine), share)
    if chunks == 1:
        back = in_rank_order(jnp.concatenate([incoming[at] for at in range(segs)]), place)
    else:
        back = gathered_out(jnp.concatenate([outgoing[at] for at in range(segs)]), chunks)
    token_grads = back.astype(F32)

    half = ff // 2

    def paired(number, start, at):
        main = (start, start + width, at, 0, (1 + number) * width)
        other = (start + width, start + 2 * width, at + number, 0, 0)
        return [main, other]

    early_regions = [
        [(0, half, 0, 0, number * half)]
        + [
            (half + at * width, half + (at + 1) * width, 1, number * half + at * width, 0)
            for at in range(half // width)
        ]
        + paired(number, ff, 2)
        for number in range(2)
    ]
    late_regions = [
        paired(number, 0, 0) + [(2 * width, 2 * width + 128, 2 + number, 0, 0)]
        for number in range(2)
    ]
    square, triple = (width, width), (width, 3 * width)
    idle = [[token_grads], [done]]
    early_grads = None
    while late.steps or early_grads is None:
        if late.steps:
            advance([late], *(idle.pop(0) if idle else []))
        if early.steps:
            if len(late.steps) % 2 == 0:
                advance([early])
        elif early_grads is None and len(late.steps) % 2 == 0:
            early.finish()
            early_grads = unpacked(early, early_regions, [(width, ff), (ff, width), triple, square])
            idle.append([early_grads[0]])
    late.finish(*[value for values in idle for value in values])
    grad_in, grad_out, grad_write, grad_wo = early_grads
    grad_qkv, grad_ao, grad_init, gains = unpacked(
        late, late_regions, [triple, square, (width, 128), (width, 128)]
    )
    grad_init = grad_init[:, :slots].T
    gains = gains[:, :3].T / consts["gains"]
    return (
        done[:, None, :seg],
        done[:, None, seg:],
        token_grads[:, None],
        gains[0],
        grad_qkv,
        grad_ao,
        gains[1],
        grad_in,
        grad_out,
        gains[2],
        grad_write,
        grad_wo,
        grad_init,
    )


def solution(mesh):
    local = P("dp", "section")
    return jax.shard_map(
        body,
        mesh=mesh,
        in_specs=(local,) * 3 + (P(),) * 10 + (local,) * 2,
        out_specs=(local,) * 3 + (P(),) * 10,
        check_vma=False,
    )
```

```python
import jax
import jax.numpy as jnp
import numpy as np
from jax import lax
from jax.experimental import pallas as pl
from jax.experimental.pallas import tpu as pltpu
from jax.sharding import PartitionSpec as P

HEADS = 8
HEAD_DIM = 64
EPS = 1e-06
MASKED = -1000000000.0
F32 = jnp.float32
BF16 = jnp.bfloat16
SQRT_2_PI = 0.7978845608028654
CUBIC = 0.044715
VMEM_LIMIT = 60 * 1024 * 1024


def nn(left, right):
    return lax.dot_general(left, right, (((1,), (0,)), ((), ())), preferred_element_type=F32)


def tn(left, right):
    return lax.dot_general(left, right, (((0,), (0,)), ((), ())), preferred_element_type=F32)


def nt(left, right):
    return lax.dot_general(left, right, (((1,), (1,)), ((), ())), preferred_element_type=F32)


def wide(column_tile, width):
    copies = max(1, width // 128)
    if width < 128:
        return column_tile[:, :width]
    return jnp.concatenate([column_tile] * copies, axis=1)


def inverse_rms(values):
    return lax.rsqrt(jnp.mean(values * values, axis=0, keepdims=True) + EPS)


def lane_sums(values):
    total = values[:, :128]
    for at in range(128, values.shape[1], 128):
        total = total + values[:, at : at + 128]
    return total


def head_mask(rows, columns):
    row_head = lax.broadcasted_iota(jnp.int32, (rows, columns), 0) // HEAD_DIM
    column_head = lax.broadcasted_iota(jnp.int32, (rows, columns), 1) // HEAD_DIM
    return row_head == column_head


def norm_back(grad_normed, normed, scale, gain, gain_inverse):
    weighed = grad_normed * normed
    mean = jnp.mean(weighed, axis=0, keepdims=True)
    return scale * (grad_normed * gain - normed * gain_inverse * mean), weighed


def gain_tiles(gains_ref, count=3):
    tiles = []
    for at in range(count):
        row = gains_ref[at : at + 1, :]
        tiles.append(jnp.broadcast_to(row, (128, row.shape[1])).T)
    return tiles


class Sources:
    def __init__(self, arrays, choices):
        self.arrays = arrays
        self.choices = choices

    def start(self, refs, at, place, buffer, sem):
        for condition, parts in self.choices(at, place):

            @pl.when(condition)
            def _():
                top = 0
                for number, index in parts:
                    source = refs[number].at[index]
                    target = buffer.at[pl.ds(top, source.shape[0]), :]
                    pltpu.make_async_copy(source, target, sem).start()
                    top += source.shape[0]

    def wait(self, buffer, sem):
        pltpu.make_async_copy(buffer, buffer, sem).wait()

    def rows_of(self, refs, steps, segment, place, buffer, sems):
        step = pl.program_id(0)
        slot = lax.rem(step, 2)

        @pl.when(step == 0)
        def _():
            self.start(refs, segment(0), place, buffer.at[0], sems.at[0])

        if steps > 1:

            @pl.when(step + 1 < steps)
            def _():
                self.start(refs, segment(step + 1), place, buffer.at[1 - slot], sems.at[1 - slot])

        self.wait(buffer.at[slot], sems.at[slot])
        return buffer.at[slot]


def forward_kernel(
    sources,
    first,
    count,
    place_ref,
    mem0_ref,
    init_ref,
    gains_ref,
    spread_ref,
    fold_ref,
    *refs,
):
    wqkv_ref, wao_ref, win_ref, wout_ref, ww_ref, wwo_ref = refs[:6]
    refs = refs[6:]
    (
        enc_ref,
        a1_ref,
        a1m_ref,
        q_ref,
        kt_ref,
        ktm_ref,
        v_ref,
        vm_ref,
        e_ref,
        em_ref,
        att_ref,
        a2_ref,
        z_ref,
        gp_ref,
        a3_ref,
        a3m_ref,
        qw_ref,
        kwt_ref,
        kwtm_ref,
        vw_ref,
        vwm_ref,
        ew_ref,
        ewm_ref,
        watt_ref,
        stat_ref,
        last_ref,
        carry,
        bias,
        k_nat,
        km_nat,
        vt,
        vtm,
        hidden,
        row_buffer,
        row_sems,
    ) = refs[-35:]
    step = pl.program_id(0)
    rows_ref = sources.rows_of(
        refs[: len(sources.arrays)], count, lambda s: s + first, place_ref[0], row_buffer, row_sems
    )
    width = wao_ref.shape[0]
    seg = q_ref.shape[2]
    slots = init_ref.shape[0]
    ff = win_ref.shape[0]

    @pl.when(step == 0)
    def _():
        carry[...] = mem0_ref[...].astype(F32)

    docs = rows_ref[seg : seg + 1, :].astype(F32)
    flag = rows_ref[seg + 1 : seg + 2, :].astype(F32)
    stat_ref[0, 5:6, :] = flag
    mem = jnp.where(flag[:, :slots] > 0.0, init_ref[...].astype(F32).T, carry[...])
    ga, gf, gw = gain_tiles(gains_ref)

    doc_rows = jnp.broadcast_to(docs, (128, seg)).T
    for at in range(0, seg, 128):
        bias[:, at : at + 128] = jnp.where(doc_rows == docs[:, at : at + 128], 0.0, MASKED)

    tokens = rows_ref[:seg, :].astype(F32).T
    r1 = inverse_rms(tokens)
    a1_ref[...] = (tokens * r1 * wide(ga, seg)).astype(BF16)
    rm = inverse_rms(mem)
    a1m_ref[0] = (mem * rm * ga[:, :slots]).astype(BF16)
    stat_ref[0, 0:1, :] = r1
    stat_ref[0, 4:5, :slots] = rm

    a1 = a1_ref[...]
    a1m = a1m_ref[0]
    q_ref[0] = (nn(wqkv_ref[:width, :], a1) * HEAD_DIM**-0.5).astype(BF16)
    kt = nn(wqkv_ref[width : 2 * width, :], a1).astype(BF16)
    kt_ref[0] = kt
    k_nat[...] = kt.T
    vt[...] = nn(wqkv_ref[2 * width :, :], a1).astype(BF16)
    v_ref[0] = vt[...].T
    ktm = nn(wqkv_ref[width : 2 * width, :], a1m).astype(BF16)
    ktm_ref[0] = ktm
    km_nat[...] = ktm.T
    vtm[...] = nn(wqkv_ref[2 * width :, :], a1m).astype(BF16)
    vm_ref[0] = vtm[...].T

    def pair(index, unused):
        lanes = pl.ds(pl.multiple_of(index * 128, 128), 128)
        keys = k_nat[:, lanes]
        mem_keys = km_nat[:, lanes]
        for half in range(2):
            head = index * 2 + half
            rows = pl.ds(pl.multiple_of(head * HEAD_DIM, HEAD_DIM), HEAD_DIM)
            queries = q_ref[0, rows, :]
            blank = jnp.zeros_like(queries)
            queries = jnp.concatenate([queries, blank] if half == 0 else [blank, queries], axis=0)
            scores = nn(keys, queries) + bias[...]
            mem_scores = nn(mem_keys, queries)
            top = jnp.maximum(
                jnp.max(scores, axis=0, keepdims=True), jnp.max(mem_scores, axis=0, keepdims=True)
            )
            raised = jnp.exp(scores - top)
            mem_raised = jnp.exp(mem_scores - top)
            inverse = 1.0 / (
                jnp.sum(raised, axis=0, keepdims=True) + jnp.sum(mem_raised, axis=0, keepdims=True)
            )
            raised = raised.astype(BF16)
            mem_raised = mem_raised.astype(BF16)
            e_ref[0, head] = raised
            em_ref[0, rows, :] = mem_raised
            mixed = nn(vt[rows, :], raised) + nn(vtm[rows, :], mem_raised)
            att_ref[rows, :] = (mixed * inverse).astype(BF16)
            stat_ref[0, pl.ds(8 + head, 1), :] = inverse
        return unused

    lax.fori_loop(0, HEADS // 2, pair, 0, unroll=HEADS // 2)

    h1 = rows_ref[:seg, :].astype(F32).T + nn(wao_ref[...], att_ref[...])
    r2 = inverse_rms(h1)
    stat_ref[0, 1:2, :] = r2
    a2_ref[...] = (h1 * r2 * wide(gf, seg)).astype(BF16)
    hidden[...] = h1
    a2 = a2_ref[...]
    for at in range(0, ff, 512):
        upper = nn(win_ref[at : at + 512, :], a2)
        square = upper * upper
        bent = jnp.tanh(upper * (SQRT_2_PI + (SQRT_2_PI * CUBIC) * square))
        cdf = 0.5 + 0.5 * bent
        z_ref[at : at + 512, :] = (upper * cdf).astype(BF16)
        slope = (0.5 * SQRT_2_PI) + (1.5 * SQRT_2_PI * CUBIC) * square
        gp_ref[0, at : at + 512, :] = (cdf + upper * (1.0 - bent * bent) * slope).astype(BF16)
    enc = hidden[...] + tn(wout_ref[...], z_ref[...])
    enc_ref[0, :seg, :] = enc.T.astype(BF16)
    r3 = inverse_rms(enc)
    stat_ref[0, 2:3, :] = r3
    a3_ref[...] = (enc * r3 * wide(gw, seg)).astype(BF16)
    a3m_ref[0] = (mem * rm * gw[:, :slots]).astype(BF16)
    a3 = a3_ref[...]
    a3m = a3m_ref[0]

    kwt = nn(ww_ref[width : 2 * width, :], a3).astype(BF16)
    kwt_ref[0] = kwt
    kw = kwt.T
    vwt = nn(ww_ref[2 * width :, :], a3).astype(BF16)
    vw_ref[0] = vwt.T
    kwtm = nn(ww_ref[width : 2 * width, :], a3m).astype(BF16)
    kwtm_ref[0] = kwtm
    vwtm = nn(ww_ref[2 * width :, :], a3m).astype(BF16)
    vwm_ref[0] = vwtm.T
    qwt = (nn(ww_ref[:width, :], a3m) * HEAD_DIM**-0.5).astype(BF16)
    own = head_mask(width, HEADS * slots)
    qw = jnp.where(own, nn(qwt, spread_ref[...]), 0.0).astype(BF16)
    qw_ref[0] = qw
    scores = nn(kw, qw)
    mem_scores = nn(kwtm.T, qw)
    slot_row = lax.broadcasted_iota(jnp.int32, mem_scores.shape, 0)
    slot_col = lax.broadcasted_iota(jnp.int32, mem_scores.shape, 1) % slots
    mem_scores = jnp.where(slot_row == slot_col, mem_scores, MASKED)
    top = jnp.maximum(
        jnp.max(scores, axis=0, keepdims=True), jnp.max(mem_scores, axis=0, keepdims=True)
    )
    raised = jnp.exp(scores - top)
    mem_raised = jnp.exp(mem_scores - top)
    inverse = 1.0 / (
        jnp.sum(raised, axis=0, keepdims=True) + jnp.sum(mem_raised, axis=0, keepdims=True)
    )
    stat_ref[0, 3:4, :] = inverse
    raised = raised.astype(BF16)
    mem_raised = mem_raised.astype(BF16)
    ew_ref[0] = raised
    ewm_ref[0] = mem_raised
    mixed = (nn(vwt, raised) + nn(vwtm, mem_raised)) * inverse
    watt = nn(jnp.where(own, mixed, 0.0).astype(BF16), fold_ref[...]).astype(BF16)
    watt_ref[0] = watt
    new_mem = (mem + nn(wwo_ref[...], watt)).astype(BF16).astype(F32)
    carry[...] = new_mem
    enc_ref[0, seg:, :] = new_mem.T.astype(BF16)
    last_ref[...] = new_mem.astype(BF16)


def chain_kernel(
    sources,
    segs,
    place_ref,
    carry0_ref,
    weights_gains_ref,
    spread_ref,
    fold_ref,
    wwo_ref,
    ww_ref,
    wout_ref,
    win_ref,
    wao_ref,
    wqkv_ref,
    a1m_ref,
    q_ref,
    vm_ref,
    em_ref,
    att_ref,
    a2_ref,
    gp_ref,
    a3_ref,
    a3m_ref,
    qw_ref,
    kwt_ref,
    kwtm_ref,
    vw_ref,
    vwm_ref,
    ew_ref,
    ewm_ref,
    stat_ref,
    *refs,
):
    source_refs, refs = refs[: len(sources.arrays)], refs[len(sources.arrays) :]
    bm_ref, gwkv_ref, gwm_ref, bf_ref, gu_ref, ba_ref, gh_ref, do_ref, dd_ref, dsm_ref = refs[:10]
    gkvm_ref, init_ref, gains_ref, sent_ref, carry, grad_buffer, grad_sems = refs[10:]
    gout_ref = sources.rows_of(
        source_refs, segs, lambda s: segs - 1 - s, place_ref[0], grad_buffer, grad_sems
    )
    step = pl.program_id(0)
    width = wao_ref.shape[0]
    ff = wout_ref.shape[0]
    seg = q_ref.shape[2]
    slots = a1m_ref.shape[2]
    reset = stat_ref[0, 5:6, :slots] > 0.0

    @pl.when(step == 0)
    def _():
        carry[...] = carry0_ref[...].astype(F32)
        init_ref[...] = jnp.zeros_like(init_ref)
        gains_ref[...] = jnp.zeros_like(gains_ref)

    ga, gf, gw = gain_tiles(weights_gains_ref)
    gai, gfi, gwi = 1.0 / ga, 1.0 / gf, 1.0 / gw
    own = head_mask(width, HEADS * slots)
    rm = stat_ref[0, 4:5, :slots]

    grad_mem = gout_ref[seg:, :].astype(F32).T + carry[...]
    branch_mem = grad_mem.astype(BF16)
    bm_ref[0] = branch_mem
    grad_watt = nn(wwo_ref[...], branch_mem).astype(BF16)
    inverse = stat_ref[0, 3:4, :]
    scaled = (jnp.where(own, nn(grad_watt, spread_ref[...]), 0.0) * inverse).astype(BF16)
    raised = ew_ref[0].astype(F32)
    mem_raised = ewm_ref[0].astype(F32)
    grad_probs = nn(vw_ref[0], scaled)
    mem_grad_probs = nn(vwm_ref[0], scaled)
    dots = (
        jnp.sum(raised * grad_probs, axis=0, keepdims=True)
        + jnp.sum(mem_raised * mem_grad_probs, axis=0, keepdims=True)
    ) * inverse
    grad_scores = (raised * (grad_probs - dots)).astype(BF16)
    mem_grad_scores = (mem_raised * (mem_grad_probs - dots)).astype(BF16)
    gwkv_ref[:width, :] = nt(qw_ref[0], grad_scores).astype(BF16)
    gwkv_ref[width:, :] = nt(scaled, ew_ref[0]).astype(BF16)
    grad_q = (nn(kwt_ref[0], grad_scores) + nn(kwtm_ref[0], mem_grad_scores)) * HEAD_DIM**-0.5
    gwm_ref[0, :width, :] = nn(jnp.where(own, grad_q, 0.0).astype(BF16), fold_ref[...]).astype(BF16)
    gwm_ref[0, width : 2 * width, :] = nt(qw_ref[0], mem_grad_scores).astype(BF16)
    gwm_ref[0, 2 * width :, :] = nt(scaled, ewm_ref[0]).astype(BF16)

    grad_a3 = nn(ww_ref[:, width:], gwkv_ref[...])
    grad_a3m = nn(ww_ref[...], gwm_ref[0])
    part, weighed = norm_back(
        grad_a3, a3_ref[...].astype(F32), stat_ref[0, 2:3, :], wide(gw, seg), wide(gwi, seg)
    )
    mem_part, mem_weighed = norm_back(
        grad_a3m, a3m_ref[0].astype(F32), rm, gw[:, :slots], gwi[:, :slots]
    )
    gains_ref[2] += lane_sums(weighed)
    gains_ref[2, :, :slots] += mem_weighed
    grad_mem_in = grad_mem + mem_part
    gh_ref[0] = gout_ref[:seg, :].astype(F32).T + part

    bf_ref[...] = gh_ref[0].astype(BF16)
    branch = bf_ref[...]
    for at in range(0, ff, 512):
        grad_z = nn(wout_ref[at : at + 512, :], branch)
        gu_ref[at : at + 512, :] = (grad_z * gp_ref[0, at : at + 512, :].astype(F32)).astype(BF16)
    grad_a2 = nn(win_ref[...], gu_ref[...])
    part, weighed = norm_back(
        grad_a2, a2_ref[...].astype(F32), stat_ref[0, 1:2, :], wide(gf, seg), wide(gfi, seg)
    )
    gains_ref[1] += lane_sums(weighed)
    gh_ref[0] += part

    ba_ref[...] = gh_ref[0].astype(BF16)
    grad_att = nn(wao_ref[...], ba_ref[...]).astype(BF16)
    products = grad_att.astype(F32) * att_ref[...].astype(F32)
    rows = []
    dots = []
    for head in range(HEADS):
        span = slice(head * HEAD_DIM, (head + 1) * HEAD_DIM)
        inverse = stat_ref[0, 8 + head : 9 + head, :]
        dots.append(jnp.sum(products[span, :], axis=0, keepdims=True) * inverse)
        rows.append((grad_att[span, :].astype(F32) * inverse).astype(BF16))
    scaled = jnp.concatenate(rows, axis=0)
    do_ref[0] = scaled
    dd_ref[0] = jnp.concatenate(dots, axis=0)
    mem_values = jnp.concatenate([vm_ref[0].astype(F32)] * HEADS, axis=0)
    mem_values = jnp.where(own, mem_values, 0.0).astype(BF16)
    grad_probs = nn(mem_values, scaled)
    parts = []
    for head in range(HEADS):
        span = slice(head * slots, (head + 1) * slots)
        parts.append(
            (em_ref[0, span, :].astype(F32) * (grad_probs[span, :] - dots[head])).astype(BF16)
        )
    grad_scores = jnp.concatenate(parts, axis=0)
    dsm_ref[0] = grad_scores
    grad_k = jnp.where(own, nt(q_ref[0], grad_scores), 0.0).astype(BF16)
    grad_v = jnp.where(own, nt(scaled, em_ref[0]), 0.0).astype(BF16)
    gkvm_ref[0, :width, :] = nn(grad_k, fold_ref[...]).astype(BF16)
    gkvm_ref[0, width:, :] = nn(grad_v, fold_ref[...]).astype(BF16)
    grad_a1m = nn(wqkv_ref[:, width:], gkvm_ref[0])
    mem_part, mem_weighed = norm_back(
        grad_a1m, a1m_ref[0].astype(F32), rm, ga[:, :slots], gai[:, :slots]
    )
    gains_ref[0, :, :slots] += mem_weighed
    grad_mem_in = grad_mem_in + mem_part
    init_ref[...] += jnp.where(reset, grad_mem_in, 0.0)
    carry[...] = jnp.where(reset, 0.0, grad_mem_in).astype(BF16).astype(F32)
    sent_ref[...] = carry[...].astype(BF16)


def attention_kernel(
    place_ref,
    do_ref,
    dd_ref,
    dsm_ref,
    gh_ref,
    q_ref,
    kt_ref,
    ktm_ref,
    v_ref,
    e_ref,
    a1_ref,
    stat_ref,
    gains_ref,
    wqkv_ref,
    *refs,
):
    gqkv_ref, out_ref, gain_ref = refs[-3:]
    pair = pl.program_id(1)
    width = wqkv_ref.shape[0]
    seg = q_ref.shape[2]
    for half in range(2):
        head = pair * 2 + half
        base = pl.multiple_of(head * HEAD_DIM, HEAD_DIM)
        span = slice(half * HEAD_DIM, (half + 1) * HEAD_DIM)
        grads = do_ref[0, span, :]
        blank = jnp.zeros_like(grads)
        padded = jnp.concatenate([grads, blank] if half == 0 else [blank, grads], axis=0)
        dots = dd_ref[0, pl.ds(head, 1), :]
        grad_probs = nn(v_ref[0], padded)
        inner = (e_ref[0, half].astype(F32) * (grad_probs - dots)).astype(BF16)
        grad_q = nn(kt_ref[0, span, :], inner) + nn(ktm_ref[0, span, :], dsm_ref[0, span, :])
        gqkv_ref[pl.ds(base, HEAD_DIM), :] = (grad_q * HEAD_DIM**-0.5).astype(BF16)
        gqkv_ref[pl.ds(width + base, HEAD_DIM), :] = nt(q_ref[0, span, :], inner).astype(BF16)
        gqkv_ref[pl.ds(2 * width + base, HEAD_DIM), :] = nt(grads, e_ref[0, half]).astype(BF16)

    @pl.when((pl.program_id(0) == 0) & (pair == 0))
    def _():
        gain_ref[...] = jnp.zeros_like(gain_ref)

    @pl.when(pair == pl.num_programs(1) - 1)
    def _():
        grad_a1 = nn(wqkv_ref[...], gqkv_ref[...])
        (ga,) = gain_tiles(gains_ref, 1)
        part, weighed = norm_back(
            grad_a1,
            a1_ref[...].astype(F32),
            stat_ref[0, 0:1, :],
            wide(ga, seg),
            wide(1.0 / ga, seg),
        )
        gain_ref[...] += lane_sums(weighed)
        out_ref[0] = (gh_ref[0] + part).T.astype(BF16)


def whole(array):
    zeros = (0,) * array.ndim
    return pl.BlockSpec(array.shape, lambda *unused: zeros, pipeline_mode=pl.Buffered(1))


def params():
    return pltpu.CompilerParams(dimension_semantics=("arbitrary",), vmem_limit_bytes=VMEM_LIMIT)


def cost(microseconds):
    return pl.CostEstimate(
        flops=int(microseconds * 1e9), bytes_accessed=1 << 20, transcendentals=0
    )


def forward_chain(sources, place, first, count, mem0, consts, w, before=None):
    segs = consts["segs"]
    seg = consts["seg"]
    width, slots = mem0.shape
    ff = w["in_t"].shape[0]

    def flat(height):
        return (
            jax.ShapeDtypeStruct((height, segs * seg), BF16),
            pl.BlockSpec((height, seg), lambda s, f: (0, s + first)),
        )

    def stack(*shape, dtype=BF16):
        tail = (0,) * len(shape)
        return (
            jax.ShapeDtypeStruct((segs,) + shape, dtype),
            pl.BlockSpec((1,) + shape, lambda s, f: (s + first,) + tail),
        )

    outs = dict(
        enc=stack(seg + slots, width),
        a1=flat(width),
        a1m=stack(width, slots),
        q=stack(width, seg),
        kt=stack(width, seg),
        ktm=stack(width, slots),
        v=stack(seg, width),
        vm=stack(slots, width),
        e=stack(HEADS, seg, seg),
        em=stack(HEADS * slots, seg),
        att=flat(width),
        a2=flat(width),
        z=flat(ff),
        gp=stack(ff, seg),
        a3=flat(width),
        a3m=stack(width, slots),
        qw=stack(width, HEADS * slots),
        kwt=stack(width, seg),
        kwtm=stack(width, slots),
        vw=stack(seg, width),
        vwm=stack(slots, width),
        ew=stack(seg, HEADS * slots),
        ewm=stack(slots, HEADS * slots),
        watt=stack(width, slots),
        stat=stack(16, seg, dtype=F32),
        last=(
            jax.ShapeDtypeStruct((width, slots), BF16),
            pl.BlockSpec((width, slots), lambda s, f: (0, 0)),
        ),
    )
    fixed = [
        mem0,
        consts["init"],
        consts["gains"],
        consts["spread"],
        consts["fold"],
    ]
    weights = [w[name] for name in ("qkv_t", "ao_t", "in_t", "out", "write_t", "wo_t")]
    passed = [] if before is None else [before[name] for name in outs if name != "last"]
    in_count = 1 + len(fixed) + len(weights) + len(sources.arrays)
    results = pl.pallas_call(
        lambda *refs: forward_kernel(sources, first, count, *refs),
        grid_spec=pltpu.PrefetchScalarGridSpec(
            num_scalar_prefetch=1,
            grid=(count,),
            in_specs=[whole(a) for a in fixed + weights]
            + [pl.BlockSpec(memory_space=pl.ANY)] * (len(sources.arrays) + len(passed)),
            out_specs=[spec for _, spec in outs.values()],
            scratch_shapes=[
                pltpu.VMEM((width, slots), F32),
                pltpu.VMEM((seg, seg), F32),
                pltpu.VMEM((seg, width), BF16),
                pltpu.VMEM((slots, width), BF16),
                pltpu.VMEM((width, seg), BF16),
                pltpu.VMEM((width, slots), BF16),
                pltpu.VMEM((width, seg), F32),
                pltpu.VMEM((2, seg + 16, width), BF16),
                pltpu.SemaphoreType.DMA((2,)),
            ],
        ),
        out_shape=[shape for shape, _ in outs.values()],
        input_output_aliases={in_count + at: at for at in range(len(passed))},
        compiler_params=params(),
        cost_estimate=cost(18 * count),
        name="forward_chain",
    )(place, *fixed, *weights, *sources.arrays, *passed)
    return dict(zip(outs, results))


def backward_chain(kept, sources, place, carry0, consts, w):
    segs = consts["segs"]
    width, slots = kept["a1m"].shape[1:]
    seg = kept["q"].shape[2]
    ff = kept["gp"].shape[1]
    last = segs - 1

    def flat(height):
        return (
            jax.ShapeDtypeStruct((height, segs * seg), BF16),
            pl.BlockSpec((height, seg), lambda s, f: (0, last - s)),
        )

    def stack(*shape, dtype=BF16):
        tail = (0,) * len(shape)
        return (
            jax.ShapeDtypeStruct((segs,) + shape, dtype),
            pl.BlockSpec((1,) + shape, lambda s, f: (last - s,) + tail),
        )

    def single(*shape, dtype=F32):
        tail = (0,) * len(shape)
        return (jax.ShapeDtypeStruct(shape, dtype), pl.BlockSpec(shape, lambda s, f: tail))

    outs = dict(
        bm=stack(width, slots),
        gwkv=flat(2 * width),
        gwm=stack(3 * width, slots),
        bf=flat(width),
        gu=flat(ff),
        ba=flat(width),
        gh=stack(width, seg, dtype=F32),
        do=stack(width, seg),
        dd=stack(HEADS, seg, dtype=F32),
        dsm=stack(HEADS * slots, seg),
        gkvm=stack(2 * width, slots),
        init=single(width, slots),
        gains=single(3, width, 128),
        sent=single(width, slots, dtype=BF16),
    )
    fixed = [
        carry0,
        consts["gains"],
        consts["spread"],
        consts["fold"],
    ]
    weights = [w[name] for name in ("wo", "write", "out", "in", "ao", "qkv")]
    blocked = ["a1m", "q", "vm", "em", "att", "a2", "gp", "a3", "a3m", "qw"]
    blocked += ["kwt", "kwtm", "vw", "vwm", "ew", "ewm", "stat"]

    def spec_of(array):
        if array.ndim == 2:
            return pl.BlockSpec((array.shape[0], seg), lambda s, f: (0, last - s))
        tail = (0,) * (array.ndim - 1)
        return pl.BlockSpec((1,) + array.shape[1:], lambda s, f: (last - s,) + tail)

    results = pl.pallas_call(
        lambda *refs: chain_kernel(sources, segs, *refs),
        grid_spec=pltpu.PrefetchScalarGridSpec(
            num_scalar_prefetch=1,
            grid=(segs,),
            in_specs=[whole(a) for a in fixed + weights]
            + [spec_of(kept[name]) for name in blocked]
            + [pl.BlockSpec(memory_space=pl.ANY)] * len(sources.arrays),
            out_specs=[spec for _, spec in outs.values()],
            scratch_shapes=[
                pltpu.VMEM((width, slots), F32),
                pltpu.VMEM((2, seg + slots, width), BF16),
                pltpu.SemaphoreType.DMA((2,)),
            ],
        ),
        out_shape=[shape for shape, _ in outs.values()],
        compiler_params=params(),
        cost_estimate=cost(11 * segs),
        name="backward_chain",
    )(place, *fixed, *weights, *[kept[name] for name in blocked], *sources.arrays)
    return dict(zip(outs, results))


def attention_back(kept, grads, which, consts, w, before):
    segs, width, seg = kept["q"].shape
    count = which.shape[0]
    pair = 2 * HEAD_DIM

    def by_pair(rows, lanes):
        return pl.BlockSpec((1, rows, lanes), lambda s, h, f: (f[s], h, 0))

    def by_seg(array):
        tail = (0,) * (array.ndim - 1)
        return pl.BlockSpec((1,) + array.shape[1:], lambda s, h, f: (f[s],) + tail)

    inputs = [
        (grads["do"], by_pair(pair, seg)),
        (grads["dd"], by_seg(grads["dd"])),
        (grads["dsm"], by_pair(pair, seg)),
        (grads["gh"], by_seg(grads["gh"])),
        (kept["q"], by_pair(pair, seg)),
        (kept["kt"], by_pair(pair, seg)),
        (kept["ktm"], by_pair(pair, kept["ktm"].shape[2])),
        (kept["v"], pl.BlockSpec((1, seg, pair), lambda s, h, f: (f[s], 0, h))),
        (kept["e"], pl.BlockSpec((1, 2, seg, seg), lambda s, h, f: (f[s], h, 0, 0))),
        (kept["a1"], pl.BlockSpec((width, seg), lambda s, h, f: (0, f[s]))),
        (kept["stat"], by_seg(kept["stat"])),
        (consts["gains"], whole(consts["gains"])),
        (w["qkv"], whole(w["qkv"])),
    ]
    passed = [] if before is None else [before]
    return pl.pallas_call(
        attention_kernel,
        grid_spec=pltpu.PrefetchScalarGridSpec(
            num_scalar_prefetch=1,
            grid=(count, HEADS // 2),
            in_specs=[spec for _, spec in inputs]
            + [pl.BlockSpec(memory_space=pl.ANY)] * len(passed),
            out_specs=[
                pl.BlockSpec((3 * width, seg), lambda s, h, f: (0, f[s])),
                pl.BlockSpec((1, seg, width), lambda s, h, f: (s, 0, 0)),
                pl.BlockSpec((width, 128), lambda s, h, f: (0, 0)),
            ],
        ),
        out_shape=[
            jax.ShapeDtypeStruct((3 * width, segs * seg), BF16),
            jax.ShapeDtypeStruct((count, seg, width), BF16),
            jax.ShapeDtypeStruct((width, 128), F32),
        ],
        input_output_aliases={1 + len(inputs): 0} if passed else {},
        compiler_params=pltpu.CompilerParams(
            dimension_semantics=("arbitrary", "arbitrary"), vmem_limit_bytes=VMEM_LIMIT
        ),
        cost_estimate=cost(10 * count),
        name="attention_back",
    )(which, *[array for array, _ in inputs], *passed)


def swap_pairs(value, axis, mask):
    size = lax.axis_size(axis)
    return lax.ppermute(value, axis, [(i, i ^ mask) for i in range(size)])


def sum_phases():
    section = [("section", 1 << at) for at in range(lax.axis_size("section").bit_length() - 1)]
    dp = [("dp", 1 << at) for at in range(lax.axis_size("dp").bit_length() - 1)]
    phases = [(step, step) for step in section[:1]]
    crossed = []
    if len(section) > 1 and dp:
        crossed = [(dp[0], section[1]), (section[1], dp[0])]
        section, dp = section[2:], dp[1:]
    else:
        section = section[1:]
    straight = [(step, step) for step in dp + section]
    return phases + crossed + straight


def phase_swap(value, phase):
    sections, dps = lax.axis_size("section"), lax.axis_size("dp")
    route = []
    for section in range(sections):
        axis, mask = phase[section % 2]
        for dp in range(dps):
            to = ((section ^ mask) * dps + dp) if axis == "section" else (section * dps + (dp ^ mask))
            route.append((section * dps + dp, to))
    return lax.ppermute(value, ("section", "dp"), route)


def phase_bit(phase):
    bits = [(lax.axis_index(axis) // mask) % 2 for axis, mask in phase]
    return jnp.where(lax.axis_index("section") % 2 == 0, bits[0], bits[1])


def half_of(value, side):
    half = value.shape[0] // 2
    return lax.dynamic_slice_in_dim(value, side * half, half, 0)


def fetch(source, target, sem):
    copy = pltpu.make_async_copy(source, target, sem)
    copy.start()
    return copy


def slot_sum(left, right):
    join = lambda ref: jnp.concatenate([ref[at] for at in range(ref.shape[0])], axis=1)
    return nt(join(left), join(right))


def early_weights_kernel(
    side_ref, a2_ref, gu_ref, bf_ref, z_ref, a3_ref, gwkv_ref, a3m_ref, gwm_ref, watt_ref, bm_ref, *refs
):
    out_ref, a2, gu, z, bf, a3, gw, a3m, gwm, left, right, staged, in_sems, out_sems = refs
    side = side_ref[0]
    width = a2.shape[0]
    folds = gu.shape[0]
    base = side * (folds * width)
    loads = []

    def load(source, target):
        loads.append(fetch(source, target, in_sems.at[len(loads)]))

    def wait(count):
        for _ in range(count):
            loads[wait.done].wait()
            wait.done += 1

    wait.done = 0
    load(a2_ref, a2)
    for at in range(folds):
        rows = pl.ds(pl.multiple_of(base + at * width, width), width)
        load(gu_ref.at[rows, :], gu.at[at])
    load(bf_ref, bf)
    for at in range(folds):
        rows = pl.ds(pl.multiple_of(base + at * width, width), width)
        load(z_ref.at[rows, :], z.at[at])
    load(a3_ref, a3)
    load(gwkv_ref.at[pl.ds(pl.multiple_of(side * width, width), width), :], gw)
    load(a3m_ref, a3m)
    load(gwm_ref.at[:, pl.ds(pl.multiple_of((1 + side) * width, width), width), :], gwm)
    last = in_sems.at[len(loads)]

    @pl.when(side == 0)
    def _():
        pltpu.make_async_copy(a3m_ref, left, last).start()
        pltpu.make_async_copy(gwm_ref.at[:, pl.ds(0, width), :], right, last).start()

    @pl.when(side == 1)
    def _():
        pltpu.make_async_copy(watt_ref, left, last).start()
        pltpu.make_async_copy(bm_ref, right, last).start()

    stores = []

    def put(tile, value):
        columns = slice(tile * width, (tile + 1) * width)
        staged[:, columns] = value.astype(BF16)
        stores.append(fetch(staged.at[:, columns], out_ref.at[:, columns], out_sems.at[tile]))

    wait(1)
    for at in range(folds):
        wait(1)
        put(at, nt(a2[...], gu[at]))
    wait(1)
    for at in range(folds):
        wait(1)
        put(folds + at, nt(z[at], bf[...]))
    wait(4)
    put(2 * folds, nt(a3[...], gw[...]) + slot_sum(a3m, gwm))
    pltpu.make_async_copy(watt_ref, left, last).wait()
    pltpu.make_async_copy(bm_ref, right, last).wait()
    put(2 * folds + 1, slot_sum(left, right))
    for store in stores:
        store.wait()


def early_weights(kept, grads, side):
    width, tokens = kept["a2"].shape
    folds = kept["z"].shape[0] // 2 // width
    inputs = [kept["a2"], grads["gu"], grads["bf"], kept["z"], kept["a3"], grads["gwkv"]]
    inputs += [kept["a3m"], grads["gwm"], kept["watt"], grads["bm"]]
    anywhere = pl.BlockSpec(memory_space=pl.ANY)
    full = pltpu.VMEM((width, tokens), BF16)
    several = pltpu.VMEM((folds, width, tokens), BF16)
    slots = pltpu.VMEM(kept["a3m"].shape, BF16)
    out = jax.ShapeDtypeStruct((width, (2 * folds + 2) * width), BF16)
    return pl.pallas_call(
        early_weights_kernel,
        grid_spec=pltpu.PrefetchScalarGridSpec(
            num_scalar_prefetch=1,
            grid=(1,),
            in_specs=[anywhere] * len(inputs),
            out_specs=anywhere,
            scratch_shapes=[full, several, several, full, full, full]
            + [slots] * 4
            + [
                pltpu.VMEM(out.shape, BF16),
                pltpu.SemaphoreType.DMA((7 + 2 * folds,)),
                pltpu.SemaphoreType.DMA((2 * folds + 2,)),
            ],
        ),
        out_shape=out,
        compiler_params=params(),
        cost_estimate=cost(9),
        name="early_weights",
    )(side, *inputs)


def late_weights_kernel(count, side_ref, a1_ref, gqkv_ref, att_ref, ba_ref, a1m_ref, gkvm_ref, *refs):
    init_ref, gains_ref, refs = refs[0], refs[1], refs[2:]
    part_refs, refs = refs[:count], refs[count:]
    out_ref, a1, main, left, right, a1m, gkvm, init, gains, parts, staged, in_sems, out_sems = refs
    side = side_ref[0]
    width = a1.shape[0]
    slots = init.shape[1]
    rows = pl.ds(pl.multiple_of((1 + side) * width, width), width)
    kv_rows = pl.ds(pl.multiple_of(side * width, width), width)
    loads = [
        fetch(a1_ref, a1, in_sems.at[0]),
        fetch(gqkv_ref.at[rows, :], main, in_sems.at[1]),
        fetch(a1m_ref, a1m, in_sems.at[2]),
        fetch(gkvm_ref.at[:, kv_rows, :], gkvm, in_sems.at[3]),
    ]

    @pl.when(side == 0)
    def _():
        pltpu.make_async_copy(a1_ref, left, in_sems.at[4]).start()
        pltpu.make_async_copy(gqkv_ref.at[pl.ds(0, width), :], right, in_sems.at[5]).start()

    @pl.when(side == 1)
    def _():
        pltpu.make_async_copy(att_ref, left, in_sems.at[4]).start()
        pltpu.make_async_copy(ba_ref, right, in_sems.at[5]).start()

    others = [fetch(init_ref, init, in_sems.at[6]), fetch(gains_ref, gains, in_sems.at[7])]
    others += [fetch(ref, parts.at[at], in_sems.at[8 + at]) for at, ref in enumerate(part_refs)]
    stores = []

    def put(columns, value):
        staged[:, columns] = value.astype(BF16)
        stores.append(fetch(staged.at[:, columns], out_ref.at[:, columns], out_sems.at[len(stores)]))

    for load in loads:
        load.wait()
    put(slice(0, width), nt(a1[...], main[...]) + slot_sum(a1m, gkvm))
    pltpu.make_async_copy(att_ref, left, in_sems.at[4]).wait()
    pltpu.make_async_copy(ba_ref, right, in_sems.at[5]).wait()
    put(slice(width, 2 * width), nt(left[...], right[...]))
    for load in others:
        load.wait()
    columns = [gains[0], gains[1], gains[2]]
    for at in range(count):
        columns[0] = columns[0] + parts[at]
    lane = lax.broadcasted_iota(jnp.int32, init.shape, 1)
    extras = jnp.zeros(init.shape, F32)
    for at, column in enumerate(columns):
        extras = jnp.where(lane == at, jnp.sum(column, axis=1, keepdims=True), extras)
    extras = jnp.where(side == 0, init[...], extras)
    extras = jnp.concatenate([extras, jnp.zeros_like(extras)], axis=1)
    put(slice(2 * width, 2 * width + 2 * slots), extras)
    for store in stores:
        store.wait()


def late_weights(kept, grads, gqkv, gain_parts, side):
    width, tokens = kept["a1"].shape
    count = len(gain_parts)
    inputs = [kept["a1"], gqkv, kept["att"], grads["ba"], kept["a1m"], grads["gkvm"]]
    inputs += [grads["init"], grads["gains"]] + list(gain_parts)
    slots = grads["init"].shape[1]
    anywhere = pl.BlockSpec(memory_space=pl.ANY)
    full = pltpu.VMEM((width, tokens), BF16)
    small = pltpu.VMEM(kept["a1m"].shape, BF16)
    out = jax.ShapeDtypeStruct((width, 2 * width + 2 * slots), BF16)
    return pl.pallas_call(
        lambda *refs: late_weights_kernel(count, *refs),
        grid_spec=pltpu.PrefetchScalarGridSpec(
            num_scalar_prefetch=1,
            grid=(1,),
            in_specs=[anywhere] * len(inputs),
            out_specs=anywhere,
            scratch_shapes=[full] * 4
            + [small] * 2
            + [
                pltpu.VMEM(grads["init"].shape, F32),
                pltpu.VMEM(grads["gains"].shape, F32),
                pltpu.VMEM((count,) + gain_parts[0].shape, F32),
                pltpu.VMEM(out.shape, BF16),
                pltpu.SemaphoreType.DMA((8 + count,)),
                pltpu.SemaphoreType.DMA((3,)),
            ],
        ),
        out_shape=out,
        compiler_params=params(),
        cost_estimate=cost(4),
        name="late_weights",
    )(side, *inputs)


class Sum:
    def __init__(self, value, share, halve_all=False):
        self.phases = sum_phases()
        inner = self.phases[1:]
        self.value = value
        self.share = share
        halvings = 0
        most = len(inner) - (0 if halve_all else 1)
        while halvings < most and value.shape[0] >> (halvings + 1) >= 16:
            halvings += 1
        self.halved = inner[:halvings]
        self.steps = [("halve", phase) for phase in self.halved]
        self.steps += [("add", phase) for phase in inner[halvings:]]
        self.steps += [("double", phase) for phase in reversed(self.halved)]
        self.steps += [("last", self.phases[0])]
        self.started = None

    def prepare(self):
        kind, phase = self.steps.pop(0)
        if kind == "halve":
            bit = phase_bit(phase)
            value = self.value
            self.sent, self.value = half_of(value, 1 - bit), half_of(value, bit)
            if self.share is not None:
                self.sent = self.sent + half_of(self.share, 1 - bit)
                self.value = self.value + half_of(self.share, bit)
        else:
            if self.share is not None:
                self.value = self.value + self.share
            self.sent = self.value
        self.share = None
        self.ready = (kind, phase)

    def launch(self):
        kind, phase = self.ready
        if kind == "last" and isinstance(self.sent, tuple):
            self.started = (kind, tuple(phase_swap(piece, phase) for piece in self.sent))
        else:
            self.started = (kind, phase_swap(self.sent, phase))

    def finish(self, *after):
        kind, other = self.started
        self.started = None
        other, after = lax.optimization_barrier((other, after))
        if kind in ("halve", "add"):
            self.value = self.value + other
        elif kind == "double" and len(self.steps) == 1:
            self.value = (self.value, other)
        elif kind == "double":
            self.value = jnp.concatenate([self.value, other], axis=0)
        elif isinstance(other, tuple):
            self.value = (self.value, other)
        else:
            self.value = ((self.value,), (other,))
        return list(after)

    def places(self):
        own = sum(phase_bit(phase) << at for at, phase in enumerate(reversed(self.halved)))
        swapped = [(late, early) for early, late in self.halved]
        other = sum(phase_bit(phase) << at for at, phase in enumerate(reversed(swapped)))
        numbers = jnp.stack([phase_bit(self.phases[0]), jnp.int32(own), jnp.int32(other)])
        return numbers.astype(jnp.int32), 1 << len(self.halved)


def advance(totals, *after, extra=()):
    going = []
    for total in totals:
        if total.started is not None:
            total.finish(*after)
        if total.steps:
            total.prepare()
            going.append(total)
    joined, extra = lax.optimization_barrier(([total.sent for total in going], list(extra)))
    for total, sent in zip(going, joined):
        if total.value is total.sent:
            total.value = sent
        total.sent = sent
        total.launch()
    return joined, extra


def unpack_kernel(count, parts, regions, kept, place_ref, *refs):
    own_refs, other_refs, refs = refs[:parts], refs[parts : 2 * parts], refs[2 * parts :]
    gains_ref = None
    if kept:
        gains_ref, refs = refs[0], refs[1:]
    outs = len(refs) // 2
    out_refs, staged, sems = refs[:outs], refs[outs : 2 * outs], refs[2 * outs]
    each = count // parts
    rows = own_refs[0].shape[0] // each
    height = rows * count

    def take(refs, side, number, sem):
        copies = []
        for start, stop, at, top, left in regions[side]:
            for block in range(count):
                target = pl.multiple_of(top + (block ^ place_ref[number]) * rows, rows)
                inner = (block % each) * rows
                value = refs[block // each][inner : inner + rows, start:stop].astype(F32)
                staged[at][pl.ds(target, rows), left : left + stop - start] = value
            if at >= outs - kept:
                continue
            slab = (pl.ds(top, height), pl.ds(left, stop - start))
            copies.append((staged[at].at[slab], out_refs[at].at[slab], sems.at[sem + len(copies)]))
            pltpu.make_async_copy(*copies[-1]).start()
        return copies

    for side in range(2):

        @pl.when(place_ref[0] == side)
        def _():
            copies = take(own_refs, side, 1, 0)
            copies += take(other_refs, 1 - side, 2, len(copies))
            for copy in copies:
                pltpu.make_async_copy(*copy).wait()

    if kept:
        init_ref, total_ref = out_refs[outs - 2 :]
        init_ref[...] = staged[outs - 2][...].T[: init_ref.shape[0], :]
        total_ref[...] = staged[outs - 1][...].T[: total_ref.shape[0], :] / gains_ref[...]


def unpacked(total, regions, shapes, slots=0, gains=None):
    own, other = total.value
    places, count = total.places()
    parts = len(own)
    kept = 0 if gains is None else 2
    vmem = pl.BlockSpec(memory_space=pltpu.VMEM)
    outs = [jax.ShapeDtypeStruct(shape, F32) for shape in shapes[: len(shapes) - kept]]
    specs = [pl.BlockSpec(memory_space=pl.ANY)] * len(outs)
    inputs = [*own, *other]
    if kept:
        inputs.append(gains)
        outs += [jax.ShapeDtypeStruct((rows, shapes[-1][0]), F32) for rows in (slots, gains.shape[0])]
        specs += [vmem] * 2
    return pl.pallas_call(
        lambda *refs: unpack_kernel(count, parts, regions, kept, *refs),
        in_specs=[pl.BlockSpec(memory_space=pltpu.SMEM)] + [vmem] * len(inputs),
        out_specs=specs,
        out_shape=outs,
        scratch_shapes=[pltpu.VMEM(shape, F32) for shape in shapes]
        + [pltpu.SemaphoreType.DMA((len(regions[0]) + len(regions[1]),))],
        compiler_params=pltpu.CompilerParams(vmem_limit_bytes=VMEM_LIMIT),
        cost_estimate=cost(4),
        name="unpack",
    )(places, *inputs)


def pieces_in(value, place):
    parts = [lax.dynamic_index_in_dim(value, place, 0, keepdims=True)]
    sent = []
    for mask in range(1, lax.axis_size("section")):
        sent.append(lax.dynamic_index_in_dim(value, place ^ mask, 0, keepdims=True))
        parts.append(swap_pairs(sent[-1], "section", mask))
    return in_rank_order(jnp.concatenate(parts, axis=0), place), sent, parts[1:]


def in_rank_order(pieces, place):
    count = pieces.shape[0]
    return jnp.stack(
        [lax.dynamic_index_in_dim(pieces, at ^ place, 0, keepdims=False) for at in range(count)]
    )


def rank_sources(arrays, place, after):
    sections = lax.axis_size("section")
    payload = []
    for mask in range(1, sections):
        picked = [lax.dynamic_index_in_dim(a, place ^ mask, 0, keepdims=True) for a in arrays]
        payload.append(jnp.concatenate(picked, axis=1))
    payload[1:] = lax.optimization_barrier(tuple(payload[1:]))
    payload[0] = tied(payload[0], *payload[1:])
    early, late = [], []
    for mask in range(1, sections):
        route = [(i, i ^ mask) for i in range(sections if mask == 1 else 1)]
        early.append(lax.ppermute(payload[mask - 1], "section", route))
    for mask in range(2, sections):
        route = [(i, i ^ mask) for i in range(1, sections)]
        late.append(lax.ppermute(tied(payload[mask - 1], *after), "section", route))
    own = len(arrays)

    def choose(at, here):
        mask = at ^ here
        yield mask == 0, [(number, here) for number in range(own)]
        for other in range(1, sections):
            yield (mask == other) & ((at == 0) | (other == 1)), [(own + other - 1, 0)]

    def choose_late(at, here):
        yield from choose(at, here)
        for other in range(2, sections):
            yield (at != 0) & ((at ^ here) == other), [(own + sections - 1 + other - 2, 0)]

    return Sources(list(arrays) + early, choose), Sources(list(arrays) + early + late, choose_late)


def sources_in(arrays, place):
    sections = lax.axis_size("section")
    sent, pieces = [], []
    for mask in range(1, sections):
        picked = [lax.dynamic_index_in_dim(a, place ^ mask, 0, keepdims=True) for a in arrays]
        sent.append(jnp.concatenate(picked, axis=1))
        pieces.append(swap_pairs(sent[-1], "section", mask))
    own = len(arrays)

    def choose(at, here):
        yield (at ^ here) == 0, [(number, here) for number in range(own)]
        for other in range(1, sections):
            yield (at ^ here) == other, [(own + other - 1, 0)]

    return Sources(list(arrays) + pieces, choose), sent


def gathered_sources(arrays, chunks):
    rows = gathered_in(jnp.concatenate(arrays, axis=1), chunks)
    return Sources([rows], lambda at, here: [(at >= 0, [(0, at)])])


def gathered_in(value, chunks):
    place = lax.axis_index("section")
    gathered = lax.all_gather(value, "section")
    own = lax.dynamic_index_in_dim(gathered, place // chunks, 1, keepdims=False)
    count = gathered.shape[0] // chunks
    return lax.dynamic_slice_in_dim(own, (place % chunks) * count, count, 0)


def gathered_out(value, chunks):
    place = lax.axis_index("section")
    gathered = lax.all_gather(value, "section")
    sections = gathered.shape[0]
    by_stream = gathered.reshape((sections // chunks, chunks * value.shape[0]) + value.shape[1:])
    return lax.dynamic_index_in_dim(by_stream, place, 1, keepdims=False)


def tied(value, *others):
    return lax.optimization_barrier((value,) + others)[0]


def body(
    tokens,
    doc_ids,
    reset_flags,
    attn_gain,
    w_qkv,
    w_attn_out,
    ffn_gain,
    w_in,
    w_out,
    write_gain,
    w_write,
    w_write_out,
    init_memory,
    out_grad,
    memory_grad,
):
    streams, _, seg, width = tokens.shape
    slots = init_memory.shape[0]
    sections = lax.axis_size("section")
    chunks = sections // streams
    segs = sections // chunks
    place = lax.axis_index("section")

    spread = np.tile(np.eye(slots, dtype=np.float32), (1, HEADS))
    consts = dict(
        segs=segs,
        seg=seg,
        init=init_memory,
        gains=jnp.stack([attn_gain, ffn_gain, write_gain]).astype(F32),
        spread=jnp.asarray(spread, BF16),
        fold=jnp.asarray(spread.T, BF16),
    )
    w = dict(
        qkv=w_qkv,
        ao=w_attn_out,
        out=w_out,
        write=w_write,
        wo=w_write_out,
        qkv_t=w_qkv.T,
        ao_t=w_attn_out.T,
        in_t=w_in.T,
        write_t=w_write.T,
        wo_t=w_write_out.T,
    )
    w["in"] = w_in

    marks = jnp.concatenate(
        [doc_ids[:, 0], jnp.broadcast_to(reset_flags, (streams, seg))], axis=1
    ).reshape(streams, 2, seg)
    marks = jnp.pad(marks, ((0, 0), (0, 14), (0, 0))).astype(BF16)
    parts_in = [tokens[:, 0], marks]
    grads_in = [out_grad[:, 0], memory_grad[:, 0]]
    empty = jnp.zeros((width, slots), BF16)
    if chunks == 1:
        after = [w[name] for name in ("qkv_t", "in_t", "write_t")]
        first, rows = rank_sources(parts_in, place, after)
        xor = place
    else:
        first = rows = gathered_sources(parts_in, chunks)
        xor = 0
    xor = jnp.full((1,), xor, jnp.int32)

    arriving = empty
    for turn in range(chunks):
        start = forward_chain(first, xor, 0, 1, arriving, consts, w)
        if turn == 0 and chunks == 1:
            gout, sent = sources_in([tied(value, start["last"]) for value in grads_in], place)
            then = tied(xor, *sent)
        elif turn == 0:
            gout = gathered_sources(grads_in, chunks)
            then = xor
        kept = forward_chain(rows, then, 1, segs - 1, start["last"], consts, w, start)
        if turn < chunks - 1:
            arriving = lax.ppermute(
                kept["last"], "section", [(i, i + 1) for i in range(sections - 1)]
            )
    if chunks == 1:
        done, sent, pieces = pieces_in(kept["enc"], place)
        then = tied(xor, *sent)
    else:
        done = gathered_out(kept["enc"], chunks)
        pieces = []
        then = xor

    returning = empty
    for turn in range(chunks):
        grads = backward_chain(kept, gout, then, returning, consts, w)
        if turn < chunks - 1:
            returning = lax.ppermute(
                grads["sent"], "section", [(i + 1, i) for i in range(sections - 1)]
            )

    ff = w_in.shape[1]
    folds = ff // width
    cores = sum_phases()[0]
    side = phase_bit(cores).reshape(1)
    grads = dict(grads, gu=tied(grads['gu'], *pieces))
    sent = early_weights(kept, grads, 1 - side)
    share = phase_swap(sent, cores)
    early = Sum(early_weights(kept, grads, tied(side, sent)), share, halve_all=True)
    after, _ = advance([early])
    turns = [[0], [2], [3], [1]] if segs == 4 else [[at] for at in range(segs)]
    gqkv = None
    gain_parts = []
    outgoing, incoming = {}, {}
    leaving, arriving = [], []
    for turn in turns:
        which = tied(jnp.concatenate([xor ^ at for at in turn]), *after, *arriving)
        gqkv, out, part = attention_back(kept, grads, which, consts, w, gqkv)
        gain_parts.append(part)
        after, (out,) = advance([early], part, extra=[out])
        arriving, leaving = leaving, []
        for number, at in enumerate(turn):
            outgoing[at] = out[number : number + 1]
            if chunks == 1 and at:
                incoming[at] = swap_pairs(outgoing[at], "section", at)
                leaving.append(incoming[at])

    sent = late_weights(kept, grads, gqkv, gain_parts, tied(1 - side, *after, *arriving))
    after, (sent,) = advance([early], sent, extra=[sent])
    share = phase_swap(sent, cores)
    mine = tied(side, sent, *after, *leaving)
    late = Sum(late_weights(kept, grads, gqkv, gain_parts, mine), share)

    half = ff // 2

    def paired(number, start, at):
        main = (start, start + width, at, 0, (1 + number) * width)
        other = (start + width, start + 2 * width, at + number, 0, 0)
        return [main, other]

    early_regions = [
        [(0, half, 0, 0, number * half)]
        + [
            (half + at * width, half + (at + 1) * width, 1, number * half + at * width, 0)
            for at in range(half // width)
        ]
        + paired(number, ff, 2)
        for number in range(2)
    ]
    late_regions = [
        paired(number, 0, 0) + [(2 * width, 2 * width + 128, 2 + number, 0, 0)]
        for number in range(2)
    ]
    square, triple = (width, width), (width, 3 * width)
    early_shapes = [(width, ff), (ff, width), triple, square]
    advance([late])
    advance([early], late.sent)
    if chunks == 1:
        incoming[0] = tied(outgoing[0], late.sent)
        back = in_rank_order(jnp.concatenate([incoming[at] for at in range(segs)]), place)
    else:
        back = gathered_out(jnp.concatenate([outgoing[at] for at in range(segs)]), chunks)
    (token_grads,) = late.finish(back.astype(F32))
    advance([late])
    (done,) = late.finish(done)
    advance([late])
    advance([early], late.sent)
    advance([late])
    advance([late])
    advance([late])
    while early.steps:
        advance([early], late.sent)
    if late.steps:
        advance([late])
    early.finish(late.sent)
    early_grads = unpacked(early, early_regions, early_shapes)
    early_grads = late.finish(*early_grads)
    while late.steps:
        advance([late])
    if late.started is not None:
        late.finish()
    grad_in, grad_out, grad_write, grad_wo = early_grads
    grad_qkv, grad_ao, grad_init, gains = unpacked(
        late, late_regions, [triple, square, (width, 128), (width, 128)], slots, consts["gains"]
    )
    return (
        done[:, None, :seg],
        done[:, None, seg:],
        token_grads[:, None],
        gains[0],
        grad_qkv,
        grad_ao,
        gains[1],
        grad_in,
        grad_out,
        gains[2],
        grad_write,
        grad_wo,
        grad_init,
    )


def solution(mesh):
    local = P("dp", "section")
    return jax.shard_map(
        body,
        mesh=mesh,
        in_specs=(local,) * 3 + (P(),) * 10 + (local,) * 2,
        out_specs=(local,) * 3 + (P(),) * 10,
        check_vma=False,
    )
```

```python
import jax
import jax.numpy as jnp
import numpy as np
from jax import lax
from jax.experimental import pallas as pl
from jax.experimental.pallas import tpu as pltpu
from jax.sharding import PartitionSpec as P

HEADS = 8
HEAD_DIM = 64
HEADS_A_STEP = 8
EPS = 1e-06
MASKED = -1000000000.0
F32 = jnp.float32
BF16 = jnp.bfloat16
SQRT_2_PI = 0.7978845608028654
CUBIC = 0.044715
VMEM_LIMIT = 60 * 1024 * 1024


def nn(left, right):
    return lax.dot_general(left, right, (((1,), (0,)), ((), ())), preferred_element_type=F32)


def tn(left, right):
    return lax.dot_general(left, right, (((0,), (0,)), ((), ())), preferred_element_type=F32)


def nt(left, right):
    return lax.dot_general(left, right, (((1,), (1,)), ((), ())), preferred_element_type=F32)


def wide(column_tile, width):
    copies = max(1, width // 128)
    if width < 128:
        return column_tile[:, :width]
    return jnp.concatenate([column_tile] * copies, axis=1)


def inverse_rms(values):
    return lax.rsqrt(jnp.mean(values * values, axis=0, keepdims=True) + EPS)


def lane_sums(values):
    total = values[:, :128]
    for at in range(128, values.shape[1], 128):
        total = total + values[:, at : at + 128]
    return total


def head_mask(rows, columns):
    row_head = lax.broadcasted_iota(jnp.int32, (rows, columns), 0) // HEAD_DIM
    column_head = lax.broadcasted_iota(jnp.int32, (rows, columns), 1) // HEAD_DIM
    return row_head == column_head


def norm_back(grad_normed, normed, scale, gain, gain_inverse):
    weighed = grad_normed * normed
    mean = jnp.mean(weighed, axis=0, keepdims=True)
    return scale * (grad_normed * gain - normed * gain_inverse * mean), weighed


def gain_tiles(gains_ref, count=3):
    tiles = []
    for at in range(count):
        row = gains_ref[at : at + 1, :]
        tiles.append(jnp.broadcast_to(row, (128, row.shape[1])).T)
    return tiles


class Sources:
    def __init__(self, arrays, choices):
        self.arrays = arrays
        self.choices = choices

    def start(self, refs, at, place, buffer, sem):
        for condition, parts in self.choices(at, place):

            @pl.when(condition)
            def _():
                top = 0
                for number, index in parts:
                    source = refs[number].at[index]
                    target = buffer.at[pl.ds(top, source.shape[0]), :]
                    pltpu.make_async_copy(source, target, sem).start()
                    top += source.shape[0]

    def wait(self, buffer, sem):
        pltpu.make_async_copy(buffer, buffer, sem).wait()

    def rows_of(self, refs, steps, segment, place, buffer, sems):
        step = pl.program_id(0)
        slot = lax.rem(step, 2)

        @pl.when(step == 0)
        def _():
            self.start(refs, segment(0), place, buffer.at[0], sems.at[0])

        if steps > 1:

            @pl.when(step + 1 < steps)
            def _():
                self.start(refs, segment(step + 1), place, buffer.at[1 - slot], sems.at[1 - slot])

        self.wait(buffer.at[slot], sems.at[slot])
        return buffer.at[slot]


def forward_kernel(
    sources,
    segs,
    place_ref,
    mem0_ref,
    init_ref,
    gains_ref,
    spread_ref,
    fold_ref,
    *refs,
):
    wqkv_ref, wao_ref, win_ref, wout_ref, ww_ref, wwo_ref = refs[:6]
    refs = refs[6:]
    (
        enc_ref,
        a1_ref,
        a1m_ref,
        q_ref,
        kt_ref,
        ktm_ref,
        v_ref,
        vm_ref,
        e_ref,
        em_ref,
        att_ref,
        a2_ref,
        z_ref,
        gp_ref,
        a3_ref,
        a3m_ref,
        qw_ref,
        kwt_ref,
        kwtm_ref,
        vw_ref,
        vwm_ref,
        ew_ref,
        ewm_ref,
        watt_ref,
        stat_ref,
        last_ref,
        carry,
        bias,
        k_nat,
        km_nat,
        vt,
        vtm,
        hidden,
        row_buffer,
        row_sems,
    ) = refs[-35:]
    step = pl.program_id(0)
    rows_ref = sources.rows_of(
        refs[: len(sources.arrays)], segs, lambda s: s, place_ref[0], row_buffer, row_sems
    )
    width = wao_ref.shape[0]
    seg = q_ref.shape[2]
    slots = init_ref.shape[0]
    ff = win_ref.shape[0]

    @pl.when(step == 0)
    def _():
        carry[...] = mem0_ref[...].astype(F32)

    docs = rows_ref[seg : seg + 1, :].astype(F32)
    flag = rows_ref[seg + 1 : seg + 2, :].astype(F32)
    stat_ref[0, 5:6, :] = flag
    mem = jnp.where(flag[:, :slots] > 0.0, init_ref[...].astype(F32).T, carry[...])
    ga, gf, gw = gain_tiles(gains_ref)

    doc_rows = jnp.broadcast_to(docs, (128, seg)).T
    for at in range(0, seg, 128):
        bias[:, at : at + 128] = jnp.where(doc_rows == docs[:, at : at + 128], 0.0, MASKED)

    tokens = rows_ref[:seg, :].astype(F32).T
    r1 = inverse_rms(tokens)
    a1_ref[...] = (tokens * r1 * wide(ga, seg)).astype(BF16)
    rm = inverse_rms(mem)
    a1m_ref[0] = (mem * rm * ga[:, :slots]).astype(BF16)
    stat_ref[0, 0:1, :] = r1
    stat_ref[0, 4:5, :slots] = rm

    a1 = a1_ref[...]
    a1m = a1m_ref[0]
    q_ref[0] = (nn(wqkv_ref[:width, :], a1) * HEAD_DIM**-0.5).astype(BF16)
    kt = nn(wqkv_ref[width : 2 * width, :], a1).astype(BF16)
    kt_ref[0] = kt
    k_nat[...] = kt.T
    vt[...] = nn(wqkv_ref[2 * width :, :], a1).astype(BF16)
    v_ref[0] = vt[...].T
    ktm = nn(wqkv_ref[width : 2 * width, :], a1m).astype(BF16)
    ktm_ref[0] = ktm
    km_nat[...] = ktm.T
    vtm[...] = nn(wqkv_ref[2 * width :, :], a1m).astype(BF16)
    vm_ref[0] = vtm[...].T

    def pair(index, unused):
        lanes = pl.ds(pl.multiple_of(index * 128, 128), 128)
        keys = k_nat[:, lanes]
        mem_keys = km_nat[:, lanes]
        for half in range(2):
            head = index * 2 + half
            rows = pl.ds(pl.multiple_of(head * HEAD_DIM, HEAD_DIM), HEAD_DIM)
            queries = q_ref[0, rows, :]
            blank = jnp.zeros_like(queries)
            queries = jnp.concatenate([queries, blank] if half == 0 else [blank, queries], axis=0)
            scores = nn(keys, queries) + bias[...]
            mem_scores = nn(mem_keys, queries)
            top = jnp.maximum(
                jnp.max(scores, axis=0, keepdims=True), jnp.max(mem_scores, axis=0, keepdims=True)
            )
            raised = jnp.exp(scores - top)
            mem_raised = jnp.exp(mem_scores - top)
            inverse = 1.0 / (
                jnp.sum(raised, axis=0, keepdims=True) + jnp.sum(mem_raised, axis=0, keepdims=True)
            )
            raised = raised.astype(BF16)
            mem_raised = mem_raised.astype(BF16)
            e_ref[0, head] = raised
            em_ref[0, rows, :] = mem_raised
            mixed = nn(vt[rows, :], raised) + nn(vtm[rows, :], mem_raised)
            att_ref[rows, :] = (mixed * inverse).astype(BF16)
            stat_ref[0, pl.ds(8 + head, 1), :] = inverse
        return unused

    lax.fori_loop(0, HEADS // 2, pair, 0, unroll=HEADS // 2)

    h1 = rows_ref[:seg, :].astype(F32).T + nn(wao_ref[...], att_ref[...])
    r2 = inverse_rms(h1)
    stat_ref[0, 1:2, :] = r2
    a2_ref[...] = (h1 * r2 * wide(gf, seg)).astype(BF16)
    hidden[...] = h1
    a2 = a2_ref[...]
    for at in range(0, ff, 512):
        upper = nn(win_ref[at : at + 512, :], a2)
        square = upper * upper
        bent = jnp.tanh(upper * (SQRT_2_PI + (SQRT_2_PI * CUBIC) * square))
        cdf = 0.5 + 0.5 * bent
        z_ref[at : at + 512, :] = (upper * cdf).astype(BF16)
        slope = (0.5 * SQRT_2_PI) + (1.5 * SQRT_2_PI * CUBIC) * square
        gp_ref[0, at : at + 512, :] = (cdf + upper * (1.0 - bent * bent) * slope).astype(BF16)
    enc = hidden[...] + tn(wout_ref[...], z_ref[...])
    enc_ref[0, :seg, :] = enc.T.astype(BF16)
    r3 = inverse_rms(enc)
    stat_ref[0, 2:3, :] = r3
    a3_ref[...] = (enc * r3 * wide(gw, seg)).astype(BF16)
    a3m_ref[0] = (mem * rm * gw[:, :slots]).astype(BF16)
    a3 = a3_ref[...]
    a3m = a3m_ref[0]

    kwt = nn(ww_ref[width : 2 * width, :], a3).astype(BF16)
    kwt_ref[0] = kwt
    kw = kwt.T
    vwt = nn(ww_ref[2 * width :, :], a3).astype(BF16)
    vw_ref[0] = vwt.T
    kwtm = nn(ww_ref[width : 2 * width, :], a3m).astype(BF16)
    kwtm_ref[0] = kwtm
    vwtm = nn(ww_ref[2 * width :, :], a3m).astype(BF16)
    vwm_ref[0] = vwtm.T
    qwt = (nn(ww_ref[:width, :], a3m) * HEAD_DIM**-0.5).astype(BF16)
    own = head_mask(width, HEADS * slots)
    qw = jnp.where(own, nn(qwt, spread_ref[...]), 0.0).astype(BF16)
    qw_ref[0] = qw
    scores = nn(kw, qw)
    mem_scores = nn(kwtm.T, qw)
    slot_row = lax.broadcasted_iota(jnp.int32, mem_scores.shape, 0)
    slot_col = lax.broadcasted_iota(jnp.int32, mem_scores.shape, 1) % slots
    mem_scores = jnp.where(slot_row == slot_col, mem_scores, MASKED)
    top = jnp.maximum(
        jnp.max(scores, axis=0, keepdims=True), jnp.max(mem_scores, axis=0, keepdims=True)
    )
    raised = jnp.exp(scores - top)
    mem_raised = jnp.exp(mem_scores - top)
    inverse = 1.0 / (
        jnp.sum(raised, axis=0, keepdims=True) + jnp.sum(mem_raised, axis=0, keepdims=True)
    )
    stat_ref[0, 3:4, :] = inverse
    raised = raised.astype(BF16)
    mem_raised = mem_raised.astype(BF16)
    ew_ref[0] = raised
    ewm_ref[0] = mem_raised
    mixed = (nn(vwt, raised) + nn(vwtm, mem_raised)) * inverse
    watt = nn(jnp.where(own, mixed, 0.0).astype(BF16), fold_ref[...]).astype(BF16)
    watt_ref[0] = watt
    new_mem = (mem + nn(wwo_ref[...], watt)).astype(BF16).astype(F32)
    carry[...] = new_mem
    enc_ref[0, seg:, :] = new_mem.T.astype(BF16)
    last_ref[...] = new_mem.astype(BF16)


def chain_kernel(
    sources,
    segs,
    place_ref,
    carry0_ref,
    weights_gains_ref,
    spread_ref,
    fold_ref,
    wwo_ref,
    ww_ref,
    wout_ref,
    win_ref,
    wao_ref,
    wqkv_ref,
    a1m_ref,
    q_ref,
    vm_ref,
    em_ref,
    att_ref,
    a2_ref,
    gp_ref,
    a3_ref,
    a3m_ref,
    qw_ref,
    kwt_ref,
    kwtm_ref,
    vw_ref,
    vwm_ref,
    ew_ref,
    ewm_ref,
    stat_ref,
    *refs,
):
    source_refs, refs = refs[: len(sources.arrays)], refs[len(sources.arrays) :]
    bm_ref, gwkv_ref, gwm_ref, bf_ref, gu_ref, ba_ref, gh_ref, do_ref, dd_ref, dsm_ref = refs[:10]
    gkvm_ref, init_ref, gains_ref, sent_ref, carry, grad_buffer, grad_sems = refs[10:]
    gout_ref = sources.rows_of(
        source_refs, segs, lambda s: segs - 1 - s, place_ref[0], grad_buffer, grad_sems
    )
    step = pl.program_id(0)
    width = wao_ref.shape[0]
    ff = wout_ref.shape[0]
    seg = q_ref.shape[2]
    slots = a1m_ref.shape[2]
    reset = stat_ref[0, 5:6, :slots] > 0.0

    @pl.when(step == 0)
    def _():
        carry[...] = carry0_ref[...].astype(F32)
        init_ref[...] = jnp.zeros_like(init_ref)
        gains_ref[...] = jnp.zeros_like(gains_ref)

    ga, gf, gw = gain_tiles(weights_gains_ref)
    gai, gfi, gwi = 1.0 / ga, 1.0 / gf, 1.0 / gw
    own = head_mask(width, HEADS * slots)
    rm = stat_ref[0, 4:5, :slots]

    grad_mem = gout_ref[seg:, :].astype(F32).T + carry[...]
    branch_mem = grad_mem.astype(BF16)
    bm_ref[0] = branch_mem
    grad_watt = nn(wwo_ref[...], branch_mem).astype(BF16)
    inverse = stat_ref[0, 3:4, :]
    scaled = (jnp.where(own, nn(grad_watt, spread_ref[...]), 0.0) * inverse).astype(BF16)
    raised = ew_ref[0].astype(F32)
    mem_raised = ewm_ref[0].astype(F32)
    grad_probs = nn(vw_ref[0], scaled)
    mem_grad_probs = nn(vwm_ref[0], scaled)
    dots = (
        jnp.sum(raised * grad_probs, axis=0, keepdims=True)
        + jnp.sum(mem_raised * mem_grad_probs, axis=0, keepdims=True)
    ) * inverse
    grad_scores = (raised * (grad_probs - dots)).astype(BF16)
    mem_grad_scores = (mem_raised * (mem_grad_probs - dots)).astype(BF16)
    gwkv_ref[:width, :] = nt(qw_ref[0], grad_scores).astype(BF16)
    gwkv_ref[width:, :] = nt(scaled, ew_ref[0]).astype(BF16)
    grad_q = (nn(kwt_ref[0], grad_scores) + nn(kwtm_ref[0], mem_grad_scores)) * HEAD_DIM**-0.5
    gwm_ref[0, :width, :] = nn(jnp.where(own, grad_q, 0.0).astype(BF16), fold_ref[...]).astype(BF16)
    gwm_ref[0, width : 2 * width, :] = nt(qw_ref[0], mem_grad_scores).astype(BF16)
    gwm_ref[0, 2 * width :, :] = nt(scaled, ewm_ref[0]).astype(BF16)

    grad_a3 = nn(ww_ref[:, width:], gwkv_ref[...])
    grad_a3m = nn(ww_ref[...], gwm_ref[0])
    part, weighed = norm_back(
        grad_a3, a3_ref[...].astype(F32), stat_ref[0, 2:3, :], wide(gw, seg), wide(gwi, seg)
    )
    mem_part, mem_weighed = norm_back(
        grad_a3m, a3m_ref[0].astype(F32), rm, gw[:, :slots], gwi[:, :slots]
    )
    gains_ref[2] += lane_sums(weighed)
    gains_ref[2, :, :slots] += mem_weighed
    grad_mem_in = grad_mem + mem_part
    gh_ref[0] = gout_ref[:seg, :].astype(F32).T + part

    bf_ref[...] = gh_ref[0].astype(BF16)
    branch = bf_ref[...]
    for at in range(0, ff, 512):
        grad_z = nn(wout_ref[at : at + 512, :], branch)
        gu_ref[at : at + 512, :] = (grad_z * gp_ref[0, at : at + 512, :].astype(F32)).astype(BF16)
    grad_a2 = nn(win_ref[...], gu_ref[...])
    part, weighed = norm_back(
        grad_a2, a2_ref[...].astype(F32), stat_ref[0, 1:2, :], wide(gf, seg), wide(gfi, seg)
    )
    gains_ref[1] += lane_sums(weighed)
    gh_ref[0] += part

    ba_ref[...] = gh_ref[0].astype(BF16)
    grad_att = nn(wao_ref[...], ba_ref[...]).astype(BF16)
    products = grad_att.astype(F32) * att_ref[...].astype(F32)
    rows = []
    dots = []
    for head in range(HEADS):
        span = slice(head * HEAD_DIM, (head + 1) * HEAD_DIM)
        inverse = stat_ref[0, 8 + head : 9 + head, :]
        dots.append(jnp.sum(products[span, :], axis=0, keepdims=True) * inverse)
        rows.append((grad_att[span, :].astype(F32) * inverse).astype(BF16))
    scaled = jnp.concatenate(rows, axis=0)
    do_ref[0] = scaled
    dd_ref[0] = jnp.concatenate(dots, axis=0)
    mem_values = jnp.concatenate([vm_ref[0].astype(F32)] * HEADS, axis=0)
    mem_values = jnp.where(own, mem_values, 0.0).astype(BF16)
    grad_probs = nn(mem_values, scaled)
    parts = []
    for head in range(HEADS):
        span = slice(head * slots, (head + 1) * slots)
        parts.append(
            (em_ref[0, span, :].astype(F32) * (grad_probs[span, :] - dots[head])).astype(BF16)
        )
    grad_scores = jnp.concatenate(parts, axis=0)
    dsm_ref[0] = grad_scores
    grad_k = jnp.where(own, nt(q_ref[0], grad_scores), 0.0).astype(BF16)
    grad_v = jnp.where(own, nt(scaled, em_ref[0]), 0.0).astype(BF16)
    gkvm_ref[0, :width, :] = nn(grad_k, fold_ref[...]).astype(BF16)
    gkvm_ref[0, width:, :] = nn(grad_v, fold_ref[...]).astype(BF16)
    grad_a1m = nn(wqkv_ref[:, width:], gkvm_ref[0])
    mem_part, mem_weighed = norm_back(
        grad_a1m, a1m_ref[0].astype(F32), rm, ga[:, :slots], gai[:, :slots]
    )
    gains_ref[0, :, :slots] += mem_weighed
    grad_mem_in = grad_mem_in + mem_part
    init_ref[...] += jnp.where(reset, grad_mem_in, 0.0)
    carry[...] = jnp.where(reset, 0.0, grad_mem_in).astype(BF16).astype(F32)
    sent_ref[...] = carry[...].astype(BF16)


def attention_kernel(
    place_ref,
    do_ref,
    dd_ref,
    dsm_ref,
    gh_ref,
    q_ref,
    kt_ref,
    ktm_ref,
    v_ref,
    e_ref,
    a1_ref,
    stat_ref,
    gains_ref,
    wqkv_ref,
    *refs,
):
    gqkv_ref, out_ref, gain_ref = refs[-3:]
    pair = pl.program_id(1)
    width = wqkv_ref.shape[0]
    seg = q_ref.shape[2]
    for half in range(HEADS_A_STEP):
        head = pair * HEADS_A_STEP + half
        base = pl.multiple_of(head * HEAD_DIM, HEAD_DIM)
        span = slice(half * HEAD_DIM, (half + 1) * HEAD_DIM)
        grads = do_ref[0, span, :]
        blank = jnp.zeros_like(grads)
        padded = jnp.concatenate([grads, blank] if half % 2 == 0 else [blank, grads], axis=0)
        dots = dd_ref[0, pl.ds(head, 1), :]
        lanes = slice(half // 2 * 128, half // 2 * 128 + 128)
        grad_probs = nn(v_ref[0, :, lanes], padded)
        inner = (e_ref[0, half].astype(F32) * (grad_probs - dots)).astype(BF16)
        grad_q = nn(kt_ref[0, span, :], inner) + nn(ktm_ref[0, span, :], dsm_ref[0, span, :])
        gqkv_ref[pl.ds(base, HEAD_DIM), :] = (grad_q * HEAD_DIM**-0.5).astype(BF16)
        gqkv_ref[pl.ds(width + base, HEAD_DIM), :] = nt(q_ref[0, span, :], inner).astype(BF16)
        gqkv_ref[pl.ds(2 * width + base, HEAD_DIM), :] = nt(grads, e_ref[0, half]).astype(BF16)

    @pl.when((pl.program_id(0) == 0) & (pair == 0))
    def _():
        gain_ref[...] = jnp.zeros_like(gain_ref)

    @pl.when(pair == pl.num_programs(1) - 1)
    def _():
        grad_a1 = nn(wqkv_ref[...], gqkv_ref[...])
        (ga,) = gain_tiles(gains_ref, 1)
        part, weighed = norm_back(
            grad_a1,
            a1_ref[...].astype(F32),
            stat_ref[0, 0:1, :],
            wide(ga, seg),
            wide(1.0 / ga, seg),
        )
        gain_ref[...] += lane_sums(weighed)
        out_ref[0] = (gh_ref[0] + part).T.astype(BF16)


def whole(array):
    zeros = (0,) * array.ndim
    return pl.BlockSpec(array.shape, lambda *unused: zeros, pipeline_mode=pl.Buffered(1))


def params():
    return pltpu.CompilerParams(dimension_semantics=("arbitrary",), vmem_limit_bytes=VMEM_LIMIT)


def cost(microseconds):
    return pl.CostEstimate(
        flops=int(microseconds * 1e9), bytes_accessed=1 << 20, transcendentals=0
    )


def forward_chain(sources, place, mem0, consts, w):
    segs = consts["segs"]
    seg = consts["seg"]
    width, slots = mem0.shape
    ff = w["in_t"].shape[0]

    def flat(height):
        return (
            jax.ShapeDtypeStruct((height, segs * seg), BF16),
            pl.BlockSpec((height, seg), lambda s, f: (0, s)),
        )

    def stack(*shape, dtype=BF16):
        tail = (0,) * len(shape)
        return (
            jax.ShapeDtypeStruct((segs,) + shape, dtype),
            pl.BlockSpec((1,) + shape, lambda s, f: (s,) + tail),
        )

    outs = dict(
        enc=stack(seg + slots, width),
        a1=flat(width),
        a1m=stack(width, slots),
        q=stack(width, seg),
        kt=stack(width, seg),
        ktm=stack(width, slots),
        v=stack(seg, width),
        vm=stack(slots, width),
        e=stack(HEADS, seg, seg),
        em=stack(HEADS * slots, seg),
        att=flat(width),
        a2=flat(width),
        z=flat(ff),
        gp=stack(ff, seg),
        a3=flat(width),
        a3m=stack(width, slots),
        qw=stack(width, HEADS * slots),
        kwt=stack(width, seg),
        kwtm=stack(width, slots),
        vw=stack(seg, width),
        vwm=stack(slots, width),
        ew=stack(seg, HEADS * slots),
        ewm=stack(slots, HEADS * slots),
        watt=stack(width, slots),
        stat=stack(16, seg, dtype=F32),
        last=(
            jax.ShapeDtypeStruct((width, slots), BF16),
            pl.BlockSpec((width, slots), lambda s, f: (0, 0)),
        ),
    )
    fixed = [
        mem0,
        consts["init"],
        consts["gains"],
        consts["spread"],
        consts["fold"],
    ]
    weights = [w[name] for name in ("qkv_t", "ao_t", "in_t", "out", "write_t", "wo_t")]
    results = pl.pallas_call(
        lambda *refs: forward_kernel(sources, segs, *refs),
        grid_spec=pltpu.PrefetchScalarGridSpec(
            num_scalar_prefetch=1,
            grid=(segs,),
            in_specs=[whole(a) for a in fixed + weights]
            + [pl.BlockSpec(memory_space=pl.ANY)] * len(sources.arrays),
            out_specs=[spec for _, spec in outs.values()],
            scratch_shapes=[
                pltpu.VMEM((width, slots), F32),
                pltpu.VMEM((seg, seg), F32),
                pltpu.VMEM((seg, width), BF16),
                pltpu.VMEM((slots, width), BF16),
                pltpu.VMEM((width, seg), BF16),
                pltpu.VMEM((width, slots), BF16),
                pltpu.VMEM((width, seg), F32),
                pltpu.VMEM((2, seg + 16, width), BF16),
                pltpu.SemaphoreType.DMA((2,)),
            ],
        ),
        out_shape=[shape for shape, _ in outs.values()],
        compiler_params=params(),
        cost_estimate=cost(15 * segs),
        name="forward_chain",
    )(place, *fixed, *weights, *sources.arrays)
    return dict(zip(outs, results))


def backward_chain(kept, sources, place, carry0, consts, w):
    segs = consts["segs"]
    width, slots = kept["a1m"].shape[1:]
    seg = kept["q"].shape[2]
    ff = kept["gp"].shape[1]
    last = segs - 1

    def flat(height):
        return (
            jax.ShapeDtypeStruct((height, segs * seg), BF16),
            pl.BlockSpec((height, seg), lambda s, f: (0, last - s)),
        )

    def stack(*shape, dtype=BF16):
        tail = (0,) * len(shape)
        return (
            jax.ShapeDtypeStruct((segs,) + shape, dtype),
            pl.BlockSpec((1,) + shape, lambda s, f: (last - s,) + tail),
        )

    def single(*shape, dtype=F32):
        tail = (0,) * len(shape)
        return (jax.ShapeDtypeStruct(shape, dtype), pl.BlockSpec(shape, lambda s, f: tail))

    outs = dict(
        bm=stack(width, slots),
        gwkv=flat(2 * width),
        gwm=stack(3 * width, slots),
        bf=flat(width),
        gu=flat(ff),
        ba=flat(width),
        gh=stack(width, seg, dtype=F32),
        do=stack(width, seg),
        dd=stack(HEADS, seg, dtype=F32),
        dsm=stack(HEADS * slots, seg),
        gkvm=stack(2 * width, slots),
        init=single(width, slots),
        gains=single(3, width, 128),
        sent=single(width, slots, dtype=BF16),
    )
    fixed = [
        carry0,
        consts["gains"],
        consts["spread"],
        consts["fold"],
    ]
    weights = [w[name] for name in ("wo", "write", "out", "in", "ao", "qkv")]
    blocked = ["a1m", "q", "vm", "em", "att", "a2", "gp", "a3", "a3m", "qw"]
    blocked += ["kwt", "kwtm", "vw", "vwm", "ew", "ewm", "stat"]

    def spec_of(array):
        if array.ndim == 2:
            return pl.BlockSpec((array.shape[0], seg), lambda s, f: (0, last - s))
        tail = (0,) * (array.ndim - 1)
        return pl.BlockSpec((1,) + array.shape[1:], lambda s, f: (last - s,) + tail)

    results = pl.pallas_call(
        lambda *refs: chain_kernel(sources, segs, *refs),
        grid_spec=pltpu.PrefetchScalarGridSpec(
            num_scalar_prefetch=1,
            grid=(segs,),
            in_specs=[whole(a) for a in fixed + weights]
            + [spec_of(kept[name]) for name in blocked]
            + [pl.BlockSpec(memory_space=pl.ANY)] * len(sources.arrays),
            out_specs=[spec for _, spec in outs.values()],
            scratch_shapes=[
                pltpu.VMEM((width, slots), F32),
                pltpu.VMEM((2, seg + slots, width), BF16),
                pltpu.SemaphoreType.DMA((2,)),
            ],
        ),
        out_shape=[shape for shape, _ in outs.values()],
        compiler_params=params(),
        cost_estimate=cost(11 * segs),
        name="backward_chain",
    )(place, *fixed, *weights, *[kept[name] for name in blocked], *sources.arrays)
    return dict(zip(outs, results))


def attention_back(kept, grads, which, consts, w, before):
    segs, width, seg = kept["q"].shape
    count = which.shape[0]
    pair = HEADS_A_STEP * HEAD_DIM

    def by_pair(rows, lanes):
        return pl.BlockSpec((1, rows, lanes), lambda s, h, f: (f[s], h, 0))

    def by_seg(array):
        tail = (0,) * (array.ndim - 1)
        return pl.BlockSpec((1,) + array.shape[1:], lambda s, h, f: (f[s],) + tail)

    inputs = [
        (grads["do"], by_pair(pair, seg)),
        (grads["dd"], by_seg(grads["dd"])),
        (grads["dsm"], by_pair(pair, seg)),
        (grads["gh"], by_seg(grads["gh"])),
        (kept["q"], by_pair(pair, seg)),
        (kept["kt"], by_pair(pair, seg)),
        (kept["ktm"], by_pair(pair, kept["ktm"].shape[2])),
        (kept["v"], pl.BlockSpec((1, seg, pair), lambda s, h, f: (f[s], 0, h))),
        (kept["e"], pl.BlockSpec((1, HEADS_A_STEP, seg, seg), lambda s, h, f: (f[s], h, 0, 0))),
        (kept["a1"], pl.BlockSpec((width, seg), lambda s, h, f: (0, f[s]))),
        (kept["stat"], by_seg(kept["stat"])),
        (consts["gains"], whole(consts["gains"])),
        (w["qkv"], whole(w["qkv"])),
    ]
    passed = [] if before is None else [before]
    return pl.pallas_call(
        attention_kernel,
        grid_spec=pltpu.PrefetchScalarGridSpec(
            num_scalar_prefetch=1,
            grid=(count, HEADS // HEADS_A_STEP),
            in_specs=[spec for _, spec in inputs]
            + [pl.BlockSpec(memory_space=pl.ANY)] * len(passed),
            out_specs=[
                pl.BlockSpec((3 * width, seg), lambda s, h, f: (0, f[s])),
                pl.BlockSpec((1, seg, width), lambda s, h, f: (s, 0, 0)),
                pl.BlockSpec((width, 128), lambda s, h, f: (0, 0)),
            ],
        ),
        out_shape=[
            jax.ShapeDtypeStruct((3 * width, segs * seg), BF16),
            jax.ShapeDtypeStruct((count, seg, width), BF16),
            jax.ShapeDtypeStruct((width, 128), F32),
        ],
        input_output_aliases={1 + len(inputs): 0} if passed else {},
        compiler_params=pltpu.CompilerParams(
            dimension_semantics=("arbitrary", "arbitrary"), vmem_limit_bytes=VMEM_LIMIT
        ),
        cost_estimate=cost(10 * count),
        name="attention_back",
    )(which, *[array for array, _ in inputs], *passed)


def swap_pairs(value, axis, mask):
    size = lax.axis_size(axis)
    return lax.ppermute(value, axis, [(i, i ^ mask) for i in range(size)])


def sum_phases(dp_first=False):
    section = [("section", 1 << at) for at in range(lax.axis_size("section").bit_length() - 1)]
    dp = [("dp", 1 << at) for at in range(lax.axis_size("dp").bit_length() - 1)]
    phases = [(step, step) for step in section[:1]]
    crossed = []
    if len(section) > 1 and dp:
        crossed = [(dp[0], section[1]), (section[1], dp[0])]
        section, dp = section[2:], dp[1:]
    else:
        section = section[1:]
    straight = [(step, step) for step in dp + section]
    return phases + (straight + crossed if dp_first else crossed + straight)


def phase_swap(value, phase):
    sections, dps = lax.axis_size("section"), lax.axis_size("dp")
    route = []
    for section in range(sections):
        axis, mask = phase[section % 2]
        for dp in range(dps):
            to = ((section ^ mask) * dps + dp) if axis == "section" else (section * dps + (dp ^ mask))
            route.append((section * dps + dp, to))
    return lax.ppermute(value, ("section", "dp"), route)


def phase_bit(phase):
    bits = [(lax.axis_index(axis) // mask) % 2 for axis, mask in phase]
    return jnp.where(lax.axis_index("section") % 2 == 0, bits[0], bits[1])


def half_of(value, side):
    half = value.shape[0] // 2
    return lax.dynamic_slice_in_dim(value, side * half, half, 0)


def fetch(source, target, sem):
    copy = pltpu.make_async_copy(source, target, sem)
    copy.start()
    return copy


def slot_sum(left, right):
    join = lambda ref: jnp.concatenate([ref[at] for at in range(ref.shape[0])], axis=1)
    return nt(join(left), join(right))


def early_weights_kernel(
    side_ref, a2_ref, gu_ref, bf_ref, z_ref, a3_ref, gwkv_ref, a3m_ref, gwm_ref, watt_ref, bm_ref, *refs
):
    ffn_ref, write_ref, a2, gu, z, bf, a3, gw, a3m, gwm, left, right, staged, in_sems, out_sems = refs
    side = side_ref[0]
    width = a2.shape[0]
    folds = gu.shape[0]
    base = side * (folds * width)
    loads = []

    def load(source, target):
        loads.append(fetch(source, target, in_sems.at[len(loads)]))

    def wait(count):
        for _ in range(count):
            loads[wait.done].wait()
            wait.done += 1

    wait.done = 0
    load(a2_ref, a2)
    for at in range(folds):
        rows = pl.ds(pl.multiple_of(base + at * width, width), width)
        load(gu_ref.at[rows, :], gu.at[at])
    load(bf_ref, bf)
    for at in range(folds):
        rows = pl.ds(pl.multiple_of(base + at * width, width), width)
        load(z_ref.at[rows, :], z.at[at])
    load(a3_ref, a3)
    load(gwkv_ref.at[pl.ds(pl.multiple_of(side * width, width), width), :], gw)
    load(a3m_ref, a3m)
    load(gwm_ref.at[:, pl.ds(pl.multiple_of((1 + side) * width, width), width), :], gwm)
    last = in_sems.at[len(loads)]

    @pl.when(side == 0)
    def _():
        pltpu.make_async_copy(a3m_ref, left, last).start()
        pltpu.make_async_copy(gwm_ref.at[:, pl.ds(0, width), :], right, last).start()

    @pl.when(side == 1)
    def _():
        pltpu.make_async_copy(watt_ref, left, last).start()
        pltpu.make_async_copy(bm_ref, right, last).start()

    stores = []

    def put(tile, value):
        columns = slice(tile * width, (tile + 1) * width)
        staged[:, columns] = value.astype(BF16)
        out, first = (ffn_ref, 0) if tile < 2 * folds else (write_ref, 2 * folds)
        target = out.at[:, pl.ds((tile - first) * width, width)]
        stores.append(fetch(staged.at[:, columns], target, out_sems.at[tile]))

    wait(1)
    for at in range(folds):
        wait(1)
        put(at, nt(a2[...], gu[at]))
    wait(1)
    for at in range(folds):
        wait(1)
        put(folds + at, nt(z[at], bf[...]))
    wait(4)
    put(2 * folds, nt(a3[...], gw[...]) + slot_sum(a3m, gwm))
    pltpu.make_async_copy(watt_ref, left, last).wait()
    pltpu.make_async_copy(bm_ref, right, last).wait()
    put(2 * folds + 1, slot_sum(left, right))
    for store in stores:
        store.wait()


def early_weights(kept, grads, side):
    width, tokens = kept["a2"].shape
    folds = kept["z"].shape[0] // 2 // width
    inputs = [kept["a2"], grads["gu"], grads["bf"], kept["z"], kept["a3"], grads["gwkv"]]
    inputs += [kept["a3m"], grads["gwm"], kept["watt"], grads["bm"]]
    anywhere = pl.BlockSpec(memory_space=pl.ANY)
    full = pltpu.VMEM((width, tokens), BF16)
    several = pltpu.VMEM((folds, width, tokens), BF16)
    slots = pltpu.VMEM(kept["a3m"].shape, BF16)
    out = jax.ShapeDtypeStruct((width, (2 * folds + 2) * width), BF16)
    return pl.pallas_call(
        early_weights_kernel,
        grid_spec=pltpu.PrefetchScalarGridSpec(
            num_scalar_prefetch=1,
            grid=(1,),
            in_specs=[anywhere] * len(inputs),
            out_specs=[anywhere] * 2,
            scratch_shapes=[full, several, several, full, full, full]
            + [slots] * 4
            + [
                pltpu.VMEM(out.shape, BF16),
                pltpu.SemaphoreType.DMA((7 + 2 * folds,)),
                pltpu.SemaphoreType.DMA((2 * folds + 2,)),
            ],
        ),
        out_shape=[
            jax.ShapeDtypeStruct((width, 2 * folds * width), BF16),
            jax.ShapeDtypeStruct((width, 2 * width), BF16),
        ],
        compiler_params=params(),
        cost_estimate=cost(9),
        name="early_weights",
    )(side, *inputs)


def late_weights_kernel(count, side_ref, a1_ref, gqkv_ref, att_ref, ba_ref, a1m_ref, gkvm_ref, *refs):
    init_ref, gains_ref, refs = refs[0], refs[1], refs[2:]
    part_refs, refs = refs[:count], refs[count:]
    out_ref, a1, main, left, right, a1m, gkvm, init, gains, parts, staged, in_sems, out_sems = refs
    side = side_ref[0]
    width = a1.shape[0]
    slots = init.shape[1]
    rows = pl.ds(pl.multiple_of((1 + side) * width, width), width)
    kv_rows = pl.ds(pl.multiple_of(side * width, width), width)
    loads = [
        fetch(a1_ref, a1, in_sems.at[0]),
        fetch(gqkv_ref.at[rows, :], main, in_sems.at[1]),
        fetch(a1m_ref, a1m, in_sems.at[2]),
        fetch(gkvm_ref.at[:, kv_rows, :], gkvm, in_sems.at[3]),
    ]

    @pl.when(side == 0)
    def _():
        pltpu.make_async_copy(a1_ref, left, in_sems.at[4]).start()
        pltpu.make_async_copy(gqkv_ref.at[pl.ds(0, width), :], right, in_sems.at[5]).start()

    @pl.when(side == 1)
    def _():
        pltpu.make_async_copy(att_ref, left, in_sems.at[4]).start()
        pltpu.make_async_copy(ba_ref, right, in_sems.at[5]).start()

    others = [fetch(init_ref, init, in_sems.at[6]), fetch(gains_ref, gains, in_sems.at[7])]
    others += [fetch(ref, parts.at[at], in_sems.at[8 + at]) for at, ref in enumerate(part_refs)]
    stores = []

    def put(columns, value):
        staged[:, columns] = value.astype(BF16)
        stores.append(fetch(staged.at[:, columns], out_ref.at[:, columns], out_sems.at[len(stores)]))

    for load in loads:
        load.wait()
    put(slice(0, width), nt(a1[...], main[...]) + slot_sum(a1m, gkvm))
    pltpu.make_async_copy(att_ref, left, in_sems.at[4]).wait()
    pltpu.make_async_copy(ba_ref, right, in_sems.at[5]).wait()
    put(slice(width, 2 * width), nt(left[...], right[...]))
    for load in others:
        load.wait()
    columns = [gains[0], gains[1], gains[2]]
    for at in range(count):
        columns[0] = columns[0] + parts[at]
    lane = lax.broadcasted_iota(jnp.int32, init.shape, 1)
    extras = jnp.zeros(init.shape, F32)
    for at, column in enumerate(columns):
        extras = jnp.where(lane == at, jnp.sum(column, axis=1, keepdims=True), extras)
    extras = jnp.where(side == 0, init[...], extras)
    extras = jnp.concatenate([extras, jnp.zeros_like(extras)], axis=1)
    put(slice(2 * width, 2 * width + 2 * slots), extras)
    for store in stores:
        store.wait()


def late_weights(kept, grads, gqkv, gain_parts, side):
    width, tokens = kept["a1"].shape
    count = len(gain_parts)
    inputs = [kept["a1"], gqkv, kept["att"], grads["ba"], kept["a1m"], grads["gkvm"]]
    inputs += [grads["init"], grads["gains"]] + list(gain_parts)
    slots = grads["init"].shape[1]
    anywhere = pl.BlockSpec(memory_space=pl.ANY)
    full = pltpu.VMEM((width, tokens), BF16)
    small = pltpu.VMEM(kept["a1m"].shape, BF16)
    out = jax.ShapeDtypeStruct((width, 2 * width + 2 * slots), BF16)
    return pl.pallas_call(
        lambda *refs: late_weights_kernel(count, *refs),
        grid_spec=pltpu.PrefetchScalarGridSpec(
            num_scalar_prefetch=1,
            grid=(1,),
            in_specs=[anywhere] * len(inputs),
            out_specs=anywhere,
            scratch_shapes=[full] * 4
            + [small] * 2
            + [
                pltpu.VMEM(grads["init"].shape, F32),
                pltpu.VMEM(grads["gains"].shape, F32),
                pltpu.VMEM((count,) + gain_parts[0].shape, F32),
                pltpu.VMEM(out.shape, BF16),
                pltpu.SemaphoreType.DMA((8 + count,)),
                pltpu.SemaphoreType.DMA((3,)),
            ],
        ),
        out_shape=out,
        compiler_params=params(),
        cost_estimate=cost(4),
        name="late_weights",
    )(side, *inputs)


class Sum:
    def __init__(self, value, share, halve_all=False, dp_first=False):
        self.phases = sum_phases(dp_first)
        inner = self.phases[1:]
        self.value = value
        self.share = share
        halvings = 0
        most = len(inner) - (0 if halve_all else 1)
        while halvings < most and value.shape[0] >> (halvings + 1) >= 16:
            halvings += 1
        self.halved = inner[:halvings]
        self.steps = [("halve", phase) for phase in self.halved]
        self.steps += [("add", phase) for phase in inner[halvings:]]
        self.steps += [("double", phase) for phase in reversed(self.halved)]
        self.steps += [("last", self.phases[0])]
        self.started = None

    def prepare(self):
        kind, phase = self.steps.pop(0)
        if kind == "halve":
            bit = phase_bit(phase)
            value = self.value
            self.sent, self.value = half_of(value, 1 - bit), half_of(value, bit)
            if self.share is not None:
                self.sent = self.sent + half_of(self.share, 1 - bit)
                self.value = self.value + half_of(self.share, bit)
        else:
            if self.share is not None:
                self.value = self.value + self.share
            self.sent = self.value
        self.share = None
        self.ready = (kind, phase)

    def launch(self):
        kind, phase = self.ready
        if kind == "last" and isinstance(self.sent, tuple):
            self.started = (kind, tuple(phase_swap(piece, phase) for piece in self.sent))
        else:
            self.started = (kind, phase_swap(self.sent, phase))

    def finish(self, *after):
        kind, other = self.started
        self.started = None
        other, after = lax.optimization_barrier((other, after))
        if kind in ("halve", "add"):
            self.value = self.value + other
        elif kind == "double" and len(self.steps) == 1:
            self.value = (self.value, other)
        elif kind == "double":
            self.value = jnp.concatenate([self.value, other], axis=0)
        elif isinstance(other, tuple):
            self.value = (self.value, other)
        else:
            self.value = ((self.value,), (other,))
        return list(after)

    def places(self):
        own = sum(phase_bit(phase) << at for at, phase in enumerate(reversed(self.halved)))
        swapped = [(late, early) for early, late in self.halved]
        other = sum(phase_bit(phase) << at for at, phase in enumerate(reversed(swapped)))
        numbers = jnp.stack([phase_bit(self.phases[0]), jnp.int32(own), jnp.int32(other)])
        return numbers.astype(jnp.int32), 1 << len(self.halved)


def advance(totals, *after, extra=()):
    going = []
    for total in totals:
        if total.started is not None:
            total.finish(*after)
        if total.steps:
            total.prepare()
            going.append(total)
    joined, extra = lax.optimization_barrier(([total.sent for total in going], list(extra)))
    for total, sent in zip(going, joined):
        if total.value is total.sent:
            total.value = sent
        total.sent = sent
        total.launch()
    return joined, extra


def unpack_kernel(count, parts, regions, kept, place_ref, *refs):
    own_refs, other_refs, refs = refs[:parts], refs[parts : 2 * parts], refs[2 * parts :]
    gains_ref = None
    if kept:
        gains_ref, refs = refs[0], refs[1:]
    outs = len(refs) // 2
    out_refs, staged, sems = refs[:outs], refs[outs : 2 * outs], refs[2 * outs]
    each = count // parts
    rows = own_refs[0].shape[0] // each
    height = rows * count

    def take(refs, side, number, sem):
        copies = []
        for start, stop, at, top, left in regions[side]:
            for block in range(count):
                target = pl.multiple_of(top + (block ^ place_ref[number]) * rows, rows)
                inner = (block % each) * rows
                value = refs[block // each][inner : inner + rows, start:stop].astype(F32)
                staged[at][pl.ds(target, rows), left : left + stop - start] = value
            if at >= outs - kept:
                continue
            slab = (pl.ds(top, height), pl.ds(left, stop - start))
            copies.append((staged[at].at[slab], out_refs[at].at[slab], sems.at[sem + len(copies)]))
            pltpu.make_async_copy(*copies[-1]).start()
        return copies

    for side in range(2):

        @pl.when(place_ref[0] == side)
        def _():
            copies = take(own_refs, side, 1, 0)
            copies += take(other_refs, 1 - side, 2, len(copies))
            for copy in copies:
                pltpu.make_async_copy(*copy).wait()

    if kept:
        init_ref, total_ref = out_refs[outs - 2 :]
        init_ref[...] = staged[outs - 2][...].T[: init_ref.shape[0], :]
        total_ref[...] = staged[outs - 1][...].T[: total_ref.shape[0], :] / gains_ref[...]


def unpacked(total, regions, shapes, slots=0, gains=None):
    own, other = total.value
    places, count = total.places()
    parts = len(own)
    kept = 0 if gains is None else 2
    vmem = pl.BlockSpec(memory_space=pltpu.VMEM)
    outs = [jax.ShapeDtypeStruct(shape, F32) for shape in shapes[: len(shapes) - kept]]
    specs = [pl.BlockSpec(memory_space=pl.ANY)] * len(outs)
    inputs = [*own, *other]
    if kept:
        inputs.append(gains)
        outs += [jax.ShapeDtypeStruct((rows, shapes[-1][0]), F32) for rows in (slots, gains.shape[0])]
        specs += [vmem] * 2
    return pl.pallas_call(
        lambda *refs: unpack_kernel(count, parts, regions, kept, *refs),
        in_specs=[pl.BlockSpec(memory_space=pltpu.SMEM)] + [vmem] * len(inputs),
        out_specs=specs,
        out_shape=outs,
        scratch_shapes=[pltpu.VMEM(shape, F32) for shape in shapes]
        + [pltpu.SemaphoreType.DMA((len(regions[0]) + len(regions[1]),))],
        compiler_params=pltpu.CompilerParams(vmem_limit_bytes=VMEM_LIMIT),
        cost_estimate=cost(4),
        name="unpack",
    )(places, *inputs)


def pieces_in(value, place):
    parts = [lax.dynamic_index_in_dim(value, place, 0, keepdims=True)]
    sent = []
    for mask in range(1, lax.axis_size("section")):
        sent.append(lax.dynamic_index_in_dim(value, place ^ mask, 0, keepdims=True))
        parts.append(swap_pairs(sent[-1], "section", mask))
    return in_rank_order(jnp.concatenate(parts, axis=0), place), sent, parts[1:]


def in_rank_order(pieces, place):
    count = pieces.shape[0]
    return jnp.stack(
        [lax.dynamic_index_in_dim(pieces, at ^ place, 0, keepdims=False) for at in range(count)]
    )


def sources_in(arrays, place):
    sections = lax.axis_size("section")
    sent = []
    for mask in range(1, sections):
        picked = [lax.dynamic_index_in_dim(a, place ^ mask, 0, keepdims=True) for a in arrays]
        sent.append(jnp.concatenate(picked, axis=1))
    sent = list(lax.optimization_barrier(tuple(sent)))
    pieces = [swap_pairs(value, "section", mask + 1) for mask, value in enumerate(sent)]
    own = len(arrays)

    def choose(at, here):
        yield (at ^ here) == 0, [(number, here) for number in range(own)]
        for other in range(1, sections):
            yield (at ^ here) == other, [(own + other - 1, 0)]

    return Sources(list(arrays) + pieces, choose), pieces, sent


def gathered_sources(arrays, chunks):
    rows = gathered_in(jnp.concatenate(arrays, axis=1), chunks)
    return Sources([rows], lambda at, here: [(at >= 0, [(0, at)])])


def gathered_in(value, chunks):
    place = lax.axis_index("section")
    gathered = lax.all_gather(value, "section")
    own = lax.dynamic_index_in_dim(gathered, place // chunks, 1, keepdims=False)
    count = gathered.shape[0] // chunks
    return lax.dynamic_slice_in_dim(own, (place % chunks) * count, count, 0)


def gathered_out(value, chunks):
    place = lax.axis_index("section")
    gathered = lax.all_gather(value, "section")
    sections = gathered.shape[0]
    by_stream = gathered.reshape((sections // chunks, chunks * value.shape[0]) + value.shape[1:])
    return lax.dynamic_index_in_dim(by_stream, place, 1, keepdims=False)


def tied(value, *others):
    return lax.optimization_barrier((value,) + others)[0]


def body(
    tokens,
    doc_ids,
    reset_flags,
    attn_gain,
    w_qkv,
    w_attn_out,
    ffn_gain,
    w_in,
    w_out,
    write_gain,
    w_write,
    w_write_out,
    init_memory,
    out_grad,
    memory_grad,
):
    streams, _, seg, width = tokens.shape
    slots = init_memory.shape[0]
    sections = lax.axis_size("section")
    chunks = sections // streams
    segs = sections // chunks
    place = lax.axis_index("section")

    spread = np.tile(np.eye(slots, dtype=np.float32), (1, HEADS))
    consts = dict(
        segs=segs,
        seg=seg,
        init=init_memory,
        gains=jnp.stack([attn_gain, ffn_gain, write_gain]).astype(F32),
        spread=jnp.asarray(spread, BF16),
        fold=jnp.asarray(spread.T, BF16),
    )
    w = dict(
        qkv=w_qkv,
        ao=w_attn_out,
        out=w_out,
        write=w_write,
        wo=w_write_out,
        qkv_t=w_qkv.T,
        ao_t=w_attn_out.T,
        in_t=w_in.T,
        write_t=w_write.T,
        wo_t=w_write_out.T,
    )
    w["in"] = w_in

    marks = jnp.concatenate(
        [doc_ids[:, 0], jnp.broadcast_to(reset_flags, (streams, seg))], axis=1
    ).reshape(streams, 2, seg)
    marks = jnp.pad(marks, ((0, 0), (0, 14), (0, 0))).astype(BF16)
    parts_in = [tokens[:, 0], marks]
    grads_in = [out_grad[:, 0], memory_grad[:, 0]]
    empty = jnp.zeros((width, slots), BF16)
    if chunks == 1:
        rows, pieces, _ = sources_in(parts_in, place)
        gout, _, sent = sources_in([tied(value, *pieces) for value in grads_in], place)
        xor = place
    else:
        rows = gathered_sources(parts_in, chunks)
        gout = gathered_sources(grads_in, chunks)
        sent = []
        xor = 0
    xor = jnp.full((1,), xor, jnp.int32)

    arriving = empty
    then = tied(xor, *sent)
    for turn in range(chunks):
        kept = forward_chain(rows, then, arriving, consts, w)
        if turn < chunks - 1:
            arriving = lax.ppermute(
                kept["last"], "section", [(i, i + 1) for i in range(sections - 1)]
            )
    if chunks == 1:
        done, sent, pieces = pieces_in(kept["enc"], place)
        then = tied(xor, *sent)
    else:
        done = gathered_out(kept["enc"], chunks)
        pieces = []
        then = xor

    returning = empty
    for turn in range(chunks):
        grads = backward_chain(kept, gout, then, returning, consts, w)
        if turn < chunks - 1:
            returning = lax.ppermute(
                grads["sent"], "section", [(i + 1, i) for i in range(sections - 1)]
            )

    ff = w_in.shape[1]
    folds = ff // width
    cores = sum_phases()[0]
    side = phase_bit(cores).reshape(1)
    grads = dict(grads, gu=tied(grads['gu'], *pieces))
    sent = early_weights(kept, grads, 1 - side)
    shares = [phase_swap(value, cores) for value in sent]
    halves = early_weights(kept, grads, tied(side, *sent))
    ffn = Sum(halves[0], shares[0], halve_all=True)
    write = Sum(halves[1], shares[1], dp_first=True)
    groups = [ffn, write]
    after, _ = advance(groups)
    turns = [[2], [0, 3], [1]] if segs == 4 else [[at] for at in range(segs)]
    gqkv = None
    gain_parts = []
    outgoing, incoming = {}, {}
    leaving, arriving = [], []
    for turn in turns:
        which = tied(jnp.concatenate([xor ^ at for at in turn]), *after, *arriving)
        gqkv, out, part = attention_back(kept, grads, which, consts, w, gqkv)
        gain_parts.append(part)
        after, (out,) = advance(groups, part, extra=[out])
        arriving, leaving = leaving, []
        for number, at in enumerate(turn):
            outgoing[at] = out[number : number + 1]
            if chunks == 1 and at:
                incoming[at] = swap_pairs(outgoing[at], "section", at)
                leaving.append(incoming[at])

    sent = late_weights(kept, grads, gqkv, gain_parts, tied(1 - side, *after, *arriving))
    after, (sent,) = advance(groups, sent, extra=[sent])
    share = phase_swap(sent, cores)
    mine = tied(side, sent, *after, *leaving)
    late = Sum(late_weights(kept, grads, gqkv, gain_parts, mine), share)

    half = ff // 2

    def paired(number, start, at):
        main = (start, start + width, at, 0, (1 + number) * width)
        other = (start + width, start + 2 * width, at + number, 0, 0)
        return [main, other]

    ffn_regions = [
        [(0, half, 0, 0, number * half)]
        + [
            (half + at * width, half + (at + 1) * width, 1, number * half + at * width, 0)
            for at in range(half // width)
        ]
        for number in range(2)
    ]
    write_regions = [paired(number, 0, 0) for number in range(2)]
    late_regions = [
        paired(number, 0, 0) + [(2 * width, 2 * width + 128, 2 + number, 0, 0)]
        for number in range(2)
    ]
    square, triple = (width, width), (width, 3 * width)
    advance([late])
    advance(groups, late.sent)
    if chunks == 1:
        incoming[0] = tied(outgoing[0], late.sent)
        back = in_rank_order(jnp.concatenate([incoming[at] for at in range(segs)]), place)
    else:
        back = gathered_out(jnp.concatenate([outgoing[at] for at in range(segs)]), chunks)
    (token_grads,) = late.finish(back.astype(F32))
    advance([late])
    advance(groups, late.sent)
    (done,) = late.finish(done)
    advance([late])
    advance([late])
    advance(groups, late.sent)
    advance([late])
    advance([late])
    while ffn.steps or write.steps:
        advance(groups, late.sent)
    if late.steps:
        advance([late])
    advance(groups, late.sent)
    grad_in, grad_out = unpacked(ffn, ffn_regions, [(width, ff), (ff, width)])
    grad_write, grad_wo = unpacked(write, write_regions, [triple, square])
    grad_in, grad_write = late.finish(grad_in, grad_write)
    while late.steps:
        advance([late])
    if late.started is not None:
        late.finish()
    grad_qkv, grad_ao, grad_init, gains = unpacked(
        late, late_regions, [triple, square, (width, 128), (width, 128)], slots, consts["gains"]
    )
    return (
        done[:, None, :seg],
        done[:, None, seg:],
        token_grads[:, None],
        gains[0],
        grad_qkv,
        grad_ao,
        gains[1],
        grad_in,
        grad_out,
        gains[2],
        grad_write,
        grad_wo,
        grad_init,
    )


def solution(mesh):
    local = P("dp", "section")
    return jax.shard_map(
        body,
        mesh=mesh,
        in_specs=(local,) * 3 + (P(),) * 10 + (local,) * 2,
        out_specs=(local,) * 3 + (P(),) * 10,
        check_vma=False,
    )
```

```python
import jax
import jax.numpy as jnp
import numpy as np
from jax import lax
from jax.experimental import pallas as pl
from jax.experimental.pallas import tpu as pltpu
from jax.sharding import PartitionSpec as P

HEADS = 8
HEAD_DIM = 64
EPS = 1e-06
MASKED = -1000000000.0
F32 = jnp.float32
BF16 = jnp.bfloat16
SQRT_2_PI = 0.7978845608028654
CUBIC = 0.044715
VMEM_LIMIT = 60 * 1024 * 1024


def nn(left, right):
    return lax.dot_general(left, right, (((1,), (0,)), ((), ())), preferred_element_type=F32)


def tn(left, right):
    return lax.dot_general(left, right, (((0,), (0,)), ((), ())), preferred_element_type=F32)


def nt(left, right):
    return lax.dot_general(left, right, (((1,), (1,)), ((), ())), preferred_element_type=F32)


def wide(column_tile, width):
    copies = max(1, width // 128)
    if width < 128:
        return column_tile[:, :width]
    return jnp.concatenate([column_tile] * copies, axis=1)


def inverse_rms(values):
    return lax.rsqrt(jnp.mean(values * values, axis=0, keepdims=True) + EPS)


def lane_sums(values):
    total = values[:, :128]
    for at in range(128, values.shape[1], 128):
        total = total + values[:, at : at + 128]
    return total


def head_mask(rows, columns):
    row_head = lax.broadcasted_iota(jnp.int32, (rows, columns), 0) // HEAD_DIM
    column_head = lax.broadcasted_iota(jnp.int32, (rows, columns), 1) // HEAD_DIM
    return row_head == column_head


def spread_slots(values):
    pair = jnp.concatenate([values, values], axis=1)
    return jnp.concatenate([pair] * (HEADS // 2), axis=1)


def fold_slots(values):
    total = lane_sums(values)
    half = total.shape[1] // 2
    return total[:, :half] + total[:, half:]


def norm_back(grad_normed, normed, scale, gain, gain_inverse):
    weighed = grad_normed * normed
    mean = jnp.mean(weighed, axis=0, keepdims=True)
    return scale * (grad_normed * gain - normed * gain_inverse * mean), weighed


def gain_tiles(gains_ref, count=3):
    tiles = []
    for at in range(count):
        row = gains_ref[at : at + 1, :]
        tiles.append(jnp.broadcast_to(row, (128, row.shape[1])).T)
    return tiles


class Sources:
    def __init__(self, arrays, choices):
        self.arrays = arrays
        self.choices = choices

    def start(self, refs, at, place, buffer, sem):
        for condition, parts in self.choices(at, place):

            @pl.when(condition)
            def _():
                top = 0
                for number, index in parts:
                    source = refs[number].at[index]
                    target = buffer.at[pl.ds(top, source.shape[0]), :]
                    pltpu.make_async_copy(source, target, sem).start()
                    top += source.shape[0]

    def wait(self, buffer, sem):
        pltpu.make_async_copy(buffer, buffer, sem).wait()

    def rows_of(self, refs, steps, segment, place, buffer, sems):
        step = pl.program_id(0)
        slot = lax.rem(step, 2)

        @pl.when(step == 0)
        def _():
            self.start(refs, segment(0), place, buffer.at[0], sems.at[0])

        if steps > 1:

            @pl.when(step + 1 < steps)
            def _():
                self.start(refs, segment(step + 1), place, buffer.at[1 - slot], sems.at[1 - slot])

        self.wait(buffer.at[slot], sems.at[slot])
        return buffer.at[slot]


def forward_kernel(
    sources,
    segs,
    place_ref,
    mem0_ref,
    init_ref,
    gains_ref,
    spread_ref,
    fold_ref,
    *refs,
):
    wqkv_ref, wao_ref, win_ref, wout_ref, ww_ref, wwo_ref = refs[:6]
    refs = refs[6:]
    (
        enc_ref,
        a1_ref,
        a1m_ref,
        q_ref,
        kt_ref,
        ktm_ref,
        v_ref,
        vm_ref,
        e_ref,
        em_ref,
        att_ref,
        a2_ref,
        z_ref,
        gp_ref,
        a3_ref,
        a3m_ref,
        qw_ref,
        kwt_ref,
        kwtm_ref,
        vw_ref,
        vwm_ref,
        ew_ref,
        ewm_ref,
        watt_ref,
        stat_ref,
        last_ref,
        carry,
        bias,
        k_nat,
        km_nat,
        vt,
        vtm,
        hidden,
        row_buffer,
        row_sems,
    ) = refs[-35:]
    step = pl.program_id(0)
    rows_ref = sources.rows_of(
        refs[: len(sources.arrays)], segs, lambda s: s, place_ref[0], row_buffer, row_sems
    )
    width = wao_ref.shape[0]
    seg = q_ref.shape[2]
    slots = init_ref.shape[0]
    ff = win_ref.shape[0]

    @pl.when(step == 0)
    def _():
        carry[...] = mem0_ref[...].astype(F32)

    docs = rows_ref[seg : seg + 1, :].astype(F32)
    flag = rows_ref[seg + 1 : seg + 2, :].astype(F32)
    stat_ref[0, 5:6, :] = flag
    mem = jnp.where(flag[:, :slots] > 0.0, init_ref[...].astype(F32).T, carry[...])
    ga, gf, gw = gain_tiles(gains_ref)

    doc_rows = jnp.broadcast_to(docs, (128, seg)).T
    for at in range(0, seg, 128):
        bias[:, at : at + 128] = jnp.where(doc_rows == docs[:, at : at + 128], 0.0, MASKED)

    tokens = rows_ref[:seg, :].astype(F32).T
    r1 = inverse_rms(tokens)
    a1_ref[...] = (tokens * r1 * wide(ga, seg)).astype(BF16)
    rm = inverse_rms(mem)
    a1m_ref[0] = (mem * rm * ga[:, :slots]).astype(BF16)
    stat_ref[0, 0:1, :] = r1
    stat_ref[0, 4:5, :slots] = rm

    a1 = a1_ref[...]
    a1m = a1m_ref[0]
    q_ref[0] = (nn(wqkv_ref[:width, :], a1) * HEAD_DIM**-0.5).astype(BF16)
    kt = nn(wqkv_ref[width : 2 * width, :], a1).astype(BF16)
    kt_ref[0] = kt
    k_nat[...] = kt.T
    vt[...] = nn(wqkv_ref[2 * width :, :], a1).astype(BF16)
    v_ref[0] = vt[...].T
    ktm = nn(wqkv_ref[width : 2 * width, :], a1m).astype(BF16)
    ktm_ref[0] = ktm
    km_nat[...] = ktm.T
    vtm[...] = nn(wqkv_ref[2 * width :, :], a1m).astype(BF16)
    vm_ref[0] = vtm[...].T

    def pair(index, unused):
        lanes = pl.ds(pl.multiple_of(index * 128, 128), 128)
        keys = k_nat[:, lanes]
        mem_keys = km_nat[:, lanes]
        for half in range(2):
            head = index * 2 + half
            rows = pl.ds(pl.multiple_of(head * HEAD_DIM, HEAD_DIM), HEAD_DIM)
            queries = q_ref[0, rows, :]
            blank = jnp.zeros_like(queries)
            queries = jnp.concatenate([queries, blank] if half == 0 else [blank, queries], axis=0)
            scores = nn(keys, queries) + bias[...]
            mem_scores = nn(mem_keys, queries)
            top = jnp.maximum(
                jnp.max(scores, axis=0, keepdims=True), jnp.max(mem_scores, axis=0, keepdims=True)
            )
            raised = jnp.exp(scores - top)
            mem_raised = jnp.exp(mem_scores - top)
            inverse = 1.0 / (
                jnp.sum(raised, axis=0, keepdims=True) + jnp.sum(mem_raised, axis=0, keepdims=True)
            )
            raised = raised.astype(BF16)
            mem_raised = mem_raised.astype(BF16)
            e_ref[0, head] = raised
            em_ref[0, rows, :] = mem_raised
            mixed = nn(vt[rows, :], raised) + nn(vtm[rows, :], mem_raised)
            att_ref[rows, :] = (mixed * inverse).astype(BF16)
            stat_ref[0, pl.ds(8 + head, 1), :] = inverse
        return unused

    lax.fori_loop(0, HEADS // 2, pair, 0, unroll=HEADS // 2)

    h1 = rows_ref[:seg, :].astype(F32).T + nn(wao_ref[...], att_ref[...])
    r2 = inverse_rms(h1)
    stat_ref[0, 1:2, :] = r2
    a2_ref[...] = (h1 * r2 * wide(gf, seg)).astype(BF16)
    hidden[...] = h1
    a2 = a2_ref[...]
    for at in range(0, ff, 512):
        upper = nn(win_ref[at : at + 512, :], a2)
        square = upper * upper
        bent = jnp.tanh(upper * (SQRT_2_PI + (SQRT_2_PI * CUBIC) * square))
        cdf = 0.5 + 0.5 * bent
        z_ref[at : at + 512, :] = (upper * cdf).astype(BF16)
        slope = (0.5 * SQRT_2_PI) + (1.5 * SQRT_2_PI * CUBIC) * square
        gp_ref[0, at : at + 512, :] = (cdf + upper * (1.0 - bent * bent) * slope).astype(BF16)
    enc = hidden[...] + tn(wout_ref[...], z_ref[...])
    enc_ref[0, :seg, :] = enc.T.astype(BF16)
    r3 = inverse_rms(enc)
    stat_ref[0, 2:3, :] = r3
    a3_ref[...] = (enc * r3 * wide(gw, seg)).astype(BF16)
    a3m_ref[0] = (mem * rm * gw[:, :slots]).astype(BF16)
    a3 = a3_ref[...]
    a3m = a3m_ref[0]

    kwt = nn(ww_ref[width : 2 * width, :], a3).astype(BF16)
    kwt_ref[0] = kwt
    kw = kwt.T
    vwt = nn(ww_ref[2 * width :, :], a3).astype(BF16)
    vw_ref[0] = vwt.T
    kwtm = nn(ww_ref[width : 2 * width, :], a3m).astype(BF16)
    kwtm_ref[0] = kwtm
    vwtm = nn(ww_ref[2 * width :, :], a3m).astype(BF16)
    vwm_ref[0] = vwtm.T
    qwt = (nn(ww_ref[:width, :], a3m) * HEAD_DIM**-0.5).astype(BF16)
    own = head_mask(width, HEADS * slots)
    qw = jnp.where(own, nn(qwt, spread_ref[...]), 0.0).astype(BF16)
    qw_ref[0] = qw
    scores = nn(kw, qw)
    mem_scores = nn(kwtm.T, qw)
    slot_row = lax.broadcasted_iota(jnp.int32, mem_scores.shape, 0)
    slot_col = lax.broadcasted_iota(jnp.int32, mem_scores.shape, 1) % slots
    mem_scores = jnp.where(slot_row == slot_col, mem_scores, MASKED)
    top = jnp.maximum(
        jnp.max(scores, axis=0, keepdims=True), jnp.max(mem_scores, axis=0, keepdims=True)
    )
    raised = jnp.exp(scores - top)
    mem_raised = jnp.exp(mem_scores - top)
    inverse = 1.0 / (
        jnp.sum(raised, axis=0, keepdims=True) + jnp.sum(mem_raised, axis=0, keepdims=True)
    )
    stat_ref[0, 3:4, :] = inverse
    raised = raised.astype(BF16)
    mem_raised = mem_raised.astype(BF16)
    ew_ref[0] = raised
    ewm_ref[0] = mem_raised
    mixed = (nn(vwt, raised) + nn(vwtm, mem_raised)) * inverse
    watt = fold_slots(jnp.where(own, mixed, 0.0)).astype(BF16)
    watt_ref[0] = watt
    new_mem = (mem + nn(wwo_ref[...], watt)).astype(BF16).astype(F32)
    carry[...] = new_mem
    enc_ref[0, seg:, :] = new_mem.T.astype(BF16)
    last_ref[...] = new_mem.astype(BF16)


def chain_kernel(
    sources,
    segs,
    place_ref,
    carry0_ref,
    weights_gains_ref,
    wwo_ref,
    ww_ref,
    wout_ref,
    win_ref,
    wao_ref,
    wqkv_ref,
    a1m_ref,
    q_ref,
    vm_ref,
    em_ref,
    att_ref,
    a2_ref,
    gp_ref,
    a3_ref,
    a3m_ref,
    qw_ref,
    kwt_ref,
    kwtm_ref,
    vw_ref,
    vwm_ref,
    ew_ref,
    ewm_ref,
    stat_ref,
    *refs,
):
    source_refs, refs = refs[: len(sources.arrays)], refs[len(sources.arrays) :]
    bm_ref, gwkv_ref, gwm_ref, bf_ref, gu_ref, ba_ref, gh_ref, do_ref, dd_ref, dsm_ref = refs[:10]
    gkvm_ref, init_ref, gains_ref, sent_ref, carry, grad_buffer, grad_sems = refs[10:]
    gout_ref = sources.rows_of(
        source_refs, segs, lambda s: segs - 1 - s, place_ref[0], grad_buffer, grad_sems
    )
    step = pl.program_id(0)
    width = wao_ref.shape[0]
    ff = wout_ref.shape[0]
    seg = q_ref.shape[2]
    slots = a1m_ref.shape[2]
    reset = stat_ref[0, 5:6, :slots] > 0.0

    @pl.when(step == 0)
    def _():
        carry[...] = carry0_ref[...].astype(F32)
        init_ref[...] = jnp.zeros_like(init_ref)
        gains_ref[...] = jnp.zeros_like(gains_ref)

    ga, gf, gw = gain_tiles(weights_gains_ref)
    gai, gfi, gwi = 1.0 / ga, 1.0 / gf, 1.0 / gw
    own = head_mask(width, HEADS * slots)
    rm = stat_ref[0, 4:5, :slots]

    grad_mem = gout_ref[seg:, :].astype(F32).T + carry[...]
    branch_mem = grad_mem.astype(BF16)
    bm_ref[0] = branch_mem
    grad_watt = nn(wwo_ref[...], branch_mem).astype(BF16)
    inverse = stat_ref[0, 3:4, :]
    scaled = (jnp.where(own, spread_slots(grad_watt.astype(F32)), 0.0) * inverse).astype(BF16)
    raised = ew_ref[0].astype(F32)
    mem_raised = ewm_ref[0].astype(F32)
    grad_probs = nn(vw_ref[0], scaled)
    mem_grad_probs = nn(vwm_ref[0], scaled)
    dots = (
        jnp.sum(raised * grad_probs, axis=0, keepdims=True)
        + jnp.sum(mem_raised * mem_grad_probs, axis=0, keepdims=True)
    ) * inverse
    grad_scores = (raised * (grad_probs - dots)).astype(BF16)
    mem_grad_scores = (mem_raised * (mem_grad_probs - dots)).astype(BF16)
    gwkv_ref[:width, :] = nt(qw_ref[0], grad_scores).astype(BF16)
    gwkv_ref[width:, :] = nt(scaled, ew_ref[0]).astype(BF16)
    grad_q = (nn(kwt_ref[0], grad_scores) + nn(kwtm_ref[0], mem_grad_scores)) * HEAD_DIM**-0.5
    gwm_ref[0, :width, :] = fold_slots(jnp.where(own, grad_q, 0.0)).astype(BF16)
    gwm_ref[0, width : 2 * width, :] = nt(qw_ref[0], mem_grad_scores).astype(BF16)
    gwm_ref[0, 2 * width :, :] = nt(scaled, ewm_ref[0]).astype(BF16)

    grad_a3 = nn(ww_ref[:, width:], gwkv_ref[...])
    grad_a3m = nn(ww_ref[...], gwm_ref[0])
    part, weighed = norm_back(
        grad_a3, a3_ref[...].astype(F32), stat_ref[0, 2:3, :], wide(gw, seg), wide(gwi, seg)
    )
    mem_part, mem_weighed = norm_back(
        grad_a3m, a3m_ref[0].astype(F32), rm, gw[:, :slots], gwi[:, :slots]
    )
    gains_ref[2] += lane_sums(weighed)
    gains_ref[2, :, :slots] += mem_weighed
    grad_mem_in = grad_mem + mem_part
    gh_ref[0] = gout_ref[:seg, :].astype(F32).T + part

    bf_ref[...] = gh_ref[0].astype(BF16)
    branch = bf_ref[...]
    for at in range(0, ff, 512):
        grad_z = nn(wout_ref[at : at + 512, :], branch)
        gu_ref[at : at + 512, :] = (grad_z * gp_ref[0, at : at + 512, :].astype(F32)).astype(BF16)
    grad_a2 = nn(win_ref[...], gu_ref[...])
    part, weighed = norm_back(
        grad_a2, a2_ref[...].astype(F32), stat_ref[0, 1:2, :], wide(gf, seg), wide(gfi, seg)
    )
    gains_ref[1] += lane_sums(weighed)
    gh_ref[0] += part

    ba_ref[...] = gh_ref[0].astype(BF16)
    grad_att = nn(wao_ref[...], ba_ref[...]).astype(BF16)
    products = grad_att.astype(F32) * att_ref[...].astype(F32)
    rows = []
    dots = []
    for head in range(HEADS):
        span = slice(head * HEAD_DIM, (head + 1) * HEAD_DIM)
        inverse = stat_ref[0, 8 + head : 9 + head, :]
        dots.append(jnp.sum(products[span, :], axis=0, keepdims=True) * inverse)
        rows.append((grad_att[span, :].astype(F32) * inverse).astype(BF16))
    scaled = jnp.concatenate(rows, axis=0)
    do_ref[0] = scaled
    dd_ref[0] = jnp.concatenate(dots, axis=0)
    mem_values = jnp.concatenate([vm_ref[0].astype(F32)] * HEADS, axis=0)
    mem_values = jnp.where(own, mem_values, 0.0).astype(BF16)
    grad_probs = nn(mem_values, scaled)
    parts = []
    for head in range(HEADS):
        span = slice(head * slots, (head + 1) * slots)
        parts.append(
            (em_ref[0, span, :].astype(F32) * (grad_probs[span, :] - dots[head])).astype(BF16)
        )
    grad_scores = jnp.concatenate(parts, axis=0)
    dsm_ref[0] = grad_scores
    grad_k = jnp.where(own, nt(q_ref[0], grad_scores), 0.0)
    grad_v = jnp.where(own, nt(scaled, em_ref[0]), 0.0)
    gkvm_ref[0, :width, :] = fold_slots(grad_k).astype(BF16)
    gkvm_ref[0, width:, :] = fold_slots(grad_v).astype(BF16)
    grad_a1m = nn(wqkv_ref[:, width:], gkvm_ref[0])
    mem_part, mem_weighed = norm_back(
        grad_a1m, a1m_ref[0].astype(F32), rm, ga[:, :slots], gai[:, :slots]
    )
    gains_ref[0, :, :slots] += mem_weighed
    grad_mem_in = grad_mem_in + mem_part
    init_ref[...] += jnp.where(reset, grad_mem_in, 0.0)
    carry[...] = jnp.where(reset, 0.0, grad_mem_in).astype(BF16).astype(F32)
    sent_ref[...] = carry[...].astype(BF16)


def attention_kernel(
    alone,
    place_ref,
    do_ref,
    dd_ref,
    dsm_ref,
    q_ref,
    kt_ref,
    ktm_ref,
    v_ref,
    e_ref,
    stat_ref,
    gains_ref,
    gh_ref,
    a1_ref,
    wqkv_ref,
    *refs,
):
    step = pl.program_id(0)
    copies = []
    if alone:
        gqkv_ref, out_ref, gain_ref, *buffers, sems = refs[-7:]
        place = place_ref[0]
        tokens = gh_ref.shape[2]
        lanes = pl.ds(pl.multiple_of(place * tokens, tokens), tokens)
        sources = [gh_ref.at[pl.ds(place, 1)], a1_ref.at[:, lanes], wqkv_ref]
        for at, (source, target) in enumerate(zip(sources, buffers)):
            copies.append(fetch(source, target, sems.at[at]))
        gh_ref, a1_ref, wqkv_ref = buffers
    else:
        gqkv_ref, out_ref, gain_ref = refs[-3:]
    width = wqkv_ref.shape[0]
    seg = q_ref.shape[2]
    for head in range(HEADS):
        span = slice(head * HEAD_DIM, (head + 1) * HEAD_DIM)
        key_span = slice(width + head * HEAD_DIM, width + (head + 1) * HEAD_DIM)
        value_span = slice(2 * width + head * HEAD_DIM, 2 * width + (head + 1) * HEAD_DIM)
        grads = do_ref[0, span, :]
        blank = jnp.zeros_like(grads)
        padded = jnp.concatenate([grads, blank] if head % 2 == 0 else [blank, grads], axis=0)
        dots = dd_ref[0, head : head + 1, :]
        lanes = slice(head // 2 * 128, head // 2 * 128 + 128)
        grad_probs = nn(v_ref[0, :, lanes], padded)
        inner = (e_ref[0, head].astype(F32) * (grad_probs - dots)).astype(BF16)
        grad_q = nn(kt_ref[0, span, :], inner) + nn(ktm_ref[0, span, :], dsm_ref[0, span, :])
        gqkv_ref[span, :] = (grad_q * HEAD_DIM**-0.5).astype(BF16)
        gqkv_ref[key_span, :] = nt(q_ref[0, span, :], inner).astype(BF16)
        gqkv_ref[value_span, :] = nt(grads, e_ref[0, head]).astype(BF16)

    for copy in copies:
        copy.wait()
    grad_a1 = nn(wqkv_ref[...], gqkv_ref[...])
    (ga,) = gain_tiles(gains_ref, 1)
    part, weighed = norm_back(
        grad_a1,
        a1_ref[...].astype(F32),
        stat_ref[0, 0:1, :],
        wide(ga, seg),
        wide(1.0 / ga, seg),
    )
    gain_ref[...] = jnp.where(step == 0, 0.0, gain_ref[...]) + lane_sums(weighed)
    out_ref[0] = (gh_ref[0] + part).T.astype(BF16)


def whole(array):
    zeros = (0,) * array.ndim
    return pl.BlockSpec(array.shape, lambda *unused: zeros, pipeline_mode=pl.Buffered(1))


def params():
    return pltpu.CompilerParams(dimension_semantics=("arbitrary",), vmem_limit_bytes=VMEM_LIMIT)


def cost(microseconds):
    return pl.CostEstimate(
        flops=int(microseconds * 1e9), bytes_accessed=1 << 20, transcendentals=0
    )


def forward_chain(sources, place, mem0, consts, w):
    segs = consts["segs"]
    seg = consts["seg"]
    width, slots = mem0.shape
    ff = w["in_t"].shape[0]

    def flat(height):
        return (
            jax.ShapeDtypeStruct((height, segs * seg), BF16),
            pl.BlockSpec((height, seg), lambda s, f: (0, s)),
        )

    def stack(*shape, dtype=BF16):
        tail = (0,) * len(shape)
        return (
            jax.ShapeDtypeStruct((segs,) + shape, dtype),
            pl.BlockSpec((1,) + shape, lambda s, f: (s,) + tail),
        )

    outs = dict(
        enc=stack(seg + slots, width),
        a1=flat(width),
        a1m=stack(width, slots),
        q=stack(width, seg),
        kt=stack(width, seg),
        ktm=stack(width, slots),
        v=stack(seg, width),
        vm=stack(slots, width),
        e=stack(HEADS, seg, seg),
        em=stack(HEADS * slots, seg),
        att=flat(width),
        a2=flat(width),
        z=flat(ff),
        gp=stack(ff, seg),
        a3=flat(width),
        a3m=stack(width, slots),
        qw=stack(width, HEADS * slots),
        kwt=stack(width, seg),
        kwtm=stack(width, slots),
        vw=stack(seg, width),
        vwm=stack(slots, width),
        ew=stack(seg, HEADS * slots),
        ewm=stack(slots, HEADS * slots),
        watt=stack(width, slots),
        stat=stack(16, seg, dtype=F32),
        last=(
            jax.ShapeDtypeStruct((width, slots), BF16),
            pl.BlockSpec((width, slots), lambda s, f: (0, 0)),
        ),
    )
    fixed = [
        mem0,
        consts["init"],
        consts["gains"],
        consts["spread"],
        consts["fold"],
    ]
    weights = [w[name] for name in ("qkv_t", "ao_t", "in_t", "out", "write_t", "wo_t")]
    results = pl.pallas_call(
        lambda *refs: forward_kernel(sources, segs, *refs),
        grid_spec=pltpu.PrefetchScalarGridSpec(
            num_scalar_prefetch=1,
            grid=(segs,),
            in_specs=[whole(a) for a in fixed + weights]
            + [pl.BlockSpec(memory_space=pl.ANY)] * len(sources.arrays),
            out_specs=[spec for _, spec in outs.values()],
            scratch_shapes=[
                pltpu.VMEM((width, slots), F32),
                pltpu.VMEM((seg, seg), F32),
                pltpu.VMEM((seg, width), BF16),
                pltpu.VMEM((slots, width), BF16),
                pltpu.VMEM((width, seg), BF16),
                pltpu.VMEM((width, slots), BF16),
                pltpu.VMEM((width, seg), F32),
                pltpu.VMEM((2, seg + 16, width), BF16),
                pltpu.SemaphoreType.DMA((2,)),
            ],
        ),
        out_shape=[shape for shape, _ in outs.values()],
        compiler_params=params(),
        cost_estimate=cost(15 * segs),
        name="forward_chain",
    )(place, *fixed, *weights, *sources.arrays)
    return dict(zip(outs, results))


def backward_chain(kept, sources, place, carry0, consts, w):
    segs = consts["segs"]
    width, slots = kept["a1m"].shape[1:]
    seg = kept["q"].shape[2]
    ff = kept["gp"].shape[1]
    last = segs - 1

    def flat(height):
        return (
            jax.ShapeDtypeStruct((height, segs * seg), BF16),
            pl.BlockSpec((height, seg), lambda s, f: (0, last - s)),
        )

    def stack(*shape, dtype=BF16):
        tail = (0,) * len(shape)
        return (
            jax.ShapeDtypeStruct((segs,) + shape, dtype),
            pl.BlockSpec((1,) + shape, lambda s, f: (last - s,) + tail),
        )

    def single(*shape, dtype=F32):
        tail = (0,) * len(shape)
        return (jax.ShapeDtypeStruct(shape, dtype), pl.BlockSpec(shape, lambda s, f: tail))

    outs = dict(
        bm=stack(width, slots),
        gwkv=flat(2 * width),
        gwm=stack(3 * width, slots),
        bf=flat(width),
        gu=flat(ff),
        ba=flat(width),
        gh=stack(width, seg, dtype=F32),
        do=stack(width, seg),
        dd=stack(HEADS, seg, dtype=F32),
        dsm=stack(HEADS * slots, seg),
        gkvm=stack(2 * width, slots),
        init=single(width, slots),
        gains=single(3, width, 128),
        sent=single(width, slots, dtype=BF16),
    )
    fixed = [
        carry0,
        consts["gains"],
    ]
    weights = [w[name] for name in ("wo", "write", "out", "in", "ao", "qkv")]
    blocked = ["a1m", "q", "vm", "em", "att", "a2", "gp", "a3", "a3m", "qw"]
    blocked += ["kwt", "kwtm", "vw", "vwm", "ew", "ewm", "stat"]

    def spec_of(array):
        if array.ndim == 2:
            return pl.BlockSpec((array.shape[0], seg), lambda s, f: (0, last - s))
        tail = (0,) * (array.ndim - 1)
        return pl.BlockSpec((1,) + array.shape[1:], lambda s, f: (last - s,) + tail)

    results = pl.pallas_call(
        lambda *refs: chain_kernel(sources, segs, *refs),
        grid_spec=pltpu.PrefetchScalarGridSpec(
            num_scalar_prefetch=1,
            grid=(segs,),
            in_specs=[whole(a) for a in fixed + weights]
            + [spec_of(kept[name]) for name in blocked]
            + [pl.BlockSpec(memory_space=pl.ANY)] * len(sources.arrays),
            out_specs=[spec for _, spec in outs.values()],
            scratch_shapes=[
                pltpu.VMEM((width, slots), F32),
                pltpu.VMEM((2, seg + slots, width), BF16),
                pltpu.SemaphoreType.DMA((2,)),
            ],
        ),
        out_shape=[shape for shape, _ in outs.values()],
        compiler_params=params(),
        cost_estimate=cost(11 * segs),
        name="backward_chain",
    )(place, *fixed, *weights, *[kept[name] for name in blocked], *sources.arrays)
    return dict(zip(outs, results))


def attention_back(kept, grads, which, consts, w, before):
    segs, width, seg = kept["q"].shape
    count = which.shape[0]

    def by_seg(array):
        if array.ndim == 2:
            return pl.BlockSpec((array.shape[0], seg), lambda s, f: (0, f[s]))
        tail = (0,) * (array.ndim - 1)
        return pl.BlockSpec((1,) + array.shape[1:], lambda s, f: (f[s],) + tail)

    alone = count == 1
    blocked = [grads[name] for name in ("do", "dd", "dsm")]
    blocked += [kept[name] for name in ("q", "kt", "ktm", "v", "e", "stat")]
    inputs = [(array, by_seg(array)) for array in blocked]
    inputs.append((consts["gains"], whole(consts["gains"])))
    last = [grads["gh"], kept["a1"], w["qkv"]]
    scratch = []
    if alone:
        inputs += [(array, pl.BlockSpec(memory_space=pl.ANY)) for array in last]
        scratch = [
            pltpu.VMEM((1, width, seg), F32),
            pltpu.VMEM((width, seg), BF16),
            pltpu.VMEM(w["qkv"].shape, BF16),
            pltpu.SemaphoreType.DMA((3,)),
        ]
    else:
        inputs += [(array, by_seg(array)) for array in last[:2]] + [(last[2], whole(last[2]))]
    passed = [] if before is None else [before]
    return pl.pallas_call(
        lambda *refs: attention_kernel(alone, *refs),
        grid_spec=pltpu.PrefetchScalarGridSpec(
            num_scalar_prefetch=1,
            grid=(count,),
            in_specs=[spec for _, spec in inputs]
            + [pl.BlockSpec(memory_space=pl.ANY)] * len(passed),
            out_specs=[
                pl.BlockSpec((3 * width, seg), lambda s, f: (0, f[s])),
                pl.BlockSpec((1, seg, width), lambda s, f: (s, 0, 0)),
                pl.BlockSpec((width, 128), lambda s, f: (0, 0)),
            ],
            scratch_shapes=scratch,
        ),
        out_shape=[
            jax.ShapeDtypeStruct((3 * width, segs * seg), BF16),
            jax.ShapeDtypeStruct((count, seg, width), BF16),
            jax.ShapeDtypeStruct((width, 128), F32),
        ],
        input_output_aliases={1 + len(inputs): 0} if passed else {},
        compiler_params=params(),
        cost_estimate=cost(10 * count),
        name="attention_back",
    )(which, *[array for array, _ in inputs], *passed)


def swap_pairs(value, axis, mask):
    size = lax.axis_size(axis)
    return lax.ppermute(value, axis, [(i, i ^ mask) for i in range(size)])


def sum_phases(dp_first=False):
    section = [("section", 1 << at) for at in range(lax.axis_size("section").bit_length() - 1)]
    dp = [("dp", 1 << at) for at in range(lax.axis_size("dp").bit_length() - 1)]
    phases = [(step, step) for step in section[:1]]
    crossed = []
    if len(section) > 1 and dp:
        crossed = [(dp[0], section[1]), (section[1], dp[0])]
        section, dp = section[2:], dp[1:]
    else:
        section = section[1:]
    straight = [(step, step) for step in dp + section]
    return phases + (straight + crossed if dp_first else crossed + straight)


def phase_swap(value, phase):
    sections, dps = lax.axis_size("section"), lax.axis_size("dp")
    route = []
    for section in range(sections):
        axis, mask = phase[section % 2]
        for dp in range(dps):
            to = ((section ^ mask) * dps + dp) if axis == "section" else (section * dps + (dp ^ mask))
            route.append((section * dps + dp, to))
    return lax.ppermute(value, ("section", "dp"), route)


def phase_bit(phase):
    bits = [(lax.axis_index(axis) // mask) % 2 for axis, mask in phase]
    return jnp.where(lax.axis_index("section") % 2 == 0, bits[0], bits[1])


def half_of(value, side):
    half = value.shape[0] // 2
    return lax.dynamic_slice_in_dim(value, side * half, half, 0)


def fetch(source, target, sem):
    copy = pltpu.make_async_copy(source, target, sem)
    copy.start()
    return copy


def slot_sum(left, right):
    join = lambda ref: jnp.concatenate([ref[at] for at in range(ref.shape[0])], axis=1)
    return nt(join(left), join(right))


def early_weights_kernel(
    side_ref, a2_ref, gu_ref, bf_ref, z_ref, a3_ref, gwkv_ref, a3m_ref, gwm_ref, watt_ref, bm_ref, *refs
):
    ffn_ref, write_ref, a2, gu, z, bf, a3, gw, a3m, gwm, left, right, staged, in_sems, out_sems = refs
    side = side_ref[0]
    width = a2.shape[0]
    folds = gu.shape[0]
    base = side * (folds * width)
    loads = []

    def load(source, target):
        loads.append(fetch(source, target, in_sems.at[len(loads)]))

    def wait(count):
        for _ in range(count):
            loads[wait.done].wait()
            wait.done += 1

    wait.done = 0
    load(a2_ref, a2)
    for at in range(folds):
        rows = pl.ds(pl.multiple_of(base + at * width, width), width)
        load(gu_ref.at[rows, :], gu.at[at])
    load(bf_ref, bf)
    for at in range(folds):
        rows = pl.ds(pl.multiple_of(base + at * width, width), width)
        load(z_ref.at[rows, :], z.at[at])
    load(a3_ref, a3)
    load(gwkv_ref.at[pl.ds(pl.multiple_of(side * width, width), width), :], gw)
    load(a3m_ref, a3m)
    load(gwm_ref.at[:, pl.ds(pl.multiple_of((1 + side) * width, width), width), :], gwm)
    last = in_sems.at[len(loads)]

    @pl.when(side == 0)
    def _():
        pltpu.make_async_copy(a3m_ref, left, last).start()
        pltpu.make_async_copy(gwm_ref.at[:, pl.ds(0, width), :], right, last).start()

    @pl.when(side == 1)
    def _():
        pltpu.make_async_copy(watt_ref, left, last).start()
        pltpu.make_async_copy(bm_ref, right, last).start()

    stores = []

    def put(tile, value):
        columns = slice(tile * width, (tile + 1) * width)
        staged[:, columns] = value.astype(BF16)
        out, first = (ffn_ref, 0) if tile < 2 * folds else (write_ref, 2 * folds)
        target = out.at[:, pl.ds((tile - first) * width, width)]
        stores.append(fetch(staged.at[:, columns], target, out_sems.at[tile]))

    wait(1)
    for at in range(folds):
        wait(1)
        put(at, nt(a2[...], gu[at]))
    wait(1)
    for at in range(folds):
        wait(1)
        put(folds + at, nt(z[at], bf[...]))
    wait(4)
    put(2 * folds, nt(a3[...], gw[...]) + slot_sum(a3m, gwm))
    pltpu.make_async_copy(watt_ref, left, last).wait()
    pltpu.make_async_copy(bm_ref, right, last).wait()
    put(2 * folds + 1, slot_sum(left, right))
    for store in stores:
        store.wait()


def early_weights(kept, grads, side):
    width, tokens = kept["a2"].shape
    folds = kept["z"].shape[0] // 2 // width
    inputs = [kept["a2"], grads["gu"], grads["bf"], kept["z"], kept["a3"], grads["gwkv"]]
    inputs += [kept["a3m"], grads["gwm"], kept["watt"], grads["bm"]]
    anywhere = pl.BlockSpec(memory_space=pl.ANY)
    full = pltpu.VMEM((width, tokens), BF16)
    several = pltpu.VMEM((folds, width, tokens), BF16)
    slots = pltpu.VMEM(kept["a3m"].shape, BF16)
    out = jax.ShapeDtypeStruct((width, (2 * folds + 2) * width), BF16)
    return pl.pallas_call(
        early_weights_kernel,
        grid_spec=pltpu.PrefetchScalarGridSpec(
            num_scalar_prefetch=1,
            grid=(1,),
            in_specs=[anywhere] * len(inputs),
            out_specs=[anywhere] * 2,
            scratch_shapes=[full, several, several, full, full, full]
            + [slots] * 4
            + [
                pltpu.VMEM(out.shape, BF16),
                pltpu.SemaphoreType.DMA((7 + 2 * folds,)),
                pltpu.SemaphoreType.DMA((2 * folds + 2,)),
            ],
        ),
        out_shape=[
            jax.ShapeDtypeStruct((width, 2 * folds * width), BF16),
            jax.ShapeDtypeStruct((width, 2 * width), BF16),
        ],
        compiler_params=params(),
        cost_estimate=cost(9),
        name="early_weights",
    )(side, *inputs)


def late_weights_kernel(count, side_ref, a1_ref, gqkv_ref, att_ref, ba_ref, a1m_ref, gkvm_ref, *refs):
    init_ref, gains_ref, refs = refs[0], refs[1], refs[2:]
    part_refs, refs = refs[:count], refs[count:]
    out_ref, a1, main, left, right, a1m, gkvm, init, gains, parts, staged, in_sems, out_sems = refs
    side = side_ref[0]
    width = a1.shape[0]
    slots = init.shape[1]
    rows = pl.ds(pl.multiple_of((1 + side) * width, width), width)
    kv_rows = pl.ds(pl.multiple_of(side * width, width), width)
    loads = [
        fetch(a1_ref, a1, in_sems.at[0]),
        fetch(gqkv_ref.at[rows, :], main, in_sems.at[1]),
        fetch(a1m_ref, a1m, in_sems.at[2]),
        fetch(gkvm_ref.at[:, kv_rows, :], gkvm, in_sems.at[3]),
    ]

    @pl.when(side == 0)
    def _():
        pltpu.make_async_copy(a1_ref, left, in_sems.at[4]).start()
        pltpu.make_async_copy(gqkv_ref.at[pl.ds(0, width), :], right, in_sems.at[5]).start()

    @pl.when(side == 1)
    def _():
        pltpu.make_async_copy(att_ref, left, in_sems.at[4]).start()
        pltpu.make_async_copy(ba_ref, right, in_sems.at[5]).start()

    others = [fetch(init_ref, init, in_sems.at[6]), fetch(gains_ref, gains, in_sems.at[7])]
    others += [fetch(ref, parts.at[at], in_sems.at[8 + at]) for at, ref in enumerate(part_refs)]
    stores = []

    def put(columns, value):
        staged[:, columns] = value.astype(BF16)
        stores.append(fetch(staged.at[:, columns], out_ref.at[:, columns], out_sems.at[len(stores)]))

    for load in loads:
        load.wait()
    put(slice(0, width), nt(a1[...], main[...]) + slot_sum(a1m, gkvm))
    pltpu.make_async_copy(att_ref, left, in_sems.at[4]).wait()
    pltpu.make_async_copy(ba_ref, right, in_sems.at[5]).wait()
    put(slice(width, 2 * width), nt(left[...], right[...]))
    for load in others:
        load.wait()
    columns = [gains[0], gains[1], gains[2]]
    for at in range(count):
        columns[0] = columns[0] + parts[at]
    lane = lax.broadcasted_iota(jnp.int32, init.shape, 1)
    extras = jnp.zeros(init.shape, F32)
    for at, column in enumerate(columns):
        extras = jnp.where(lane == at, jnp.sum(column, axis=1, keepdims=True), extras)
    extras = jnp.where(side == 0, init[...], extras)
    extras = jnp.concatenate([extras, jnp.zeros_like(extras)], axis=1)
    put(slice(2 * width, 2 * width + 2 * slots), extras)
    for store in stores:
        store.wait()


def late_weights(kept, grads, gqkv, gain_parts, side):
    width, tokens = kept["a1"].shape
    count = len(gain_parts)
    inputs = [kept["a1"], gqkv, kept["att"], grads["ba"], kept["a1m"], grads["gkvm"]]
    inputs += [grads["init"], grads["gains"]] + list(gain_parts)
    slots = grads["init"].shape[1]
    anywhere = pl.BlockSpec(memory_space=pl.ANY)
    full = pltpu.VMEM((width, tokens), BF16)
    small = pltpu.VMEM(kept["a1m"].shape, BF16)
    out = jax.ShapeDtypeStruct((width, 2 * width + 2 * slots), BF16)
    return pl.pallas_call(
        lambda *refs: late_weights_kernel(count, *refs),
        grid_spec=pltpu.PrefetchScalarGridSpec(
            num_scalar_prefetch=1,
            grid=(1,),
            in_specs=[anywhere] * len(inputs),
            out_specs=anywhere,
            scratch_shapes=[full] * 4
            + [small] * 2
            + [
                pltpu.VMEM(grads["init"].shape, F32),
                pltpu.VMEM(grads["gains"].shape, F32),
                pltpu.VMEM((count,) + gain_parts[0].shape, F32),
                pltpu.VMEM(out.shape, BF16),
                pltpu.SemaphoreType.DMA((8 + count,)),
                pltpu.SemaphoreType.DMA((3,)),
            ],
        ),
        out_shape=out,
        compiler_params=params(),
        cost_estimate=cost(4),
        name="late_weights",
    )(side, *inputs)


class Sum:
    def __init__(self, value, share, halve_all=False, dp_first=False):
        self.phases = sum_phases(dp_first)
        inner = self.phases[1:]
        self.value = value
        self.share = share
        halvings = 0
        most = len(inner) - (0 if halve_all else 1)
        while halvings < most and value.shape[0] >> (halvings + 1) >= 16:
            halvings += 1
        self.halved = inner[:halvings]
        self.steps = [("halve", phase) for phase in self.halved]
        self.steps += [("add", phase) for phase in inner[halvings:]]
        self.steps += [("double", phase) for phase in reversed(self.halved)]
        self.steps += [("last", self.phases[0])]
        self.started = None

    def prepare(self):
        kind, phase = self.steps.pop(0)
        if kind == "halve":
            bit = phase_bit(phase)
            value = self.value
            self.sent, self.value = half_of(value, 1 - bit), half_of(value, bit)
            if self.share is not None:
                self.sent = self.sent + half_of(self.share, 1 - bit)
                self.value = self.value + half_of(self.share, bit)
        else:
            if self.share is not None:
                self.value = self.value + self.share
            self.sent = self.value
        self.share = None
        self.ready = (kind, phase)

    def launch(self):
        kind, phase = self.ready
        if kind == "last" and isinstance(self.sent, tuple):
            self.started = (kind, tuple(phase_swap(piece, phase) for piece in self.sent))
        else:
            self.started = (kind, phase_swap(self.sent, phase))

    def finish(self, *after):
        kind, other = self.started
        self.started = None
        other, after = lax.optimization_barrier((other, after))
        if kind in ("halve", "add"):
            self.value = self.value + other
        elif kind == "double" and len(self.steps) == 1:
            self.value = (self.value, other)
        elif kind == "double":
            self.value = jnp.concatenate([self.value, other], axis=0)
        elif isinstance(other, tuple):
            self.value = (self.value, other)
        else:
            self.value = ((self.value,), (other,))
        return list(after)

    def places(self):
        own = sum(phase_bit(phase) << at for at, phase in enumerate(reversed(self.halved)))
        swapped = [(late, early) for early, late in self.halved]
        other = sum(phase_bit(phase) << at for at, phase in enumerate(reversed(swapped)))
        numbers = jnp.stack([phase_bit(self.phases[0]), jnp.int32(own), jnp.int32(other)])
        return numbers.astype(jnp.int32), 1 << len(self.halved)


def advance(totals, *after, extra=()):
    going = []
    for total in totals:
        if total.started is not None:
            total.finish(*after)
        if total.steps:
            total.prepare()
            going.append(total)
    joined, extra = lax.optimization_barrier(([total.sent for total in going], list(extra)))
    for total, sent in zip(going, joined):
        if total.value is total.sent:
            total.value = sent
        total.sent = sent
        total.launch()
    return joined, extra


def unpack_kernel(count, parts, regions, kept, place_ref, *refs):
    own_refs, other_refs, refs = refs[:parts], refs[parts : 2 * parts], refs[2 * parts :]
    gains_ref = None
    if kept:
        gains_ref, refs = refs[0], refs[1:]
    outs = len(refs) // 2
    out_refs, staged, sems = refs[:outs], refs[outs : 2 * outs], refs[2 * outs]
    each = count // parts
    rows = own_refs[0].shape[0] // each
    height = rows * count

    def take(refs, side, number, sem):
        copies = []
        for start, stop, at, top, left in regions[side]:
            for block in range(count):
                target = pl.multiple_of(top + (block ^ place_ref[number]) * rows, rows)
                inner = (block % each) * rows
                value = refs[block // each][inner : inner + rows, start:stop].astype(F32)
                staged[at][pl.ds(target, rows), left : left + stop - start] = value
            if at >= outs - kept:
                continue
            slab = (pl.ds(top, height), pl.ds(left, stop - start))
            copies.append((staged[at].at[slab], out_refs[at].at[slab], sems.at[sem + len(copies)]))
            pltpu.make_async_copy(*copies[-1]).start()
        return copies

    for side in range(2):

        @pl.when(place_ref[0] == side)
        def _():
            copies = take(own_refs, side, 1, 0)
            copies += take(other_refs, 1 - side, 2, len(copies))
            for copy in copies:
                pltpu.make_async_copy(*copy).wait()

    if kept:
        init_ref, total_ref = out_refs[outs - 2 :]
        init_ref[...] = staged[outs - 2][...].T[: init_ref.shape[0], :]
        total_ref[...] = staged[outs - 1][...].T[: total_ref.shape[0], :] / gains_ref[...]


def unpacked(total, regions, shapes, slots=0, gains=None):
    own, other = total.value
    places, count = total.places()
    parts = len(own)
    kept = 0 if gains is None else 2
    vmem = pl.BlockSpec(memory_space=pltpu.VMEM)
    outs = [jax.ShapeDtypeStruct(shape, F32) for shape in shapes[: len(shapes) - kept]]
    specs = [pl.BlockSpec(memory_space=pl.ANY)] * len(outs)
    inputs = [*own, *other]
    if kept:
        inputs.append(gains)
        outs += [jax.ShapeDtypeStruct((rows, shapes[-1][0]), F32) for rows in (slots, gains.shape[0])]
        specs += [vmem] * 2
    return pl.pallas_call(
        lambda *refs: unpack_kernel(count, parts, regions, kept, *refs),
        in_specs=[pl.BlockSpec(memory_space=pltpu.SMEM)] + [vmem] * len(inputs),
        out_specs=specs,
        out_shape=outs,
        scratch_shapes=[pltpu.VMEM(shape, F32) for shape in shapes]
        + [pltpu.SemaphoreType.DMA((len(regions[0]) + len(regions[1]),))],
        compiler_params=pltpu.CompilerParams(vmem_limit_bytes=VMEM_LIMIT),
        cost_estimate=cost(60 if kept else 0.1),
        name="unpack",
    )(places, *inputs)


def pieces_in(value, place):
    parts = [lax.dynamic_index_in_dim(value, place, 0, keepdims=True)]
    sent = []
    for mask in range(1, lax.axis_size("section")):
        sent.append(lax.dynamic_index_in_dim(value, place ^ mask, 0, keepdims=True))
        parts.append(swap_pairs(sent[-1], "section", mask))
    return in_rank_order(jnp.concatenate(parts, axis=0), place), sent, parts[1:]


def in_rank_order(pieces, place):
    count = pieces.shape[0]
    return jnp.stack(
        [lax.dynamic_index_in_dim(pieces, at ^ place, 0, keepdims=False) for at in range(count)]
    )


def sources_in(arrays, place):
    sections = lax.axis_size("section")
    sent = []
    for mask in range(1, sections):
        picked = [lax.dynamic_index_in_dim(a, place ^ mask, 0, keepdims=True) for a in arrays]
        sent.append(jnp.concatenate(picked, axis=1))
    sent = list(lax.optimization_barrier(tuple(sent)))
    pieces = [swap_pairs(value, "section", mask + 1) for mask, value in enumerate(sent)]
    own = len(arrays)

    def choose(at, here):
        yield (at ^ here) == 0, [(number, here) for number in range(own)]
        for other in range(1, sections):
            yield (at ^ here) == other, [(own + other - 1, 0)]

    return Sources(list(arrays) + pieces, choose), pieces, sent


def gathered_sources(arrays, chunks):
    rows = gathered_in(jnp.concatenate(arrays, axis=1), chunks)
    return Sources([rows], lambda at, here: [(at >= 0, [(0, at)])])


def gathered_in(value, chunks):
    place = lax.axis_index("section")
    gathered = lax.all_gather(value, "section")
    own = lax.dynamic_index_in_dim(gathered, place // chunks, 1, keepdims=False)
    count = gathered.shape[0] // chunks
    return lax.dynamic_slice_in_dim(own, (place % chunks) * count, count, 0)


def gathered_out(value, chunks):
    place = lax.axis_index("section")
    gathered = lax.all_gather(value, "section")
    sections = gathered.shape[0]
    by_stream = gathered.reshape((sections // chunks, chunks * value.shape[0]) + value.shape[1:])
    return lax.dynamic_index_in_dim(by_stream, place, 1, keepdims=False)


def tied(value, *others):
    return lax.optimization_barrier((value,) + others)[0]


def body(
    tokens,
    doc_ids,
    reset_flags,
    attn_gain,
    w_qkv,
    w_attn_out,
    ffn_gain,
    w_in,
    w_out,
    write_gain,
    w_write,
    w_write_out,
    init_memory,
    out_grad,
    memory_grad,
):
    streams, _, seg, width = tokens.shape
    slots = init_memory.shape[0]
    sections = lax.axis_size("section")
    chunks = sections // streams
    segs = sections // chunks
    place = lax.axis_index("section")

    spread = np.tile(np.eye(slots, dtype=np.float32), (1, HEADS))
    consts = dict(
        segs=segs,
        seg=seg,
        init=init_memory,
        gains=jnp.stack([attn_gain, ffn_gain, write_gain]).astype(F32),
        spread=jnp.asarray(spread, BF16),
        fold=jnp.asarray(spread.T, BF16),
    )
    w = dict(
        qkv=w_qkv,
        ao=w_attn_out,
        out=w_out,
        write=w_write,
        wo=w_write_out,
        qkv_t=w_qkv.T,
        ao_t=w_attn_out.T,
        in_t=w_in.T,
        write_t=w_write.T,
        wo_t=w_write_out.T,
    )
    w["in"] = w_in

    marks = jnp.concatenate(
        [doc_ids[:, 0], jnp.broadcast_to(reset_flags, (streams, seg))], axis=1
    ).reshape(streams, 2, seg)
    marks = jnp.pad(marks, ((0, 0), (0, 14), (0, 0))).astype(BF16)
    parts_in = [tokens[:, 0], marks]
    grads_in = [out_grad[:, 0], memory_grad[:, 0]]
    empty = jnp.zeros((width, slots), BF16)
    if chunks == 1:
        rows, pieces, _ = sources_in(parts_in, place)
        gout, _, sent = sources_in([tied(value, *pieces) for value in grads_in], place)
        xor = place
    else:
        rows = gathered_sources(parts_in, chunks)
        gout = gathered_sources(grads_in, chunks)
        sent = []
        xor = 0
    xor = jnp.full((1,), xor, jnp.int32)

    arriving = empty
    then = tied(xor, *sent)
    for turn in range(chunks):
        kept = forward_chain(rows, then, arriving, consts, w)
        if turn < chunks - 1:
            arriving = lax.ppermute(
                kept["last"], "section", [(i, i + 1) for i in range(sections - 1)]
            )
    if chunks == 1:
        done, sent, pieces = pieces_in(kept["enc"], place)
        then = tied(xor, *sent)
    else:
        done = gathered_out(kept["enc"], chunks)
        pieces = []
        then = xor

    returning = empty
    for turn in range(chunks):
        grads = backward_chain(kept, gout, then, returning, consts, w)
        if turn < chunks - 1:
            returning = lax.ppermute(
                grads["sent"], "section", [(i + 1, i) for i in range(sections - 1)]
            )

    ff = w_in.shape[1]
    folds = ff // width
    cores = sum_phases()[0]
    side = phase_bit(cores).reshape(1)
    grads = dict(grads, gu=tied(grads['gu'], *pieces))
    sent = early_weights(kept, grads, 1 - side)
    shares = [phase_swap(value, cores) for value in sent]
    halves = early_weights(kept, grads, tied(side, *sent))
    ffn = Sum(halves[0], shares[0], halve_all=True)
    write = Sum(halves[1], shares[1], dp_first=True)
    groups = [ffn, write]
    after, _ = advance(groups)
    turns = [[2], [0, 3], [1]] if segs == 4 else [[at] for at in range(segs)]
    gqkv = None
    gain_parts = []
    outgoing, incoming = {}, {}
    leaving, arriving = [], []
    for turn in turns:
        which = tied(jnp.concatenate([xor ^ at for at in turn]), *after, *arriving)
        gqkv, out, part = attention_back(kept, grads, which, consts, w, gqkv)
        gain_parts.append(part)
        after, (out,) = advance(groups, part, extra=[out])
        arriving, leaving = leaving, []
        for number, at in enumerate(turn):
            outgoing[at] = out[number : number + 1]
            if chunks == 1 and at:
                incoming[at] = swap_pairs(outgoing[at], "section", at)
                leaving.append(incoming[at])

    sent = late_weights(kept, grads, gqkv, gain_parts, tied(1 - side, *after, *arriving))
    after, (sent,) = advance(groups, sent, extra=[sent])
    share = phase_swap(sent, cores)
    mine = tied(side, sent, *after, *leaving)
    late = Sum(late_weights(kept, grads, gqkv, gain_parts, mine), share)

    half = ff // 2

    def paired(number, start, at):
        main = (start, start + width, at, 0, (1 + number) * width)
        other = (start + width, start + 2 * width, at + number, 0, 0)
        return [main, other]

    ffn_regions = [
        [(0, half, 0, 0, number * half)]
        + [
            (half + at * width, half + (at + 1) * width, 1, number * half + at * width, 0)
            for at in range(half // width)
        ]
        for number in range(2)
    ]
    write_regions = [paired(number, 0, 0) for number in range(2)]
    late_regions = [
        paired(number, 0, 0) + [(2 * width, 2 * width + 128, 2 + number, 0, 0)]
        for number in range(2)
    ]
    square, triple = (width, width), (width, 3 * width)
    advance([late])
    advance(groups, late.sent)
    if chunks == 1:
        incoming[0] = tied(outgoing[0], late.sent)
        back = in_rank_order(jnp.concatenate([incoming[at] for at in range(segs)]), place)
    else:
        back = gathered_out(jnp.concatenate([outgoing[at] for at in range(segs)]), chunks)
    (token_grads,) = late.finish(back.astype(F32))
    advance([late])
    advance(groups, late.sent)
    (done,) = late.finish(done)
    advance([late])
    advance([late])
    advance(groups, late.sent)
    advance([late])
    advance([late])
    while ffn.steps or write.steps:
        advance(groups, late.sent)
    if late.steps:
        advance([late])
    advance(groups, late.sent)
    grad_write, grad_wo = unpacked(write, write_regions, [triple, square])
    grad_in, grad_out = unpacked(ffn, ffn_regions, [(width, ff), (ff, width)])
    grad_in, grad_write = late.finish(grad_in, grad_write)
    while late.steps:
        advance([late])
    if late.started is not None:
        late.finish()
    grad_qkv, grad_ao, grad_init, gains = unpacked(
        late, late_regions, [triple, square, (width, 128), (width, 128)], slots, consts["gains"]
    )
    return (
        done[:, None, :seg],
        done[:, None, seg:],
        token_grads[:, None],
        gains[0],
        grad_qkv,
        grad_ao,
        gains[1],
        grad_in,
        grad_out,
        gains[2],
        grad_write,
        grad_wo,
        grad_init,
    )


def solution(mesh):
    local = P("dp", "section")
    return jax.shard_map(
        body,
        mesh=mesh,
        in_specs=(local,) * 3 + (P(),) * 10 + (local,) * 2,
        out_specs=(local,) * 3 + (P(),) * 10,
        check_vma=False,
    )
```

```python
import jax
import jax.numpy as jnp
import numpy as np
from jax import lax
from jax.experimental import pallas as pl
from jax.experimental.pallas import tpu as pltpu
from jax.sharding import PartitionSpec as P

HEADS = 8
HEAD_DIM = 64
EPS = 1e-06
MASKED = -1000000000.0
F32 = jnp.float32
BF16 = jnp.bfloat16
SQRT_2_PI = 0.7978845608028654
CUBIC = 0.044715
VMEM_LIMIT = 60 * 1024 * 1024


def nn(left, right):
    return lax.dot_general(left, right, (((1,), (0,)), ((), ())), preferred_element_type=F32)


def tn(left, right):
    return lax.dot_general(left, right, (((0,), (0,)), ((), ())), preferred_element_type=F32)


def nt(left, right):
    return lax.dot_general(left, right, (((1,), (1,)), ((), ())), preferred_element_type=F32)


def wide(column_tile, width):
    copies = max(1, width // 128)
    if width < 128:
        return column_tile[:, :width]
    return jnp.concatenate([column_tile] * copies, axis=1)


def inverse_rms(values):
    return lax.rsqrt(jnp.mean(values * values, axis=0, keepdims=True) + EPS)


def lane_sums(values):
    total = values[:, :128]
    for at in range(128, values.shape[1], 128):
        total = total + values[:, at : at + 128]
    return total


def head_mask(rows, columns):
    row_head = lax.broadcasted_iota(jnp.int32, (rows, columns), 0) // HEAD_DIM
    column_head = lax.broadcasted_iota(jnp.int32, (rows, columns), 1) // HEAD_DIM
    return row_head == column_head


def spread_slots(values):
    pair = jnp.concatenate([values, values], axis=1)
    return jnp.concatenate([pair] * (HEADS // 2), axis=1)


def fold_slots(values):
    total = lane_sums(values)
    half = total.shape[1] // 2
    return total[:, :half] + total[:, half:]


def norm_back(grad_normed, normed, scale, gain, gain_inverse):
    weighed = grad_normed * normed
    mean = jnp.mean(weighed, axis=0, keepdims=True)
    return scale * (grad_normed * gain - normed * gain_inverse * mean), weighed


def gain_tiles(gains_ref, count=3):
    tiles = []
    for at in range(count):
        row = gains_ref[at : at + 1, :]
        tiles.append(jnp.broadcast_to(row, (128, row.shape[1])).T)
    return tiles


class Sources:
    def __init__(self, arrays, choices):
        self.arrays = arrays
        self.choices = choices

    def start(self, refs, at, place, buffer, sem):
        for condition, parts in self.choices(at, place):

            @pl.when(condition)
            def _():
                top = 0
                for number, index in parts:
                    source = refs[number].at[index]
                    target = buffer.at[pl.ds(top, source.shape[0]), :]
                    pltpu.make_async_copy(source, target, sem).start()
                    top += source.shape[0]

    def wait(self, buffer, sem):
        pltpu.make_async_copy(buffer, buffer, sem).wait()

    def rows_of(self, refs, steps, segment, place, buffer, sems):
        step = pl.program_id(0)
        slot = lax.rem(step, 2)

        @pl.when(step == 0)
        def _():
            self.start(refs, segment(0), place, buffer.at[0], sems.at[0])

        if steps > 1:

            @pl.when(step + 1 < steps)
            def _():
                self.start(refs, segment(step + 1), place, buffer.at[1 - slot], sems.at[1 - slot])

        self.wait(buffer.at[slot], sems.at[slot])
        return buffer.at[slot]


def forward_kernel(
    sources,
    segs,
    place_ref,
    mem0_ref,
    init_ref,
    gains_ref,
    spread_ref,
    fold_ref,
    *refs,
):
    wqkv_ref, wao_ref, win_ref, wout_ref, ww_ref, wwo_ref = refs[:6]
    refs = refs[6:]
    (
        enc_ref,
        a1_ref,
        a1m_ref,
        q_ref,
        kt_ref,
        ktm_ref,
        v_ref,
        vm_ref,
        e_ref,
        em_ref,
        att_ref,
        a2_ref,
        z_ref,
        gp_ref,
        a3_ref,
        a3m_ref,
        qw_ref,
        kwt_ref,
        kwtm_ref,
        vw_ref,
        vwm_ref,
        ew_ref,
        ewm_ref,
        watt_ref,
        stat_ref,
        last_ref,
        carry,
        bias,
        k_nat,
        km_nat,
        vt,
        vtm,
        hidden,
        row_buffer,
        row_sems,
    ) = refs[-35:]
    step = pl.program_id(0)
    rows_ref = sources.rows_of(
        refs[: len(sources.arrays)], segs, lambda s: s, place_ref[0], row_buffer, row_sems
    )
    width = wao_ref.shape[0]
    seg = q_ref.shape[2]
    slots = init_ref.shape[0]
    ff = win_ref.shape[0]

    @pl.when(step == 0)
    def _():
        carry[...] = mem0_ref[...].astype(F32)

    docs = rows_ref[seg : seg + 1, :].astype(F32)
    flag = rows_ref[seg + 1 : seg + 2, :].astype(F32)
    stat_ref[0, 5:6, :] = flag
    mem = jnp.where(flag[:, :slots] > 0.0, init_ref[...].astype(F32).T, carry[...])
    ga, gf, gw = gain_tiles(gains_ref)

    doc_rows = jnp.broadcast_to(docs, (128, seg)).T
    for at in range(0, seg, 128):
        bias[:, at : at + 128] = jnp.where(doc_rows == docs[:, at : at + 128], 0.0, MASKED)

    tokens = rows_ref[:seg, :].astype(F32).T
    r1 = inverse_rms(tokens)
    a1_ref[...] = (tokens * r1 * wide(ga, seg)).astype(BF16)
    rm = inverse_rms(mem)
    a1m_ref[0] = (mem * rm * ga[:, :slots]).astype(BF16)
    stat_ref[0, 0:1, :] = r1
    stat_ref[0, 4:5, :slots] = rm

    a1 = a1_ref[...]
    a1m = a1m_ref[0]
    q_ref[0] = (nn(wqkv_ref[:width, :], a1) * HEAD_DIM**-0.5).astype(BF16)
    kt = nn(wqkv_ref[width : 2 * width, :], a1).astype(BF16)
    kt_ref[0] = kt
    k_nat[...] = kt.T
    vt[...] = nn(wqkv_ref[2 * width :, :], a1).astype(BF16)
    v_ref[0] = vt[...].T
    ktm = nn(wqkv_ref[width : 2 * width, :], a1m).astype(BF16)
    ktm_ref[0] = ktm
    km_nat[...] = ktm.T
    vtm[...] = nn(wqkv_ref[2 * width :, :], a1m).astype(BF16)
    vm_ref[0] = vtm[...].T

    def pair(index, unused):
        lanes = pl.ds(pl.multiple_of(index * 128, 128), 128)
        keys = k_nat[:, lanes]
        mem_keys = km_nat[:, lanes]
        for half in range(2):
            head = index * 2 + half
            rows = pl.ds(pl.multiple_of(head * HEAD_DIM, HEAD_DIM), HEAD_DIM)
            queries = q_ref[0, rows, :]
            blank = jnp.zeros_like(queries)
            queries = jnp.concatenate([queries, blank] if half == 0 else [blank, queries], axis=0)
            scores = nn(keys, queries) + bias[...]
            mem_scores = nn(mem_keys, queries)
            top = jnp.maximum(
                jnp.max(scores, axis=0, keepdims=True), jnp.max(mem_scores, axis=0, keepdims=True)
            )
            raised = jnp.exp(scores - top)
            mem_raised = jnp.exp(mem_scores - top)
            inverse = 1.0 / (
                jnp.sum(raised, axis=0, keepdims=True) + jnp.sum(mem_raised, axis=0, keepdims=True)
            )
            raised = raised.astype(BF16)
            mem_raised = mem_raised.astype(BF16)
            e_ref[0, head] = raised
            em_ref[0, rows, :] = mem_raised
            mixed = nn(vt[rows, :], raised) + nn(vtm[rows, :], mem_raised)
            att_ref[rows, :] = (mixed * inverse).astype(BF16)
            stat_ref[0, pl.ds(8 + head, 1), :] = inverse
        return unused

    lax.fori_loop(0, HEADS // 2, pair, 0, unroll=HEADS // 2)

    h1 = rows_ref[:seg, :].astype(F32).T + nn(wao_ref[...], att_ref[...])
    r2 = inverse_rms(h1)
    stat_ref[0, 1:2, :] = r2
    a2_ref[...] = (h1 * r2 * wide(gf, seg)).astype(BF16)
    hidden[...] = h1
    a2 = a2_ref[...]
    for at in range(0, ff, 512):
        upper = nn(win_ref[at : at + 512, :], a2)
        square = upper * upper
        bent = jnp.tanh(upper * (SQRT_2_PI + (SQRT_2_PI * CUBIC) * square))
        cdf = 0.5 + 0.5 * bent
        z_ref[at : at + 512, :] = (upper * cdf).astype(BF16)
        slope = (0.5 * SQRT_2_PI) + (1.5 * SQRT_2_PI * CUBIC) * square
        gp_ref[0, at : at + 512, :] = (cdf + upper * (1.0 - bent * bent) * slope).astype(BF16)
    enc = hidden[...] + tn(wout_ref[...], z_ref[...])
    enc_ref[0, :seg, :] = enc.T.astype(BF16)
    r3 = inverse_rms(enc)
    stat_ref[0, 2:3, :] = r3
    a3_ref[...] = (enc * r3 * wide(gw, seg)).astype(BF16)
    a3m_ref[0] = (mem * rm * gw[:, :slots]).astype(BF16)
    a3 = a3_ref[...]
    a3m = a3m_ref[0]

    kwt = nn(ww_ref[width : 2 * width, :], a3).astype(BF16)
    kwt_ref[0] = kwt
    kw = kwt.T
    vwt = nn(ww_ref[2 * width :, :], a3).astype(BF16)
    vw_ref[0] = vwt.T
    kwtm = nn(ww_ref[width : 2 * width, :], a3m).astype(BF16)
    kwtm_ref[0] = kwtm
    vwtm = nn(ww_ref[2 * width :, :], a3m).astype(BF16)
    vwm_ref[0] = vwtm.T
    qwt = (nn(ww_ref[:width, :], a3m) * HEAD_DIM**-0.5).astype(BF16)
    own = head_mask(width, HEADS * slots)
    qw = jnp.where(own, nn(qwt, spread_ref[...]), 0.0).astype(BF16)
    qw_ref[0] = qw
    scores = nn(kw, qw)
    mem_scores = nn(kwtm.T, qw)
    slot_row = lax.broadcasted_iota(jnp.int32, mem_scores.shape, 0)
    slot_col = lax.broadcasted_iota(jnp.int32, mem_scores.shape, 1) % slots
    mem_scores = jnp.where(slot_row == slot_col, mem_scores, MASKED)
    top = jnp.maximum(
        jnp.max(scores, axis=0, keepdims=True), jnp.max(mem_scores, axis=0, keepdims=True)
    )
    raised = jnp.exp(scores - top)
    mem_raised = jnp.exp(mem_scores - top)
    inverse = 1.0 / (
        jnp.sum(raised, axis=0, keepdims=True) + jnp.sum(mem_raised, axis=0, keepdims=True)
    )
    stat_ref[0, 3:4, :] = inverse
    raised = raised.astype(BF16)
    mem_raised = mem_raised.astype(BF16)
    ew_ref[0] = raised
    ewm_ref[0] = mem_raised
    mixed = (nn(vwt, raised) + nn(vwtm, mem_raised)) * inverse
    watt = fold_slots(jnp.where(own, mixed, 0.0)).astype(BF16)
    watt_ref[0] = watt
    new_mem = (mem + nn(wwo_ref[...], watt)).astype(BF16).astype(F32)
    carry[...] = new_mem
    enc_ref[0, seg:, :] = new_mem.T.astype(BF16)
    last_ref[...] = new_mem.astype(BF16)


def chain_kernel(
    sources,
    segs,
    place_ref,
    carry0_ref,
    weights_gains_ref,
    wwo_ref,
    ww_ref,
    wout_ref,
    win_ref,
    wao_ref,
    wqkv_ref,
    a1m_ref,
    q_ref,
    vm_ref,
    em_ref,
    att_ref,
    a2_ref,
    gp_ref,
    a3_ref,
    a3m_ref,
    qw_ref,
    kwt_ref,
    kwtm_ref,
    vw_ref,
    vwm_ref,
    ew_ref,
    ewm_ref,
    stat_ref,
    *refs,
):
    source_refs, refs = refs[: len(sources.arrays)], refs[len(sources.arrays) :]
    bm_ref, gwkv_ref, gwm_ref, bf_ref, gu_ref, ba_ref, gh_ref, do_ref, dd_ref, dsm_ref = refs[:10]
    gkvm_ref, init_ref, gains_ref, sent_ref, carry, grad_buffer, grad_sems = refs[10:]
    gout_ref = sources.rows_of(
        source_refs, segs, lambda s: segs - 1 - s, place_ref[0], grad_buffer, grad_sems
    )
    step = pl.program_id(0)
    width = wao_ref.shape[0]
    ff = wout_ref.shape[0]
    seg = q_ref.shape[2]
    slots = a1m_ref.shape[2]
    reset = stat_ref[0, 5:6, :slots] > 0.0

    @pl.when(step == 0)
    def _():
        carry[...] = carry0_ref[...].astype(F32)
        init_ref[...] = jnp.zeros_like(init_ref)
        gains_ref[...] = jnp.zeros_like(gains_ref)

    ga, gf, gw = gain_tiles(weights_gains_ref)
    gai, gfi, gwi = 1.0 / ga, 1.0 / gf, 1.0 / gw
    own = head_mask(width, HEADS * slots)
    rm = stat_ref[0, 4:5, :slots]

    grad_mem = gout_ref[seg:, :].astype(F32).T + carry[...]
    branch_mem = grad_mem.astype(BF16)
    bm_ref[0] = branch_mem
    grad_watt = nn(wwo_ref[...], branch_mem).astype(BF16)
    inverse = stat_ref[0, 3:4, :]
    scaled = (jnp.where(own, spread_slots(grad_watt.astype(F32)), 0.0) * inverse).astype(BF16)
    raised = ew_ref[0].astype(F32)
    mem_raised = ewm_ref[0].astype(F32)
    grad_probs = nn(vw_ref[0], scaled)
    mem_grad_probs = nn(vwm_ref[0], scaled)
    dots = (
        jnp.sum(raised * grad_probs, axis=0, keepdims=True)
        + jnp.sum(mem_raised * mem_grad_probs, axis=0, keepdims=True)
    ) * inverse
    grad_scores = (raised * (grad_probs - dots)).astype(BF16)
    mem_grad_scores = (mem_raised * (mem_grad_probs - dots)).astype(BF16)
    gwkv_ref[:width, :] = nt(qw_ref[0], grad_scores).astype(BF16)
    gwkv_ref[width:, :] = nt(scaled, ew_ref[0]).astype(BF16)
    grad_q = (nn(kwt_ref[0], grad_scores) + nn(kwtm_ref[0], mem_grad_scores)) * HEAD_DIM**-0.5
    gwm_ref[0, :width, :] = fold_slots(jnp.where(own, grad_q, 0.0)).astype(BF16)
    gwm_ref[0, width : 2 * width, :] = nt(qw_ref[0], mem_grad_scores).astype(BF16)
    gwm_ref[0, 2 * width :, :] = nt(scaled, ewm_ref[0]).astype(BF16)

    grad_a3 = nn(ww_ref[:, width:], gwkv_ref[...])
    grad_a3m = nn(ww_ref[...], gwm_ref[0])
    part, weighed = norm_back(
        grad_a3, a3_ref[...].astype(F32), stat_ref[0, 2:3, :], wide(gw, seg), wide(gwi, seg)
    )
    mem_part, mem_weighed = norm_back(
        grad_a3m, a3m_ref[0].astype(F32), rm, gw[:, :slots], gwi[:, :slots]
    )
    gains_ref[2] += lane_sums(weighed)
    gains_ref[2, :, :slots] += mem_weighed
    grad_mem_in = grad_mem + mem_part
    gh_ref[0] = gout_ref[:seg, :].astype(F32).T + part

    bf_ref[...] = gh_ref[0].astype(BF16)
    branch = bf_ref[...]
    for at in range(0, ff, 512):
        grad_z = nn(wout_ref[at : at + 512, :], branch)
        gu_ref[at : at + 512, :] = (grad_z * gp_ref[0, at : at + 512, :].astype(F32)).astype(BF16)
    grad_a2 = nn(win_ref[...], gu_ref[...])
    part, weighed = norm_back(
        grad_a2, a2_ref[...].astype(F32), stat_ref[0, 1:2, :], wide(gf, seg), wide(gfi, seg)
    )
    gains_ref[1] += lane_sums(weighed)
    gh_ref[0] += part

    ba_ref[...] = gh_ref[0].astype(BF16)
    grad_att = nn(wao_ref[...], ba_ref[...]).astype(BF16)
    products = grad_att.astype(F32) * att_ref[...].astype(F32)
    rows = []
    dots = []
    for head in range(HEADS):
        span = slice(head * HEAD_DIM, (head + 1) * HEAD_DIM)
        inverse = stat_ref[0, 8 + head : 9 + head, :]
        dots.append(jnp.sum(products[span, :], axis=0, keepdims=True) * inverse)
        rows.append((grad_att[span, :].astype(F32) * inverse).astype(BF16))
    scaled = jnp.concatenate(rows, axis=0)
    do_ref[0] = scaled
    dd_ref[0] = jnp.concatenate(dots, axis=0)
    mem_values = jnp.concatenate([vm_ref[0].astype(F32)] * HEADS, axis=0)
    mem_values = jnp.where(own, mem_values, 0.0).astype(BF16)
    grad_probs = nn(mem_values, scaled)
    parts = []
    for head in range(HEADS):
        span = slice(head * slots, (head + 1) * slots)
        parts.append(
            (em_ref[0, span, :].astype(F32) * (grad_probs[span, :] - dots[head])).astype(BF16)
        )
    grad_scores = jnp.concatenate(parts, axis=0)
    dsm_ref[0] = grad_scores
    grad_k = jnp.where(own, nt(q_ref[0], grad_scores), 0.0)
    grad_v = jnp.where(own, nt(scaled, em_ref[0]), 0.0)
    gkvm_ref[0, :width, :] = fold_slots(grad_k).astype(BF16)
    gkvm_ref[0, width:, :] = fold_slots(grad_v).astype(BF16)
    grad_a1m = nn(wqkv_ref[:, width:], gkvm_ref[0])
    mem_part, mem_weighed = norm_back(
        grad_a1m, a1m_ref[0].astype(F32), rm, ga[:, :slots], gai[:, :slots]
    )
    gains_ref[0, :, :slots] += mem_weighed
    grad_mem_in = grad_mem_in + mem_part
    init_ref[...] += jnp.where(reset, grad_mem_in, 0.0)
    carry[...] = jnp.where(reset, 0.0, grad_mem_in).astype(BF16).astype(F32)
    sent_ref[...] = carry[...].astype(BF16)


def attention_kernel(
    alone,
    place_ref,
    do_ref,
    dd_ref,
    dsm_ref,
    q_ref,
    kt_ref,
    ktm_ref,
    v_ref,
    e_ref,
    stat_ref,
    gains_ref,
    gh_ref,
    a1_ref,
    wqkv_ref,
    *refs,
):
    step = pl.program_id(0)
    copies = []
    if alone:
        gqkv_ref, out_ref, gain_ref, *buffers, sems = refs[-7:]
        place = place_ref[0]
        tokens = gh_ref.shape[2]
        lanes = pl.ds(pl.multiple_of(place * tokens, tokens), tokens)
        sources = [gh_ref.at[pl.ds(place, 1)], a1_ref.at[:, lanes], wqkv_ref]
        for at, (source, target) in enumerate(zip(sources, buffers)):
            copies.append(fetch(source, target, sems.at[at]))
        gh_ref, a1_ref, wqkv_ref = buffers
    else:
        gqkv_ref, out_ref, gain_ref = refs[-3:]
    width = wqkv_ref.shape[0]
    seg = q_ref.shape[2]
    for head in range(HEADS):
        span = slice(head * HEAD_DIM, (head + 1) * HEAD_DIM)
        key_span = slice(width + head * HEAD_DIM, width + (head + 1) * HEAD_DIM)
        value_span = slice(2 * width + head * HEAD_DIM, 2 * width + (head + 1) * HEAD_DIM)
        grads = do_ref[0, span, :]
        blank = jnp.zeros_like(grads)
        padded = jnp.concatenate([grads, blank] if head % 2 == 0 else [blank, grads], axis=0)
        dots = dd_ref[0, head : head + 1, :]
        lanes = slice(head // 2 * 128, head // 2 * 128 + 128)
        grad_probs = nn(v_ref[0, :, lanes], padded)
        inner = (e_ref[0, head].astype(F32) * (grad_probs - dots)).astype(BF16)
        grad_q = nn(kt_ref[0, span, :], inner) + nn(ktm_ref[0, span, :], dsm_ref[0, span, :])
        gqkv_ref[span, :] = (grad_q * HEAD_DIM**-0.5).astype(BF16)
        gqkv_ref[key_span, :] = nt(q_ref[0, span, :], inner).astype(BF16)
        gqkv_ref[value_span, :] = nt(grads, e_ref[0, head]).astype(BF16)

    for copy in copies:
        copy.wait()
    grad_a1 = nn(wqkv_ref[...], gqkv_ref[...])
    (ga,) = gain_tiles(gains_ref, 1)
    part, weighed = norm_back(
        grad_a1,
        a1_ref[...].astype(F32),
        stat_ref[0, 0:1, :],
        wide(ga, seg),
        wide(1.0 / ga, seg),
    )
    gain_ref[...] = jnp.where(step == 0, 0.0, gain_ref[...]) + lane_sums(weighed)
    out_ref[0] = (gh_ref[0] + part).T.astype(BF16)


def whole(array):
    zeros = (0,) * array.ndim
    return pl.BlockSpec(array.shape, lambda *unused: zeros, pipeline_mode=pl.Buffered(1))


def params():
    return pltpu.CompilerParams(dimension_semantics=("arbitrary",), vmem_limit_bytes=VMEM_LIMIT)


def cost(microseconds):
    return pl.CostEstimate(
        flops=int(microseconds * 1e9), bytes_accessed=1 << 20, transcendentals=0
    )


def forward_chain(sources, place, mem0, consts, w):
    segs = consts["segs"]
    seg = consts["seg"]
    width, slots = mem0.shape
    ff = w["in_t"].shape[0]

    def flat(height):
        return (
            jax.ShapeDtypeStruct((height, segs * seg), BF16),
            pl.BlockSpec((height, seg), lambda s, f: (0, s)),
        )

    def stack(*shape, dtype=BF16):
        tail = (0,) * len(shape)
        return (
            jax.ShapeDtypeStruct((segs,) + shape, dtype),
            pl.BlockSpec((1,) + shape, lambda s, f: (s,) + tail),
        )

    outs = dict(
        enc=stack(seg + slots, width),
        a1=flat(width),
        a1m=stack(width, slots),
        q=stack(width, seg),
        kt=stack(width, seg),
        ktm=stack(width, slots),
        v=stack(seg, width),
        vm=stack(slots, width),
        e=stack(HEADS, seg, seg),
        em=stack(HEADS * slots, seg),
        att=flat(width),
        a2=flat(width),
        z=flat(ff),
        gp=stack(ff, seg),
        a3=flat(width),
        a3m=stack(width, slots),
        qw=stack(width, HEADS * slots),
        kwt=stack(width, seg),
        kwtm=stack(width, slots),
        vw=stack(seg, width),
        vwm=stack(slots, width),
        ew=stack(seg, HEADS * slots),
        ewm=stack(slots, HEADS * slots),
        watt=stack(width, slots),
        stat=stack(16, seg, dtype=F32),
        last=(
            jax.ShapeDtypeStruct((width, slots), BF16),
            pl.BlockSpec((width, slots), lambda s, f: (0, 0)),
        ),
    )
    fixed = [
        mem0,
        consts["init"],
        consts["gains"],
        consts["spread"],
        consts["fold"],
    ]
    weights = [w[name] for name in ("qkv_t", "ao_t", "in_t", "out", "write_t", "wo_t")]
    results = pl.pallas_call(
        lambda *refs: forward_kernel(sources, segs, *refs),
        grid_spec=pltpu.PrefetchScalarGridSpec(
            num_scalar_prefetch=1,
            grid=(segs,),
            in_specs=[whole(a) for a in fixed + weights]
            + [pl.BlockSpec(memory_space=pl.ANY)] * len(sources.arrays),
            out_specs=[spec for _, spec in outs.values()],
            scratch_shapes=[
                pltpu.VMEM((width, slots), F32),
                pltpu.VMEM((seg, seg), F32),
                pltpu.VMEM((seg, width), BF16),
                pltpu.VMEM((slots, width), BF16),
                pltpu.VMEM((width, seg), BF16),
                pltpu.VMEM((width, slots), BF16),
                pltpu.VMEM((width, seg), F32),
                pltpu.VMEM((2, seg + 16, width), BF16),
                pltpu.SemaphoreType.DMA((2,)),
            ],
        ),
        out_shape=[shape for shape, _ in outs.values()],
        compiler_params=params(),
        cost_estimate=cost(15 * segs),
        name="forward_chain",
    )(place, *fixed, *weights, *sources.arrays)
    return dict(zip(outs, results))


def backward_chain(kept, sources, place, carry0, consts, w):
    segs = consts["segs"]
    width, slots = kept["a1m"].shape[1:]
    seg = kept["q"].shape[2]
    ff = kept["gp"].shape[1]
    last = segs - 1

    def flat(height):
        return (
            jax.ShapeDtypeStruct((height, segs * seg), BF16),
            pl.BlockSpec((height, seg), lambda s, f: (0, last - s)),
        )

    def stack(*shape, dtype=BF16):
        tail = (0,) * len(shape)
        return (
            jax.ShapeDtypeStruct((segs,) + shape, dtype),
            pl.BlockSpec((1,) + shape, lambda s, f: (last - s,) + tail),
        )

    def single(*shape, dtype=F32):
        tail = (0,) * len(shape)
        return (jax.ShapeDtypeStruct(shape, dtype), pl.BlockSpec(shape, lambda s, f: tail))

    outs = dict(
        bm=stack(width, slots),
        gwkv=flat(2 * width),
        gwm=stack(3 * width, slots),
        bf=flat(width),
        gu=flat(ff),
        ba=flat(width),
        gh=stack(width, seg, dtype=F32),
        do=stack(width, seg),
        dd=stack(HEADS, seg, dtype=F32),
        dsm=stack(HEADS * slots, seg),
        gkvm=stack(2 * width, slots),
        init=single(width, slots),
        gains=single(3, width, 128),
        sent=single(width, slots, dtype=BF16),
    )
    fixed = [
        carry0,
        consts["gains"],
    ]
    weights = [w[name] for name in ("wo", "write", "out", "in", "ao", "qkv")]
    blocked = ["a1m", "q", "vm", "em", "att", "a2", "gp", "a3", "a3m", "qw"]
    blocked += ["kwt", "kwtm", "vw", "vwm", "ew", "ewm", "stat"]

    def spec_of(array):
        if array.ndim == 2:
            return pl.BlockSpec((array.shape[0], seg), lambda s, f: (0, last - s))
        tail = (0,) * (array.ndim - 1)
        return pl.BlockSpec((1,) + array.shape[1:], lambda s, f: (last - s,) + tail)

    results = pl.pallas_call(
        lambda *refs: chain_kernel(sources, segs, *refs),
        grid_spec=pltpu.PrefetchScalarGridSpec(
            num_scalar_prefetch=1,
            grid=(segs,),
            in_specs=[whole(a) for a in fixed + weights]
            + [spec_of(kept[name]) for name in blocked]
            + [pl.BlockSpec(memory_space=pl.ANY)] * len(sources.arrays),
            out_specs=[spec for _, spec in outs.values()],
            scratch_shapes=[
                pltpu.VMEM((width, slots), F32),
                pltpu.VMEM((2, seg + slots, width), BF16),
                pltpu.SemaphoreType.DMA((2,)),
            ],
        ),
        out_shape=[shape for shape, _ in outs.values()],
        compiler_params=params(),
        cost_estimate=cost(11 * segs),
        name="backward_chain",
    )(place, *fixed, *weights, *[kept[name] for name in blocked], *sources.arrays)
    return dict(zip(outs, results))


def attention_back(kept, grads, which, consts, w, before):
    segs, width, seg = kept["q"].shape
    count = which.shape[0]

    def by_seg(array):
        if array.ndim == 2:
            return pl.BlockSpec((array.shape[0], seg), lambda s, f: (0, f[s]))
        tail = (0,) * (array.ndim - 1)
        return pl.BlockSpec((1,) + array.shape[1:], lambda s, f: (f[s],) + tail)

    alone = count == 1
    blocked = [grads[name] for name in ("do", "dd", "dsm")]
    blocked += [kept[name] for name in ("q", "kt", "ktm", "v", "e", "stat")]
    inputs = [(array, by_seg(array)) for array in blocked]
    inputs.append((consts["gains"], whole(consts["gains"])))
    last = [grads["gh"], kept["a1"], w["qkv"]]
    scratch = []
    if alone:
        inputs += [(array, pl.BlockSpec(memory_space=pl.ANY)) for array in last]
        scratch = [
            pltpu.VMEM((1, width, seg), F32),
            pltpu.VMEM((width, seg), BF16),
            pltpu.VMEM(w["qkv"].shape, BF16),
            pltpu.SemaphoreType.DMA((3,)),
        ]
    else:
        inputs += [(array, by_seg(array)) for array in last[:2]] + [(last[2], whole(last[2]))]
    passed = [] if before is None else [before]
    return pl.pallas_call(
        lambda *refs: attention_kernel(alone, *refs),
        grid_spec=pltpu.PrefetchScalarGridSpec(
            num_scalar_prefetch=1,
            grid=(count,),
            in_specs=[spec for _, spec in inputs]
            + [pl.BlockSpec(memory_space=pl.ANY)] * len(passed),
            out_specs=[
                pl.BlockSpec((3 * width, seg), lambda s, f: (0, f[s])),
                pl.BlockSpec((1, seg, width), lambda s, f: (s, 0, 0)),
                pl.BlockSpec((width, 128), lambda s, f: (0, 0)),
            ],
            scratch_shapes=scratch,
        ),
        out_shape=[
            jax.ShapeDtypeStruct((3 * width, segs * seg), BF16),
            jax.ShapeDtypeStruct((count, seg, width), BF16),
            jax.ShapeDtypeStruct((width, 128), F32),
        ],
        input_output_aliases={1 + len(inputs): 0} if passed else {},
        compiler_params=params(),
        cost_estimate=cost(10 * count),
        name="attention_back",
    )(which, *[array for array, _ in inputs], *passed)


def swap_pairs(value, axis, mask):
    size = lax.axis_size(axis)
    return lax.ppermute(value, axis, [(i, i ^ mask) for i in range(size)])


def sum_phases(dp_first=False):
    section = [("section", 1 << at) for at in range(lax.axis_size("section").bit_length() - 1)]
    dp = [("dp", 1 << at) for at in range(lax.axis_size("dp").bit_length() - 1)]
    phases = [(step, step) for step in section[:1]]
    crossed = []
    if len(section) > 1 and dp:
        crossed = [(dp[0], section[1]), (section[1], dp[0])]
        section, dp = section[2:], dp[1:]
    else:
        section = section[1:]
    straight = [(step, step) for step in dp + section]
    return phases + (straight + crossed if dp_first else crossed + straight)


def phase_swap(value, phase):
    sections, dps = lax.axis_size("section"), lax.axis_size("dp")
    route = []
    for section in range(sections):
        axis, mask = phase[section % 2]
        for dp in range(dps):
            to = ((section ^ mask) * dps + dp) if axis == "section" else (section * dps + (dp ^ mask))
            route.append((section * dps + dp, to))
    return lax.ppermute(value, ("section", "dp"), route)


def phase_bit(phase):
    bits = [(lax.axis_index(axis) // mask) % 2 for axis, mask in phase]
    return jnp.where(lax.axis_index("section") % 2 == 0, bits[0], bits[1])


def half_of(value, side):
    half = value.shape[0] // 2
    return lax.dynamic_slice_in_dim(value, side * half, half, 0)


def fetch(source, target, sem):
    copy = pltpu.make_async_copy(source, target, sem)
    copy.start()
    return copy


def slot_sum(left, right):
    join = lambda ref: jnp.concatenate([ref[at] for at in range(ref.shape[0])], axis=1)
    return nt(join(left), join(right))


def early_weights_kernel(
    side_ref, a2_ref, gu_ref, bf_ref, z_ref, a3_ref, gwkv_ref, a3m_ref, gwm_ref, watt_ref, bm_ref, *refs
):
    ffn_ref, write_ref, a2, gu, z, bf, a3, gw, a3m, gwm, left, right, staged, in_sems, out_sems = refs
    side = side_ref[0]
    width = a2.shape[0]
    folds = gu.shape[0]
    base = side * (folds * width)
    loads = []

    def load(source, target):
        loads.append(fetch(source, target, in_sems.at[len(loads)]))

    def wait(count):
        for _ in range(count):
            loads[wait.done].wait()
            wait.done += 1

    wait.done = 0
    load(a2_ref, a2)
    for at in range(folds):
        rows = pl.ds(pl.multiple_of(base + at * width, width), width)
        load(gu_ref.at[rows, :], gu.at[at])
    load(bf_ref, bf)
    for at in range(folds):
        rows = pl.ds(pl.multiple_of(base + at * width, width), width)
        load(z_ref.at[rows, :], z.at[at])
    load(a3_ref, a3)
    load(gwkv_ref.at[pl.ds(pl.multiple_of(side * width, width), width), :], gw)
    load(a3m_ref, a3m)
    load(gwm_ref.at[:, pl.ds(pl.multiple_of((1 + side) * width, width), width), :], gwm)
    last = in_sems.at[len(loads)]

    @pl.when(side == 0)
    def _():
        pltpu.make_async_copy(a3m_ref, left, last).start()
        pltpu.make_async_copy(gwm_ref.at[:, pl.ds(0, width), :], right, last).start()

    @pl.when(side == 1)
    def _():
        pltpu.make_async_copy(watt_ref, left, last).start()
        pltpu.make_async_copy(bm_ref, right, last).start()

    stores = []

    def put(tile, value):
        columns = slice(tile * width, (tile + 1) * width)
        staged[:, columns] = value.astype(BF16)
        out, first = (ffn_ref, 0) if tile < 2 * folds else (write_ref, 2 * folds)
        target = out.at[:, pl.ds((tile - first) * width, width)]
        stores.append(fetch(staged.at[:, columns], target, out_sems.at[tile]))

    wait(1)
    for at in range(folds):
        wait(1)
        put(at, nt(a2[...], gu[at]))
    wait(1)
    for at in range(folds):
        wait(1)
        put(folds + at, nt(z[at], bf[...]))
    wait(4)
    put(2 * folds, nt(a3[...], gw[...]) + slot_sum(a3m, gwm))
    pltpu.make_async_copy(watt_ref, left, last).wait()
    pltpu.make_async_copy(bm_ref, right, last).wait()
    put(2 * folds + 1, slot_sum(left, right))
    for store in stores:
        store.wait()


def early_weights(kept, grads, side):
    width, tokens = kept["a2"].shape
    folds = kept["z"].shape[0] // 2 // width
    inputs = [kept["a2"], grads["gu"], grads["bf"], kept["z"], kept["a3"], grads["gwkv"]]
    inputs += [kept["a3m"], grads["gwm"], kept["watt"], grads["bm"]]
    anywhere = pl.BlockSpec(memory_space=pl.ANY)
    full = pltpu.VMEM((width, tokens), BF16)
    several = pltpu.VMEM((folds, width, tokens), BF16)
    slots = pltpu.VMEM(kept["a3m"].shape, BF16)
    out = jax.ShapeDtypeStruct((width, (2 * folds + 2) * width), BF16)
    return pl.pallas_call(
        early_weights_kernel,
        grid_spec=pltpu.PrefetchScalarGridSpec(
            num_scalar_prefetch=1,
            grid=(1,),
            in_specs=[anywhere] * len(inputs),
            out_specs=[anywhere] * 2,
            scratch_shapes=[full, several, several, full, full, full]
            + [slots] * 4
            + [
                pltpu.VMEM(out.shape, BF16),
                pltpu.SemaphoreType.DMA((7 + 2 * folds,)),
                pltpu.SemaphoreType.DMA((2 * folds + 2,)),
            ],
        ),
        out_shape=[
            jax.ShapeDtypeStruct((width, 2 * folds * width), BF16),
            jax.ShapeDtypeStruct((width, 2 * width), BF16),
        ],
        compiler_params=params(),
        cost_estimate=cost(9),
        name="early_weights",
    )(side, *inputs)


def late_weights_kernel(count, side_ref, a1_ref, gqkv_ref, att_ref, ba_ref, a1m_ref, gkvm_ref, *refs):
    init_ref, gains_ref, refs = refs[0], refs[1], refs[2:]
    part_refs, refs = refs[:count], refs[count:]
    out_ref, a1, main, left, right, a1m, gkvm, init, gains, parts, staged, in_sems, out_sems = refs
    side = side_ref[0]
    width = a1.shape[0]
    slots = init.shape[1]
    rows = pl.ds(pl.multiple_of((1 + side) * width, width), width)
    kv_rows = pl.ds(pl.multiple_of(side * width, width), width)
    loads = [
        fetch(a1_ref, a1, in_sems.at[0]),
        fetch(gqkv_ref.at[rows, :], main, in_sems.at[1]),
        fetch(a1m_ref, a1m, in_sems.at[2]),
        fetch(gkvm_ref.at[:, kv_rows, :], gkvm, in_sems.at[3]),
    ]

    @pl.when(side == 0)
    def _():
        pltpu.make_async_copy(a1_ref, left, in_sems.at[4]).start()
        pltpu.make_async_copy(gqkv_ref.at[pl.ds(0, width), :], right, in_sems.at[5]).start()

    @pl.when(side == 1)
    def _():
        pltpu.make_async_copy(att_ref, left, in_sems.at[4]).start()
        pltpu.make_async_copy(ba_ref, right, in_sems.at[5]).start()

    others = [fetch(init_ref, init, in_sems.at[6]), fetch(gains_ref, gains, in_sems.at[7])]
    others += [fetch(ref, parts.at[at], in_sems.at[8 + at]) for at, ref in enumerate(part_refs)]
    stores = []

    def put(columns, value):
        staged[:, columns] = value.astype(BF16)
        stores.append(fetch(staged.at[:, columns], out_ref.at[:, columns], out_sems.at[len(stores)]))

    for load in loads:
        load.wait()
    put(slice(0, width), nt(a1[...], main[...]) + slot_sum(a1m, gkvm))
    pltpu.make_async_copy(att_ref, left, in_sems.at[4]).wait()
    pltpu.make_async_copy(ba_ref, right, in_sems.at[5]).wait()
    put(slice(width, 2 * width), nt(left[...], right[...]))
    for load in others:
        load.wait()
    columns = [gains[0], gains[1], gains[2]]
    for at in range(count):
        columns[0] = columns[0] + parts[at]
    lane = lax.broadcasted_iota(jnp.int32, init.shape, 1)
    extras = jnp.zeros(init.shape, F32)
    for at, column in enumerate(columns):
        extras = jnp.where(lane == at, jnp.sum(column, axis=1, keepdims=True), extras)
    extras = jnp.where(side == 0, init[...], extras)
    extras = jnp.concatenate([extras, jnp.zeros_like(extras)], axis=1)
    put(slice(2 * width, 2 * width + 2 * slots), extras)
    for store in stores:
        store.wait()


def late_weights(kept, grads, gqkv, gain_parts, side):
    width, tokens = kept["a1"].shape
    count = len(gain_parts)
    inputs = [kept["a1"], gqkv, kept["att"], grads["ba"], kept["a1m"], grads["gkvm"]]
    inputs += [grads["init"], grads["gains"]] + list(gain_parts)
    slots = grads["init"].shape[1]
    anywhere = pl.BlockSpec(memory_space=pl.ANY)
    full = pltpu.VMEM((width, tokens), BF16)
    small = pltpu.VMEM(kept["a1m"].shape, BF16)
    out = jax.ShapeDtypeStruct((width, 2 * width + 2 * slots), BF16)
    return pl.pallas_call(
        lambda *refs: late_weights_kernel(count, *refs),
        grid_spec=pltpu.PrefetchScalarGridSpec(
            num_scalar_prefetch=1,
            grid=(1,),
            in_specs=[anywhere] * len(inputs),
            out_specs=anywhere,
            scratch_shapes=[full] * 4
            + [small] * 2
            + [
                pltpu.VMEM(grads["init"].shape, F32),
                pltpu.VMEM(grads["gains"].shape, F32),
                pltpu.VMEM((count,) + gain_parts[0].shape, F32),
                pltpu.VMEM(out.shape, BF16),
                pltpu.SemaphoreType.DMA((8 + count,)),
                pltpu.SemaphoreType.DMA((3,)),
            ],
        ),
        out_shape=out,
        compiler_params=params(),
        cost_estimate=cost(4),
        name="late_weights",
    )(side, *inputs)


class Sum:
    def __init__(self, value, share, halve_all=False, dp_first=False):
        self.phases = sum_phases(dp_first)
        inner = self.phases[1:]
        self.value = value
        self.share = share
        halvings = 0
        most = len(inner) - (0 if halve_all else 1)
        while halvings < most and value.shape[0] >> (halvings + 1) >= 16:
            halvings += 1
        self.halved = inner[:halvings]
        self.steps = [("halve", phase) for phase in self.halved]
        self.steps += [("add", phase) for phase in inner[halvings:]]
        self.steps += [("double", phase) for phase in reversed(self.halved)]
        self.steps += [("last", self.phases[0])]
        self.started = None

    def prepare(self):
        kind, phase = self.steps.pop(0)
        if kind == "halve":
            bit = phase_bit(phase)
            value = self.value
            self.sent, self.value = half_of(value, 1 - bit), half_of(value, bit)
            if self.share is not None:
                self.sent = self.sent + half_of(self.share, 1 - bit)
                self.value = self.value + half_of(self.share, bit)
        else:
            if self.share is not None:
                self.value = self.value + self.share
            self.sent = self.value
        self.share = None
        self.ready = (kind, phase)

    def launch(self):
        kind, phase = self.ready
        if kind == "last" and isinstance(self.sent, tuple):
            self.started = (kind, tuple(phase_swap(piece, phase) for piece in self.sent))
        else:
            self.started = (kind, phase_swap(self.sent, phase))

    def finish(self, *after):
        kind, other = self.started
        self.started = None
        other, after = lax.optimization_barrier((other, after))
        if kind in ("halve", "add"):
            self.value = self.value + other
        elif kind == "double" and len(self.steps) == 1:
            self.value = (self.value, other)
        elif kind == "double":
            self.value = jnp.concatenate([self.value, other], axis=0)
        elif isinstance(other, tuple):
            self.value = (self.value, other)
        else:
            self.value = ((self.value,), (other,))
        return list(after)

    def places(self):
        own = sum(phase_bit(phase) << at for at, phase in enumerate(reversed(self.halved)))
        swapped = [(late, early) for early, late in self.halved]
        other = sum(phase_bit(phase) << at for at, phase in enumerate(reversed(swapped)))
        numbers = jnp.stack([phase_bit(self.phases[0]), jnp.int32(own), jnp.int32(other)])
        return numbers.astype(jnp.int32), 1 << len(self.halved)


def advance(totals, *after, extra=()):
    going = []
    for total in totals:
        if total.started is not None:
            total.finish(*after)
        if total.steps:
            total.prepare()
            going.append(total)
    joined, extra = lax.optimization_barrier(([total.sent for total in going], list(extra)))
    for total, sent in zip(going, joined):
        if total.value is total.sent:
            total.value = sent
        total.sent = sent
        total.launch()
    return joined, extra


def unpack_kernel(count, parts, regions, kept, place_ref, *refs):
    own_refs, other_refs, refs = refs[:parts], refs[parts : 2 * parts], refs[2 * parts :]
    gains_ref = None
    if kept:
        gains_ref, refs = refs[0], refs[1:]
    outs = len(refs) // 2
    out_refs, staged, sems = refs[:outs], refs[outs : 2 * outs], refs[2 * outs]
    each = count // parts
    rows = own_refs[0].shape[0] // each
    height = rows * count

    def take(refs, side, number, sem):
        copies = []
        for start, stop, at, top, left in regions[side]:
            for block in range(count):
                target = pl.multiple_of(top + (block ^ place_ref[number]) * rows, rows)
                inner = (block % each) * rows
                value = refs[block // each][inner : inner + rows, start:stop].astype(F32)
                staged[at][pl.ds(target, rows), left : left + stop - start] = value
            if at >= outs - kept:
                continue
            slab = (pl.ds(top, height), pl.ds(left, stop - start))
            copies.append((staged[at].at[slab], out_refs[at].at[slab], sems.at[sem + len(copies)]))
            pltpu.make_async_copy(*copies[-1]).start()
        return copies

    for side in range(2):

        @pl.when(place_ref[0] == side)
        def _():
            copies = take(own_refs, side, 1, 0)
            copies += take(other_refs, 1 - side, 2, len(copies))
            for copy in copies:
                pltpu.make_async_copy(*copy).wait()

    if kept:
        init_ref, total_ref = out_refs[outs - 2 :]
        init_ref[...] = staged[outs - 2][...].T[: init_ref.shape[0], :]
        total_ref[...] = staged[outs - 1][...].T[: total_ref.shape[0], :] / gains_ref[...]


def unpacked(total, regions, shapes, slots=0, gains=None):
    own, other = total.value
    places, count = total.places()
    parts = len(own)
    kept = 0 if gains is None else 2
    vmem = pl.BlockSpec(memory_space=pltpu.VMEM)
    outs = [jax.ShapeDtypeStruct(shape, F32) for shape in shapes[: len(shapes) - kept]]
    specs = [pl.BlockSpec(memory_space=pl.ANY)] * len(outs)
    inputs = [*own, *other]
    if kept:
        inputs.append(gains)
        outs += [jax.ShapeDtypeStruct((rows, shapes[-1][0]), F32) for rows in (slots, gains.shape[0])]
        specs += [vmem] * 2
    return pl.pallas_call(
        lambda *refs: unpack_kernel(count, parts, regions, kept, *refs),
        in_specs=[pl.BlockSpec(memory_space=pltpu.SMEM)] + [vmem] * len(inputs),
        out_specs=specs,
        out_shape=outs,
        scratch_shapes=[pltpu.VMEM(shape, F32) for shape in shapes]
        + [pltpu.SemaphoreType.DMA((len(regions[0]) + len(regions[1]),))],
        compiler_params=pltpu.CompilerParams(vmem_limit_bytes=VMEM_LIMIT),
        cost_estimate=cost(60 if kept else 0.1),
        name="unpack",
    )(places, *inputs)


def pieces_in(value, place):
    parts = [lax.dynamic_index_in_dim(value, place, 0, keepdims=True)]
    sent = []
    for mask in range(1, lax.axis_size("section")):
        sent.append(lax.dynamic_index_in_dim(value, place ^ mask, 0, keepdims=True))
        parts.append(swap_pairs(sent[-1], "section", mask))
    return in_rank_order(jnp.concatenate(parts, axis=0), place), sent, parts[1:]


def in_rank_order(pieces, place):
    count = pieces.shape[0]
    return jnp.stack(
        [lax.dynamic_index_in_dim(pieces, at ^ place, 0, keepdims=False) for at in range(count)]
    )


def sources_in(arrays, place):
    sections = lax.axis_size("section")
    sent = []
    for mask in range(1, sections):
        picked = [lax.dynamic_index_in_dim(a, place ^ mask, 0, keepdims=True) for a in arrays]
        sent.append(jnp.concatenate(picked, axis=1))
    sent = list(lax.optimization_barrier(tuple(sent)))
    pieces = [swap_pairs(value, "section", mask + 1) for mask, value in enumerate(sent)]
    own = len(arrays)

    def choose(at, here):
        yield (at ^ here) == 0, [(number, here) for number in range(own)]
        for other in range(1, sections):
            yield (at ^ here) == other, [(own + other - 1, 0)]

    return Sources(list(arrays) + pieces, choose), pieces, sent


def gathered_sources(arrays, chunks):
    rows = gathered_in(jnp.concatenate(arrays, axis=1), chunks)
    return Sources([rows], lambda at, here: [(at >= 0, [(0, at)])])


def gathered_in(value, chunks):
    place = lax.axis_index("section")
    gathered = lax.all_gather(value, "section")
    own = lax.dynamic_index_in_dim(gathered, place // chunks, 1, keepdims=False)
    count = gathered.shape[0] // chunks
    return lax.dynamic_slice_in_dim(own, (place % chunks) * count, count, 0)


def gathered_out(value, chunks):
    place = lax.axis_index("section")
    gathered = lax.all_gather(value, "section")
    sections = gathered.shape[0]
    by_stream = gathered.reshape((sections // chunks, chunks * value.shape[0]) + value.shape[1:])
    return lax.dynamic_index_in_dim(by_stream, place, 1, keepdims=False)


def tied(value, *others):
    return lax.optimization_barrier((value,) + others)[0]


def body(
    tokens,
    doc_ids,
    reset_flags,
    attn_gain,
    w_qkv,
    w_attn_out,
    ffn_gain,
    w_in,
    w_out,
    write_gain,
    w_write,
    w_write_out,
    init_memory,
    out_grad,
    memory_grad,
):
    streams, _, seg, width = tokens.shape
    slots = init_memory.shape[0]
    sections = lax.axis_size("section")
    chunks = sections // streams
    segs = sections // chunks
    place = lax.axis_index("section")

    spread = np.tile(np.eye(slots, dtype=np.float32), (1, HEADS))
    consts = dict(
        segs=segs,
        seg=seg,
        init=init_memory,
        gains=jnp.stack([attn_gain, ffn_gain, write_gain]).astype(F32),
        spread=jnp.asarray(spread, BF16),
        fold=jnp.asarray(spread.T, BF16),
    )
    w = dict(
        qkv=w_qkv,
        ao=w_attn_out,
        out=w_out,
        write=w_write,
        wo=w_write_out,
        qkv_t=w_qkv.T,
        ao_t=w_attn_out.T,
        in_t=w_in.T,
        write_t=w_write.T,
        wo_t=w_write_out.T,
    )
    w["in"] = w_in

    marks = jnp.concatenate(
        [doc_ids[:, 0], jnp.broadcast_to(reset_flags, (streams, seg))], axis=1
    ).reshape(streams, 2, seg)
    marks = jnp.pad(marks, ((0, 0), (0, 14), (0, 0))).astype(BF16)
    parts_in = [tokens[:, 0], marks]
    grads_in = [out_grad[:, 0], memory_grad[:, 0]]
    empty = jnp.zeros((width, slots), BF16)
    if chunks == 1:
        rows, pieces, _ = sources_in(parts_in, place)
        gout, _, sent = sources_in([tied(value, *pieces) for value in grads_in], place)
        xor = place
    else:
        rows = gathered_sources(parts_in, chunks)
        gout = gathered_sources(grads_in, chunks)
        sent = []
        xor = 0
    xor = jnp.full((1,), xor, jnp.int32)

    arriving = empty
    then = tied(xor, *sent)
    for turn in range(chunks):
        kept = forward_chain(rows, then, arriving, consts, w)
        if turn < chunks - 1:
            arriving = lax.ppermute(
                kept["last"], "section", [(i, i + 1) for i in range(sections - 1)]
            )
    if chunks == 1:
        done, sent, pieces = pieces_in(kept["enc"], place)
        then = tied(xor, *sent)
    else:
        done = gathered_out(kept["enc"], chunks)
        pieces = []
        then = xor

    returning = empty
    for turn in range(chunks):
        grads = backward_chain(kept, gout, then, returning, consts, w)
        if turn < chunks - 1:
            returning = lax.ppermute(
                grads["sent"], "section", [(i + 1, i) for i in range(sections - 1)]
            )

    ff = w_in.shape[1]
    folds = ff // width
    cores = sum_phases()[0]
    side = phase_bit(cores).reshape(1)
    grads = dict(grads, gu=tied(grads['gu'], *pieces))
    sent = early_weights(kept, grads, 1 - side)
    shares = [phase_swap(value, cores) for value in sent]
    halves = early_weights(kept, grads, tied(side, *sent))
    ffn = Sum(halves[0], shares[0], halve_all=True)
    write = Sum(halves[1], shares[1], dp_first=True)
    groups = [ffn, write]
    after, _ = advance(groups)
    turns = [[2], [0, 3], [1]] if segs == 4 else [[at] for at in range(segs)]
    gqkv = None
    gain_parts = []
    outgoing, incoming = {}, {}
    leaving, arriving = [], []
    for turn in turns:
        which = tied(jnp.concatenate([xor ^ at for at in turn]), *after, *arriving)
        gqkv, out, part = attention_back(kept, grads, which, consts, w, gqkv)
        gain_parts.append(part)
        after, (out,) = advance(groups, part, extra=[out])
        arriving, leaving = leaving, []
        for number, at in enumerate(turn):
            outgoing[at] = out[number : number + 1]
            if chunks == 1 and at:
                incoming[at] = swap_pairs(outgoing[at], "section", at)
                leaving.append(incoming[at])

    sent = late_weights(kept, grads, gqkv, gain_parts, tied(1 - side, *after, *arriving))
    after, (sent,) = advance(groups, sent, extra=[sent])
    share = phase_swap(sent, cores)
    mine = tied(side, sent, *after, *leaving)
    late = Sum(late_weights(kept, grads, gqkv, gain_parts, mine), share)

    half = ff // 2

    def paired(number, start, at):
        main = (start, start + width, at, 0, (1 + number) * width)
        other = (start + width, start + 2 * width, at + number, 0, 0)
        return [main, other]

    ffn_regions = [
        [(0, half, 0, 0, number * half)]
        + [
            (half + at * width, half + (at + 1) * width, 1, number * half + at * width, 0)
            for at in range(half // width)
        ]
        for number in range(2)
    ]
    write_regions = [paired(number, 0, 0) for number in range(2)]
    late_regions = [
        paired(number, 0, 0) + [(2 * width, 2 * width + 128, 2 + number, 0, 0)]
        for number in range(2)
    ]
    square, triple = (width, width), (width, 3 * width)
    advance([late])
    advance(groups, late.sent)
    if chunks == 1:
        incoming[0] = tied(outgoing[0], late.sent)
        back = in_rank_order(jnp.concatenate([incoming[at] for at in range(segs)]), place)
    else:
        back = gathered_out(jnp.concatenate([outgoing[at] for at in range(segs)]), chunks)
    (token_grads,) = late.finish(back.astype(F32))
    advance([late])
    advance(groups, late.sent)
    (done,) = late.finish(done)
    advance([late])
    advance([late])
    advance([ffn], late.sent)
    advance([late])
    advance([write], late.sent)
    advance([late])
    while ffn.steps or write.steps:
        advance(groups, late.sent)
    if late.steps:
        advance([late])
    advance(groups, late.sent)
    grad_write, grad_wo = unpacked(write, write_regions, [triple, square])
    grad_in, grad_out = unpacked(ffn, ffn_regions, [(width, ff), (ff, width)])
    grad_in, grad_write = late.finish(grad_in, grad_write)
    while late.steps:
        advance([late])
    if late.started is not None:
        late.finish()
    grad_qkv, grad_ao, grad_init, gains = unpacked(
        late, late_regions, [triple, square, (width, 128), (width, 128)], slots, consts["gains"]
    )
    return (
        done[:, None, :seg],
        done[:, None, seg:],
        token_grads[:, None],
        gains[0],
        grad_qkv,
        grad_ao,
        gains[1],
        grad_in,
        grad_out,
        gains[2],
        grad_write,
        grad_wo,
        grad_init,
    )


def solution(mesh):
    local = P("dp", "section")
    return jax.shard_map(
        body,
        mesh=mesh,
        in_specs=(local,) * 3 + (P(),) * 10 + (local,) * 2,
        out_specs=(local,) * 3 + (P(),) * 10,
        check_vma=False,
    )
```

```python
import jax
import jax.numpy as jnp
import numpy as np
from jax import lax
from jax.experimental import pallas as pl
from jax.experimental.pallas import tpu as pltpu
from jax.sharding import PartitionSpec as P

HEADS = 8
HEAD_DIM = 64
EPS = 1e-06
MASKED = -1000000000.0
F32 = jnp.float32
BF16 = jnp.bfloat16
SQRT_2_PI = 0.7978845608028654
CUBIC = 0.044715
VMEM_LIMIT = 60 * 1024 * 1024


def nn(left, right):
    return lax.dot_general(left, right, (((1,), (0,)), ((), ())), preferred_element_type=F32)


def tn(left, right):
    return lax.dot_general(left, right, (((0,), (0,)), ((), ())), preferred_element_type=F32)


def nt(left, right):
    return lax.dot_general(left, right, (((1,), (1,)), ((), ())), preferred_element_type=F32)


def wide(column_tile, width):
    copies = max(1, width // 128)
    if width < 128:
        return column_tile[:, :width]
    return jnp.concatenate([column_tile] * copies, axis=1)


def inverse_rms(values):
    return lax.rsqrt(jnp.mean(values * values, axis=0, keepdims=True) + EPS)


def lane_sums(values):
    total = values[:, :128]
    for at in range(128, values.shape[1], 128):
        total = total + values[:, at : at + 128]
    return total


def head_mask(rows, columns):
    row_head = lax.broadcasted_iota(jnp.int32, (rows, columns), 0) // HEAD_DIM
    column_head = lax.broadcasted_iota(jnp.int32, (rows, columns), 1) // HEAD_DIM
    return row_head == column_head


def spread_slots(values):
    pair = jnp.concatenate([values, values], axis=1)
    return jnp.concatenate([pair] * (HEADS // 2), axis=1)


def fold_slots(values):
    total = lane_sums(values)
    half = total.shape[1] // 2
    return total[:, :half] + total[:, half:]


def norm_back(grad_normed, normed, scale, gain, gain_inverse):
    weighed = grad_normed * normed
    mean = jnp.mean(weighed, axis=0, keepdims=True)
    return scale * (grad_normed * gain - normed * gain_inverse * mean), weighed


def gain_tiles(gains_ref, count=3):
    tiles = []
    for at in range(count):
        row = gains_ref[at : at + 1, :]
        tiles.append(jnp.broadcast_to(row, (128, row.shape[1])).T)
    return tiles


class Sources:
    def __init__(self, arrays, choices):
        self.arrays = arrays
        self.choices = choices

    def start(self, refs, at, place, buffer, sem):
        for condition, parts in self.choices(at, place):

            @pl.when(condition)
            def _():
                top = 0
                for number, index in parts:
                    source = refs[number].at[index]
                    target = buffer.at[pl.ds(top, source.shape[0]), :]
                    pltpu.make_async_copy(source, target, sem).start()
                    top += source.shape[0]

    def wait(self, buffer, sem):
        pltpu.make_async_copy(buffer, buffer, sem).wait()

    def rows_of(self, refs, steps, segment, place, buffer, sems):
        step = pl.program_id(0)
        slot = lax.rem(step, 2)

        @pl.when(step == 0)
        def _():
            self.start(refs, segment(0), place, buffer.at[0], sems.at[0])

        if steps > 1:

            @pl.when(step + 1 < steps)
            def _():
                self.start(refs, segment(step + 1), place, buffer.at[1 - slot], sems.at[1 - slot])

        self.wait(buffer.at[slot], sems.at[slot])
        return buffer.at[slot]


def forward_kernel(
    sources,
    segs,
    place_ref,
    mem0_ref,
    init_ref,
    gains_ref,
    spread_ref,
    fold_ref,
    *refs,
):
    wqkv_ref, wao_ref, win_ref, wout_ref, ww_ref, wwo_ref = refs[:6]
    refs = refs[6:]
    (
        enc_ref,
        a1_ref,
        a1m_ref,
        q_ref,
        kt_ref,
        ktm_ref,
        v_ref,
        vm_ref,
        e_ref,
        em_ref,
        att_ref,
        a2_ref,
        z_ref,
        gp_ref,
        a3_ref,
        a3m_ref,
        qw_ref,
        kwt_ref,
        kwtm_ref,
        vw_ref,
        vwm_ref,
        ew_ref,
        ewm_ref,
        watt_ref,
        stat_ref,
        last_ref,
        carry,
        bias,
        k_nat,
        km_nat,
        vt,
        vtm,
        hidden,
        row_buffer,
        row_sems,
    ) = refs[-35:]
    step = pl.program_id(0)
    rows_ref = sources.rows_of(
        refs[: len(sources.arrays)], segs, lambda s: s, place_ref[0], row_buffer, row_sems
    )
    width = wao_ref.shape[0]
    seg = q_ref.shape[2]
    slots = init_ref.shape[0]
    ff = win_ref.shape[0]

    @pl.when(step == 0)
    def _():
        carry[...] = mem0_ref[...].astype(F32)

    docs = rows_ref[seg : seg + 1, :].astype(F32)
    flag = rows_ref[seg + 1 : seg + 2, :].astype(F32)
    stat_ref[0, 5:6, :] = flag
    mem = jnp.where(flag[:, :slots] > 0.0, init_ref[...].astype(F32).T, carry[...])
    ga, gf, gw = gain_tiles(gains_ref)

    doc_rows = jnp.broadcast_to(docs, (128, seg)).T
    for at in range(0, seg, 128):
        bias[:, at : at + 128] = jnp.where(doc_rows == docs[:, at : at + 128], 0.0, MASKED)

    tokens = rows_ref[:seg, :].astype(F32).T
    r1 = inverse_rms(tokens)
    a1_ref[...] = (tokens * r1 * wide(ga, seg)).astype(BF16)
    rm = inverse_rms(mem)
    a1m_ref[0] = (mem * rm * ga[:, :slots]).astype(BF16)
    stat_ref[0, 0:1, :] = r1
    stat_ref[0, 4:5, :slots] = rm

    a1 = a1_ref[...]
    a1m = a1m_ref[0]
    q_ref[0] = (nn(wqkv_ref[:width, :], a1) * HEAD_DIM**-0.5).astype(BF16)
    kt = nn(wqkv_ref[width : 2 * width, :], a1).astype(BF16)
    kt_ref[0] = kt
    k_nat[...] = kt.T
    vt[...] = nn(wqkv_ref[2 * width :, :], a1).astype(BF16)
    v_ref[0] = vt[...].T
    ktm = nn(wqkv_ref[width : 2 * width, :], a1m).astype(BF16)
    ktm_ref[0] = ktm
    km_nat[...] = ktm.T
    vtm[...] = nn(wqkv_ref[2 * width :, :], a1m).astype(BF16)
    vm_ref[0] = vtm[...].T

    def pair(index, unused):
        lanes = pl.ds(pl.multiple_of(index * 128, 128), 128)
        keys = k_nat[:, lanes]
        mem_keys = km_nat[:, lanes]
        for half in range(2):
            head = index * 2 + half
            rows = pl.ds(pl.multiple_of(head * HEAD_DIM, HEAD_DIM), HEAD_DIM)
            queries = q_ref[0, rows, :]
            blank = jnp.zeros_like(queries)
            queries = jnp.concatenate([queries, blank] if half == 0 else [blank, queries], axis=0)
            scores = nn(keys, queries) + bias[...]
            mem_scores = nn(mem_keys, queries)
            top = jnp.maximum(
                jnp.max(scores, axis=0, keepdims=True), jnp.max(mem_scores, axis=0, keepdims=True)
            )
            raised = jnp.exp(scores - top)
            mem_raised = jnp.exp(mem_scores - top)
            inverse = 1.0 / (
                jnp.sum(raised, axis=0, keepdims=True) + jnp.sum(mem_raised, axis=0, keepdims=True)
            )
            raised = raised.astype(BF16)
            mem_raised = mem_raised.astype(BF16)
            e_ref[0, head] = raised
            em_ref[0, rows, :] = mem_raised
            mixed = nn(vt[rows, :], raised) + nn(vtm[rows, :], mem_raised)
            att_ref[rows, :] = (mixed * inverse).astype(BF16)
            stat_ref[0, pl.ds(8 + head, 1), :] = inverse
        return unused

    lax.fori_loop(0, HEADS // 2, pair, 0, unroll=HEADS // 2)

    h1 = rows_ref[:seg, :].astype(F32).T + nn(wao_ref[...], att_ref[...])
    r2 = inverse_rms(h1)
    stat_ref[0, 1:2, :] = r2
    a2_ref[...] = (h1 * r2 * wide(gf, seg)).astype(BF16)
    hidden[...] = h1
    a2 = a2_ref[...]
    for at in range(0, ff, 512):
        upper = nn(win_ref[at : at + 512, :], a2)
        square = upper * upper
        bent = jnp.tanh(upper * (SQRT_2_PI + (SQRT_2_PI * CUBIC) * square))
        cdf = 0.5 + 0.5 * bent
        z_ref[at : at + 512, :] = (upper * cdf).astype(BF16)
        slope = (0.5 * SQRT_2_PI) + (1.5 * SQRT_2_PI * CUBIC) * square
        gp_ref[0, at : at + 512, :] = (cdf + upper * (1.0 - bent * bent) * slope).astype(BF16)
    enc = hidden[...] + tn(wout_ref[...], z_ref[...])
    enc_ref[0, :seg, :] = enc.T.astype(BF16)
    r3 = inverse_rms(enc)
    stat_ref[0, 2:3, :] = r3
    a3_ref[...] = (enc * r3 * wide(gw, seg)).astype(BF16)
    a3m_ref[0] = (mem * rm * gw[:, :slots]).astype(BF16)
    a3 = a3_ref[...]
    a3m = a3m_ref[0]

    kwt = nn(ww_ref[width : 2 * width, :], a3).astype(BF16)
    kwt_ref[0] = kwt
    kw = kwt.T
    vwt = nn(ww_ref[2 * width :, :], a3).astype(BF16)
    vw_ref[0] = vwt.T
    kwtm = nn(ww_ref[width : 2 * width, :], a3m).astype(BF16)
    kwtm_ref[0] = kwtm
    vwtm = nn(ww_ref[2 * width :, :], a3m).astype(BF16)
    vwm_ref[0] = vwtm.T
    qwt = (nn(ww_ref[:width, :], a3m) * HEAD_DIM**-0.5).astype(BF16)
    own = head_mask(width, HEADS * slots)
    qw = jnp.where(own, nn(qwt, spread_ref[...]), 0.0).astype(BF16)
    qw_ref[0] = qw
    scores = nn(kw, qw)
    mem_scores = nn(kwtm.T, qw)
    slot_row = lax.broadcasted_iota(jnp.int32, mem_scores.shape, 0)
    slot_col = lax.broadcasted_iota(jnp.int32, mem_scores.shape, 1) % slots
    mem_scores = jnp.where(slot_row == slot_col, mem_scores, MASKED)
    top = jnp.maximum(
        jnp.max(scores, axis=0, keepdims=True), jnp.max(mem_scores, axis=0, keepdims=True)
    )
    raised = jnp.exp(scores - top)
    mem_raised = jnp.exp(mem_scores - top)
    inverse = 1.0 / (
        jnp.sum(raised, axis=0, keepdims=True) + jnp.sum(mem_raised, axis=0, keepdims=True)
    )
    stat_ref[0, 3:4, :] = inverse
    raised = raised.astype(BF16)
    mem_raised = mem_raised.astype(BF16)
    ew_ref[0] = raised
    ewm_ref[0] = mem_raised
    mixed = (nn(vwt, raised) + nn(vwtm, mem_raised)) * inverse
    watt = fold_slots(jnp.where(own, mixed, 0.0)).astype(BF16)
    watt_ref[0] = watt
    new_mem = (mem + nn(wwo_ref[...], watt)).astype(BF16).astype(F32)
    carry[...] = new_mem
    enc_ref[0, seg:, :] = new_mem.T.astype(BF16)
    last_ref[...] = new_mem.astype(BF16)


def chain_kernel(
    sources,
    segs,
    place_ref,
    carry0_ref,
    weights_gains_ref,
    wwo_ref,
    ww_ref,
    wout_ref,
    win_ref,
    wao_ref,
    wqkv_ref,
    a1m_ref,
    q_ref,
    vm_ref,
    em_ref,
    att_ref,
    a2_ref,
    gp_ref,
    a3_ref,
    a3m_ref,
    qw_ref,
    kwt_ref,
    kwtm_ref,
    vw_ref,
    vwm_ref,
    ew_ref,
    ewm_ref,
    stat_ref,
    *refs,
):
    source_refs, refs = refs[: len(sources.arrays)], refs[len(sources.arrays) :]
    bm_ref, gwkv_ref, gwm_ref, bf_ref, gu_ref, ba_ref, gh_ref, do_ref, dd_ref, dsm_ref = refs[:10]
    gkvm_ref, init_ref, gains_ref, sent_ref, carry, grad_buffer, grad_sems = refs[10:]
    gout_ref = sources.rows_of(
        source_refs, segs, lambda s: segs - 1 - s, place_ref[0], grad_buffer, grad_sems
    )
    step = pl.program_id(0)
    width = wao_ref.shape[0]
    ff = wout_ref.shape[0]
    seg = q_ref.shape[2]
    slots = a1m_ref.shape[2]
    reset = stat_ref[0, 5:6, :slots] > 0.0

    @pl.when(step == 0)
    def _():
        carry[...] = carry0_ref[...].astype(F32)
        init_ref[...] = jnp.zeros_like(init_ref)
        gains_ref[...] = jnp.zeros_like(gains_ref)

    ga, gf, gw = gain_tiles(weights_gains_ref)
    gai, gfi, gwi = 1.0 / ga, 1.0 / gf, 1.0 / gw
    own = head_mask(width, HEADS * slots)
    rm = stat_ref[0, 4:5, :slots]

    grad_mem = gout_ref[seg:, :].astype(F32).T + carry[...]
    branch_mem = grad_mem.astype(BF16)
    bm_ref[0] = branch_mem
    grad_watt = nn(wwo_ref[...], branch_mem).astype(BF16)
    inverse = stat_ref[0, 3:4, :]
    scaled = (jnp.where(own, spread_slots(grad_watt.astype(F32)), 0.0) * inverse).astype(BF16)
    raised = ew_ref[0].astype(F32)
    mem_raised = ewm_ref[0].astype(F32)
    grad_probs = nn(vw_ref[0], scaled)
    mem_grad_probs = nn(vwm_ref[0], scaled)
    dots = (
        jnp.sum(raised * grad_probs, axis=0, keepdims=True)
        + jnp.sum(mem_raised * mem_grad_probs, axis=0, keepdims=True)
    ) * inverse
    grad_scores = (raised * (grad_probs - dots)).astype(BF16)
    mem_grad_scores = (mem_raised * (mem_grad_probs - dots)).astype(BF16)
    gwkv_ref[:width, :] = nt(qw_ref[0], grad_scores).astype(BF16)
    gwkv_ref[width:, :] = nt(scaled, ew_ref[0]).astype(BF16)
    grad_q = (nn(kwt_ref[0], grad_scores) + nn(kwtm_ref[0], mem_grad_scores)) * HEAD_DIM**-0.5
    gwm_ref[0, :width, :] = fold_slots(jnp.where(own, grad_q, 0.0)).astype(BF16)
    gwm_ref[0, width : 2 * width, :] = nt(qw_ref[0], mem_grad_scores).astype(BF16)
    gwm_ref[0, 2 * width :, :] = nt(scaled, ewm_ref[0]).astype(BF16)

    grad_a3 = nn(ww_ref[:, width:], gwkv_ref[...])
    grad_a3m = nn(ww_ref[...], gwm_ref[0])
    part, weighed = norm_back(
        grad_a3, a3_ref[...].astype(F32), stat_ref[0, 2:3, :], wide(gw, seg), wide(gwi, seg)
    )
    mem_part, mem_weighed = norm_back(
        grad_a3m, a3m_ref[0].astype(F32), rm, gw[:, :slots], gwi[:, :slots]
    )
    gains_ref[2] += lane_sums(weighed)
    gains_ref[2, :, :slots] += mem_weighed
    grad_mem_in = grad_mem + mem_part
    gh_ref[0] = gout_ref[:seg, :].astype(F32).T + part

    bf_ref[...] = gh_ref[0].astype(BF16)
    branch = bf_ref[...]
    for at in range(0, ff, 512):
        grad_z = nn(wout_ref[at : at + 512, :], branch)
        gu_ref[at : at + 512, :] = (grad_z * gp_ref[0, at : at + 512, :].astype(F32)).astype(BF16)
    grad_a2 = nn(win_ref[...], gu_ref[...])
    part, weighed = norm_back(
        grad_a2, a2_ref[...].astype(F32), stat_ref[0, 1:2, :], wide(gf, seg), wide(gfi, seg)
    )
    gains_ref[1] += lane_sums(weighed)
    gh_ref[0] += part

    ba_ref[...] = gh_ref[0].astype(BF16)
    grad_att = nn(wao_ref[...], ba_ref[...]).astype(BF16)
    products = grad_att.astype(F32) * att_ref[...].astype(F32)
    rows = []
    dots = []
    for head in range(HEADS):
        span = slice(head * HEAD_DIM, (head + 1) * HEAD_DIM)
        inverse = stat_ref[0, 8 + head : 9 + head, :]
        dots.append(jnp.sum(products[span, :], axis=0, keepdims=True) * inverse)
        rows.append((grad_att[span, :].astype(F32) * inverse).astype(BF16))
    scaled = jnp.concatenate(rows, axis=0)
    do_ref[0] = scaled
    dd_ref[0] = jnp.concatenate(dots, axis=0)
    mem_values = jnp.concatenate([vm_ref[0].astype(F32)] * HEADS, axis=0)
    mem_values = jnp.where(own, mem_values, 0.0).astype(BF16)
    grad_probs = nn(mem_values, scaled)
    parts = []
    for head in range(HEADS):
        span = slice(head * slots, (head + 1) * slots)
        parts.append(
            (em_ref[0, span, :].astype(F32) * (grad_probs[span, :] - dots[head])).astype(BF16)
        )
    grad_scores = jnp.concatenate(parts, axis=0)
    dsm_ref[0] = grad_scores
    grad_k = jnp.where(own, nt(q_ref[0], grad_scores), 0.0)
    grad_v = jnp.where(own, nt(scaled, em_ref[0]), 0.0)
    gkvm_ref[0, :width, :] = fold_slots(grad_k).astype(BF16)
    gkvm_ref[0, width:, :] = fold_slots(grad_v).astype(BF16)
    grad_a1m = nn(wqkv_ref[:, width:], gkvm_ref[0])
    mem_part, mem_weighed = norm_back(
        grad_a1m, a1m_ref[0].astype(F32), rm, ga[:, :slots], gai[:, :slots]
    )
    gains_ref[0, :, :slots] += mem_weighed
    grad_mem_in = grad_mem_in + mem_part
    init_ref[...] += jnp.where(reset, grad_mem_in, 0.0)
    carry[...] = jnp.where(reset, 0.0, grad_mem_in).astype(BF16).astype(F32)
    sent_ref[...] = carry[...].astype(BF16)


def attention_kernel(
    alone,
    place_ref,
    do_ref,
    dd_ref,
    dsm_ref,
    q_ref,
    kt_ref,
    ktm_ref,
    v_ref,
    e_ref,
    stat_ref,
    gains_ref,
    gh_ref,
    a1_ref,
    wqkv_ref,
    *refs,
):
    step = pl.program_id(0)
    copies = []
    if alone:
        gqkv_ref, out_ref, gain_ref, *buffers, sems = refs[-7:]
        place = place_ref[0]
        tokens = gh_ref.shape[2]
        lanes = pl.ds(pl.multiple_of(place * tokens, tokens), tokens)
        sources = [gh_ref.at[pl.ds(place, 1)], a1_ref.at[:, lanes], wqkv_ref]
        for at, (source, target) in enumerate(zip(sources, buffers)):
            copies.append(fetch(source, target, sems.at[at]))
        gh_ref, a1_ref, wqkv_ref = buffers
    else:
        gqkv_ref, out_ref, gain_ref = refs[-3:]
    width = wqkv_ref.shape[0]
    seg = q_ref.shape[2]
    for head in range(HEADS):
        span = slice(head * HEAD_DIM, (head + 1) * HEAD_DIM)
        key_span = slice(width + head * HEAD_DIM, width + (head + 1) * HEAD_DIM)
        value_span = slice(2 * width + head * HEAD_DIM, 2 * width + (head + 1) * HEAD_DIM)
        grads = do_ref[0, span, :]
        blank = jnp.zeros_like(grads)
        padded = jnp.concatenate([grads, blank] if head % 2 == 0 else [blank, grads], axis=0)
        dots = dd_ref[0, head : head + 1, :]
        lanes = slice(head // 2 * 128, head // 2 * 128 + 128)
        grad_probs = nn(v_ref[0, :, lanes], padded)
        inner = (e_ref[0, head].astype(F32) * (grad_probs - dots)).astype(BF16)
        grad_q = nn(kt_ref[0, span, :], inner) + nn(ktm_ref[0, span, :], dsm_ref[0, span, :])
        gqkv_ref[span, :] = (grad_q * HEAD_DIM**-0.5).astype(BF16)
        gqkv_ref[key_span, :] = nt(q_ref[0, span, :], inner).astype(BF16)
        gqkv_ref[value_span, :] = nt(grads, e_ref[0, head]).astype(BF16)

    for copy in copies:
        copy.wait()
    grad_a1 = nn(wqkv_ref[...], gqkv_ref[...])
    (ga,) = gain_tiles(gains_ref, 1)
    part, weighed = norm_back(
        grad_a1,
        a1_ref[...].astype(F32),
        stat_ref[0, 0:1, :],
        wide(ga, seg),
        wide(1.0 / ga, seg),
    )
    gain_ref[...] = jnp.where(step == 0, 0.0, gain_ref[...]) + lane_sums(weighed)
    out_ref[0] = (gh_ref[0] + part).T.astype(BF16)


def whole(array):
    zeros = (0,) * array.ndim
    return pl.BlockSpec(array.shape, lambda *unused: zeros, pipeline_mode=pl.Buffered(1))


def params():
    return pltpu.CompilerParams(dimension_semantics=("arbitrary",), vmem_limit_bytes=VMEM_LIMIT)


def cost(microseconds):
    return pl.CostEstimate(
        flops=int(microseconds * 1e9), bytes_accessed=1 << 20, transcendentals=0
    )


def forward_chain(sources, place, mem0, consts, w):
    segs = consts["segs"]
    seg = consts["seg"]
    width, slots = mem0.shape
    ff = w["in_t"].shape[0]

    def flat(height):
        return (
            jax.ShapeDtypeStruct((height, segs * seg), BF16),
            pl.BlockSpec((height, seg), lambda s, f: (0, s)),
        )

    def stack(*shape, dtype=BF16):
        tail = (0,) * len(shape)
        return (
            jax.ShapeDtypeStruct((segs,) + shape, dtype),
            pl.BlockSpec((1,) + shape, lambda s, f: (s,) + tail),
        )

    outs = dict(
        enc=stack(seg + slots, width),
        a1=flat(width),
        a1m=stack(width, slots),
        q=stack(width, seg),
        kt=stack(width, seg),
        ktm=stack(width, slots),
        v=stack(seg, width),
        vm=stack(slots, width),
        e=stack(HEADS, seg, seg),
        em=stack(HEADS * slots, seg),
        att=flat(width),
        a2=flat(width),
        z=flat(ff),
        gp=stack(ff, seg),
        a3=flat(width),
        a3m=stack(width, slots),
        qw=stack(width, HEADS * slots),
        kwt=stack(width, seg),
        kwtm=stack(width, slots),
        vw=stack(seg, width),
        vwm=stack(slots, width),
        ew=stack(seg, HEADS * slots),
        ewm=stack(slots, HEADS * slots),
        watt=stack(width, slots),
        stat=stack(16, seg, dtype=F32),
        last=(
            jax.ShapeDtypeStruct((width, slots), BF16),
            pl.BlockSpec((width, slots), lambda s, f: (0, 0)),
        ),
    )
    fixed = [
        mem0,
        consts["init"],
        consts["gains"],
        consts["spread"],
        consts["fold"],
    ]
    weights = [w[name] for name in ("qkv_t", "ao_t", "in_t", "out", "write_t", "wo_t")]
    results = pl.pallas_call(
        lambda *refs: forward_kernel(sources, segs, *refs),
        grid_spec=pltpu.PrefetchScalarGridSpec(
            num_scalar_prefetch=1,
            grid=(segs,),
            in_specs=[whole(a) for a in fixed + weights]
            + [pl.BlockSpec(memory_space=pl.ANY)] * len(sources.arrays),
            out_specs=[spec for _, spec in outs.values()],
            scratch_shapes=[
                pltpu.VMEM((width, slots), F32),
                pltpu.VMEM((seg, seg), F32),
                pltpu.VMEM((seg, width), BF16),
                pltpu.VMEM((slots, width), BF16),
                pltpu.VMEM((width, seg), BF16),
                pltpu.VMEM((width, slots), BF16),
                pltpu.VMEM((width, seg), F32),
                pltpu.VMEM((2, seg + 16, width), BF16),
                pltpu.SemaphoreType.DMA((2,)),
            ],
        ),
        out_shape=[shape for shape, _ in outs.values()],
        compiler_params=params(),
        cost_estimate=cost(15 * segs),
        name="forward_chain",
    )(place, *fixed, *weights, *sources.arrays)
    return dict(zip(outs, results))


def backward_chain(kept, sources, place, carry0, consts, w):
    segs = consts["segs"]
    width, slots = kept["a1m"].shape[1:]
    seg = kept["q"].shape[2]
    ff = kept["gp"].shape[1]
    last = segs - 1

    def flat(height):
        return (
            jax.ShapeDtypeStruct((height, segs * seg), BF16),
            pl.BlockSpec((height, seg), lambda s, f: (0, last - s)),
        )

    def stack(*shape, dtype=BF16):
        tail = (0,) * len(shape)
        return (
            jax.ShapeDtypeStruct((segs,) + shape, dtype),
            pl.BlockSpec((1,) + shape, lambda s, f: (last - s,) + tail),
        )

    def single(*shape, dtype=F32):
        tail = (0,) * len(shape)
        return (jax.ShapeDtypeStruct(shape, dtype), pl.BlockSpec(shape, lambda s, f: tail))

    outs = dict(
        bm=stack(width, slots),
        gwkv=flat(2 * width),
        gwm=stack(3 * width, slots),
        bf=flat(width),
        gu=flat(ff),
        ba=flat(width),
        gh=stack(width, seg, dtype=F32),
        do=stack(width, seg),
        dd=stack(HEADS, seg, dtype=F32),
        dsm=stack(HEADS * slots, seg),
        gkvm=stack(2 * width, slots),
        init=single(width, slots),
        gains=single(3, width, 128),
        sent=single(width, slots, dtype=BF16),
    )
    fixed = [
        carry0,
        consts["gains"],
    ]
    weights = [w[name] for name in ("wo", "write", "out", "in", "ao", "qkv")]
    blocked = ["a1m", "q", "vm", "em", "att", "a2", "gp", "a3", "a3m", "qw"]
    blocked += ["kwt", "kwtm", "vw", "vwm", "ew", "ewm", "stat"]

    def spec_of(array):
        if array.ndim == 2:
            return pl.BlockSpec((array.shape[0], seg), lambda s, f: (0, last - s))
        tail = (0,) * (array.ndim - 1)
        return pl.BlockSpec((1,) + array.shape[1:], lambda s, f: (last - s,) + tail)

    results = pl.pallas_call(
        lambda *refs: chain_kernel(sources, segs, *refs),
        grid_spec=pltpu.PrefetchScalarGridSpec(
            num_scalar_prefetch=1,
            grid=(segs,),
            in_specs=[whole(a) for a in fixed + weights]
            + [spec_of(kept[name]) for name in blocked]
            + [pl.BlockSpec(memory_space=pl.ANY)] * len(sources.arrays),
            out_specs=[spec for _, spec in outs.values()],
            scratch_shapes=[
                pltpu.VMEM((width, slots), F32),
                pltpu.VMEM((2, seg + slots, width), BF16),
                pltpu.SemaphoreType.DMA((2,)),
            ],
        ),
        out_shape=[shape for shape, _ in outs.values()],
        compiler_params=params(),
        cost_estimate=cost(11 * segs),
        name="backward_chain",
    )(place, *fixed, *weights, *[kept[name] for name in blocked], *sources.arrays)
    return dict(zip(outs, results))


def attention_back(kept, grads, which, consts, w, before):
    segs, width, seg = kept["q"].shape
    count = which.shape[0]

    def by_seg(array):
        if array.ndim == 2:
            return pl.BlockSpec((array.shape[0], seg), lambda s, f: (0, f[s]))
        tail = (0,) * (array.ndim - 1)
        return pl.BlockSpec((1,) + array.shape[1:], lambda s, f: (f[s],) + tail)

    alone = count == 1
    blocked = [grads[name] for name in ("do", "dd", "dsm")]
    blocked += [kept[name] for name in ("q", "kt", "ktm", "v", "e", "stat")]
    inputs = [(array, by_seg(array)) for array in blocked]
    inputs.append((consts["gains"], whole(consts["gains"])))
    last = [grads["gh"], kept["a1"], w["qkv"]]
    scratch = []
    if alone:
        inputs += [(array, pl.BlockSpec(memory_space=pl.ANY)) for array in last]
        scratch = [
            pltpu.VMEM((1, width, seg), F32),
            pltpu.VMEM((width, seg), BF16),
            pltpu.VMEM(w["qkv"].shape, BF16),
            pltpu.SemaphoreType.DMA((3,)),
        ]
    else:
        inputs += [(array, by_seg(array)) for array in last[:2]] + [(last[2], whole(last[2]))]
    passed = [] if before is None else [before]
    return pl.pallas_call(
        lambda *refs: attention_kernel(alone, *refs),
        grid_spec=pltpu.PrefetchScalarGridSpec(
            num_scalar_prefetch=1,
            grid=(count,),
            in_specs=[spec for _, spec in inputs]
            + [pl.BlockSpec(memory_space=pl.ANY)] * len(passed),
            out_specs=[
                pl.BlockSpec((3 * width, seg), lambda s, f: (0, f[s])),
                pl.BlockSpec((1, seg, width), lambda s, f: (s, 0, 0)),
                pl.BlockSpec((width, 128), lambda s, f: (0, 0)),
            ],
            scratch_shapes=scratch,
        ),
        out_shape=[
            jax.ShapeDtypeStruct((3 * width, segs * seg), BF16),
            jax.ShapeDtypeStruct((count, seg, width), BF16),
            jax.ShapeDtypeStruct((width, 128), F32),
        ],
        input_output_aliases={1 + len(inputs): 0} if passed else {},
        compiler_params=params(),
        cost_estimate=cost(10 * count),
        name="attention_back",
    )(which, *[array for array, _ in inputs], *passed)


def swap_pairs(value, axis, mask):
    size = lax.axis_size(axis)
    return lax.ppermute(value, axis, [(i, i ^ mask) for i in range(size)])


def sum_phases(dp_first=False):
    section = [("section", 1 << at) for at in range(lax.axis_size("section").bit_length() - 1)]
    dp = [("dp", 1 << at) for at in range(lax.axis_size("dp").bit_length() - 1)]
    phases = [(step, step) for step in section[:1]]
    crossed = []
    if len(section) > 1 and dp:
        crossed = [(dp[0], section[1]), (section[1], dp[0])]
        section, dp = section[2:], dp[1:]
    else:
        section = section[1:]
    straight = [(step, step) for step in dp + section]
    return phases + (straight + crossed if dp_first else crossed + straight)


def phase_swap(value, phase):
    sections, dps = lax.axis_size("section"), lax.axis_size("dp")
    route = []
    for section in range(sections):
        axis, mask = phase[section % 2]
        for dp in range(dps):
            to = ((section ^ mask) * dps + dp) if axis == "section" else (section * dps + (dp ^ mask))
            route.append((section * dps + dp, to))
    return lax.ppermute(value, ("section", "dp"), route)


def phase_bit(phase):
    bits = [(lax.axis_index(axis) // mask) % 2 for axis, mask in phase]
    return jnp.where(lax.axis_index("section") % 2 == 0, bits[0], bits[1])


def half_of(value, side):
    half = value.shape[0] // 2
    return lax.dynamic_slice_in_dim(value, side * half, half, 0)


def fetch(source, target, sem):
    copy = pltpu.make_async_copy(source, target, sem)
    copy.start()
    return copy


def slot_sum(left, right):
    join = lambda ref: jnp.concatenate([ref[at] for at in range(ref.shape[0])], axis=1)
    return nt(join(left), join(right))


def early_weights_kernel(
    side_ref, a2_ref, gu_ref, bf_ref, z_ref, a3_ref, gwkv_ref, a3m_ref, gwm_ref, watt_ref, bm_ref, *refs
):
    ffn_ref, write_ref, a2, gu, z, bf, a3, gw, a3m, gwm, left, right, staged, in_sems, out_sems = refs
    side = side_ref[0]
    width = a2.shape[0]
    folds = gu.shape[0]
    base = side * (folds * width)
    loads = []

    def load(source, target):
        loads.append(fetch(source, target, in_sems.at[len(loads)]))

    def wait(count):
        for _ in range(count):
            loads[wait.done].wait()
            wait.done += 1

    wait.done = 0
    load(a2_ref, a2)
    for at in range(folds):
        rows = pl.ds(pl.multiple_of(base + at * width, width), width)
        load(gu_ref.at[rows, :], gu.at[at])
    load(bf_ref, bf)
    for at in range(folds):
        rows = pl.ds(pl.multiple_of(base + at * width, width), width)
        load(z_ref.at[rows, :], z.at[at])
    load(a3_ref, a3)
    load(gwkv_ref.at[pl.ds(pl.multiple_of(side * width, width), width), :], gw)
    load(a3m_ref, a3m)
    load(gwm_ref.at[:, pl.ds(pl.multiple_of((1 + side) * width, width), width), :], gwm)
    last = in_sems.at[len(loads)]

    @pl.when(side == 0)
    def _():
        pltpu.make_async_copy(a3m_ref, left, last).start()
        pltpu.make_async_copy(gwm_ref.at[:, pl.ds(0, width), :], right, last).start()

    @pl.when(side == 1)
    def _():
        pltpu.make_async_copy(watt_ref, left, last).start()
        pltpu.make_async_copy(bm_ref, right, last).start()

    stores = []

    def put(tile, value):
        columns = slice(tile * width, (tile + 1) * width)
        staged[:, columns] = value.astype(BF16)
        out, first = (ffn_ref, 0) if tile < 2 * folds else (write_ref, 2 * folds)
        target = out.at[:, pl.ds((tile - first) * width, width)]
        stores.append(fetch(staged.at[:, columns], target, out_sems.at[tile]))

    wait(1)
    for at in range(folds):
        wait(1)
        put(at, nt(a2[...], gu[at]))
    wait(1)
    for at in range(folds):
        wait(1)
        put(folds + at, nt(z[at], bf[...]))
    wait(4)
    put(2 * folds, nt(a3[...], gw[...]) + slot_sum(a3m, gwm))
    pltpu.make_async_copy(watt_ref, left, last).wait()
    pltpu.make_async_copy(bm_ref, right, last).wait()
    put(2 * folds + 1, slot_sum(left, right))
    for store in stores:
        store.wait()


def early_weights(kept, grads, side):
    width, tokens = kept["a2"].shape
    folds = kept["z"].shape[0] // 2 // width
    inputs = [kept["a2"], grads["gu"], grads["bf"], kept["z"], kept["a3"], grads["gwkv"]]
    inputs += [kept["a3m"], grads["gwm"], kept["watt"], grads["bm"]]
    anywhere = pl.BlockSpec(memory_space=pl.ANY)
    full = pltpu.VMEM((width, tokens), BF16)
    several = pltpu.VMEM((folds, width, tokens), BF16)
    slots = pltpu.VMEM(kept["a3m"].shape, BF16)
    out = jax.ShapeDtypeStruct((width, (2 * folds + 2) * width), BF16)
    return pl.pallas_call(
        early_weights_kernel,
        grid_spec=pltpu.PrefetchScalarGridSpec(
            num_scalar_prefetch=1,
            grid=(1,),
            in_specs=[anywhere] * len(inputs),
            out_specs=[anywhere] * 2,
            scratch_shapes=[full, several, several, full, full, full]
            + [slots] * 4
            + [
                pltpu.VMEM(out.shape, BF16),
                pltpu.SemaphoreType.DMA((7 + 2 * folds,)),
                pltpu.SemaphoreType.DMA((2 * folds + 2,)),
            ],
        ),
        out_shape=[
            jax.ShapeDtypeStruct((width, 2 * folds * width), BF16),
            jax.ShapeDtypeStruct((width, 2 * width), BF16),
        ],
        compiler_params=params(),
        cost_estimate=cost(9),
        name="early_weights",
    )(side, *inputs)


def late_weights_kernel(count, side_ref, a1_ref, gqkv_ref, att_ref, ba_ref, a1m_ref, gkvm_ref, *refs):
    init_ref, gains_ref, refs = refs[0], refs[1], refs[2:]
    part_refs, refs = refs[:count], refs[count:]
    out_ref, a1, main, left, right, a1m, gkvm, init, gains, parts, staged, in_sems, out_sems = refs
    side = side_ref[0]
    width = a1.shape[0]
    slots = init.shape[1]
    rows = pl.ds(pl.multiple_of((1 + side) * width, width), width)
    kv_rows = pl.ds(pl.multiple_of(side * width, width), width)
    loads = [
        fetch(a1_ref, a1, in_sems.at[0]),
        fetch(gqkv_ref.at[rows, :], main, in_sems.at[1]),
        fetch(a1m_ref, a1m, in_sems.at[2]),
        fetch(gkvm_ref.at[:, kv_rows, :], gkvm, in_sems.at[3]),
    ]

    @pl.when(side == 0)
    def _():
        pltpu.make_async_copy(a1_ref, left, in_sems.at[4]).start()
        pltpu.make_async_copy(gqkv_ref.at[pl.ds(0, width), :], right, in_sems.at[5]).start()

    @pl.when(side == 1)
    def _():
        pltpu.make_async_copy(att_ref, left, in_sems.at[4]).start()
        pltpu.make_async_copy(ba_ref, right, in_sems.at[5]).start()

    others = [fetch(init_ref, init, in_sems.at[6]), fetch(gains_ref, gains, in_sems.at[7])]
    others += [fetch(ref, parts.at[at], in_sems.at[8 + at]) for at, ref in enumerate(part_refs)]
    stores = []

    def put(columns, value):
        staged[:, columns] = value.astype(BF16)
        stores.append(fetch(staged.at[:, columns], out_ref.at[:, columns], out_sems.at[len(stores)]))

    for load in loads:
        load.wait()
    put(slice(0, width), nt(a1[...], main[...]) + slot_sum(a1m, gkvm))
    pltpu.make_async_copy(att_ref, left, in_sems.at[4]).wait()
    pltpu.make_async_copy(ba_ref, right, in_sems.at[5]).wait()
    put(slice(width, 2 * width), nt(left[...], right[...]))
    for load in others:
        load.wait()
    columns = [gains[0], gains[1], gains[2]]
    for at in range(count):
        columns[0] = columns[0] + parts[at]
    lane = lax.broadcasted_iota(jnp.int32, init.shape, 1)
    extras = jnp.zeros(init.shape, F32)
    for at, column in enumerate(columns):
        extras = jnp.where(lane == at, jnp.sum(column, axis=1, keepdims=True), extras)
    extras = jnp.where(side == 0, init[...], extras)
    extras = jnp.concatenate([extras, jnp.zeros_like(extras)], axis=1)
    put(slice(2 * width, 2 * width + 2 * slots), extras)
    for store in stores:
        store.wait()


def late_weights(kept, grads, gqkv, gain_parts, side):
    width, tokens = kept["a1"].shape
    count = len(gain_parts)
    inputs = [kept["a1"], gqkv, kept["att"], grads["ba"], kept["a1m"], grads["gkvm"]]
    inputs += [grads["init"], grads["gains"]] + list(gain_parts)
    slots = grads["init"].shape[1]
    anywhere = pl.BlockSpec(memory_space=pl.ANY)
    full = pltpu.VMEM((width, tokens), BF16)
    small = pltpu.VMEM(kept["a1m"].shape, BF16)
    out = jax.ShapeDtypeStruct((width, 2 * width + 2 * slots), BF16)
    return pl.pallas_call(
        lambda *refs: late_weights_kernel(count, *refs),
        grid_spec=pltpu.PrefetchScalarGridSpec(
            num_scalar_prefetch=1,
            grid=(1,),
            in_specs=[anywhere] * len(inputs),
            out_specs=anywhere,
            scratch_shapes=[full] * 4
            + [small] * 2
            + [
                pltpu.VMEM(grads["init"].shape, F32),
                pltpu.VMEM(grads["gains"].shape, F32),
                pltpu.VMEM((count,) + gain_parts[0].shape, F32),
                pltpu.VMEM(out.shape, BF16),
                pltpu.SemaphoreType.DMA((8 + count,)),
                pltpu.SemaphoreType.DMA((3,)),
            ],
        ),
        out_shape=out,
        compiler_params=params(),
        cost_estimate=cost(4),
        name="late_weights",
    )(side, *inputs)


class Sum:
    def __init__(self, value, share, halve_all=False, dp_first=False):
        self.phases = sum_phases(dp_first)
        inner = self.phases[1:]
        self.value = value
        self.share = share
        halvings = 0
        most = len(inner) - (0 if halve_all else 1)
        while halvings < most and value.shape[0] >> (halvings + 1) >= 16:
            halvings += 1
        self.halved = inner[:halvings]
        self.steps = [("halve", phase) for phase in self.halved]
        self.steps += [("add", phase) for phase in inner[halvings:]]
        self.steps += [("double", phase) for phase in reversed(self.halved)]
        self.steps += [("last", self.phases[0])]
        self.started = None

    def prepare(self):
        kind, phase = self.steps.pop(0)
        if kind == "halve":
            bit = phase_bit(phase)
            value = self.value
            self.sent, self.value = half_of(value, 1 - bit), half_of(value, bit)
            if self.share is not None:
                self.sent = self.sent + half_of(self.share, 1 - bit)
                self.value = self.value + half_of(self.share, bit)
        else:
            if self.share is not None:
                self.value = self.value + self.share
            self.sent = self.value
        self.share = None
        self.ready = (kind, phase)

    def launch(self):
        kind, phase = self.ready
        if kind == "last" and isinstance(self.sent, tuple):
            self.started = (kind, tuple(phase_swap(piece, phase) for piece in self.sent))
        else:
            self.started = (kind, phase_swap(self.sent, phase))

    def finish(self, *after):
        kind, other = self.started
        self.started = None
        other, after = lax.optimization_barrier((other, after))
        if kind in ("halve", "add"):
            self.value = self.value + other
        elif kind == "double" and len(self.steps) == 1:
            self.value = (self.value, other)
        elif kind == "double":
            self.value = jnp.concatenate([self.value, other], axis=0)
        elif isinstance(other, tuple):
            self.value = (self.value, other)
        else:
            self.value = ((self.value,), (other,))
        return list(after)

    def places(self):
        own = sum(phase_bit(phase) << at for at, phase in enumerate(reversed(self.halved)))
        swapped = [(late, early) for early, late in self.halved]
        other = sum(phase_bit(phase) << at for at, phase in enumerate(reversed(swapped)))
        numbers = jnp.stack([phase_bit(self.phases[0]), jnp.int32(own), jnp.int32(other)])
        return numbers.astype(jnp.int32), 1 << len(self.halved)


def advance(totals, *after, extra=()):
    going = []
    for total in totals:
        if total.started is not None:
            total.finish(*after)
        if total.steps:
            total.prepare()
            going.append(total)
    joined, extra = lax.optimization_barrier(([total.sent for total in going], list(extra)))
    for total, sent in zip(going, joined):
        if total.value is total.sent:
            total.value = sent
        total.sent = sent
        total.launch()
    return joined, extra


def unpack_kernel(count, parts, regions, kept, place_ref, *refs):
    own_refs, other_refs, refs = refs[:parts], refs[parts : 2 * parts], refs[2 * parts :]
    gains_ref = None
    if kept:
        gains_ref, refs = refs[0], refs[1:]
    rows_out = gains_ref.shape[0] if kept else 1
    outs = (len(refs) - rows_out) // 2
    out_refs, staged, sems = refs[: outs + rows_out - 1], refs[outs + rows_out - 1 : -1], refs[-1]
    each = count // parts
    rows = own_refs[0].shape[0] // each
    height = rows * count

    def take(refs, side, number, sem):
        copies = []
        for start, stop, at, top, left in regions[side]:
            for block in range(count):
                target = pl.multiple_of(top + (block ^ place_ref[number]) * rows, rows)
                inner = (block % each) * rows
                value = refs[block // each][inner : inner + rows, start:stop].astype(F32)
                staged[at][pl.ds(target, rows), left : left + stop - start] = value
            if at >= outs - kept:
                continue
            slab = (pl.ds(top, height), pl.ds(left, stop - start))
            copies.append((staged[at].at[slab], out_refs[at].at[slab], sems.at[sem + len(copies)]))
            pltpu.make_async_copy(*copies[-1]).start()
        return copies

    for side in range(2):

        @pl.when(place_ref[0] == side)
        def _():
            copies = take(own_refs, side, 1, 0)
            copies += take(other_refs, 1 - side, 2, len(copies))
            for copy in copies:
                pltpu.make_async_copy(*copy).wait()

    if kept:
        init_ref, total_refs = out_refs[outs - 2], out_refs[outs - 1 :]
        init_ref[...] = staged[outs - 2][...].T[: init_ref.shape[0], :]
        totals = staged[outs - 1][...].T[: gains_ref.shape[0], :] / gains_ref[...]
        for at, ref in enumerate(total_refs):
            ref[...] = totals[at : at + 1, :]


def unpacked(total, regions, shapes, slots=0, gains=None):
    own, other = total.value
    places, count = total.places()
    parts = len(own)
    kept = 0 if gains is None else 2
    vmem = pl.BlockSpec(memory_space=pltpu.VMEM)
    outs = [jax.ShapeDtypeStruct(shape, F32) for shape in shapes[: len(shapes) - kept]]
    specs = [pl.BlockSpec(memory_space=pl.ANY)] * len(outs)
    inputs = [*own, *other]
    if kept:
        inputs.append(gains)
        rows = [slots] + [1] * gains.shape[0]
        outs += [jax.ShapeDtypeStruct((height, shapes[-1][0]), F32) for height in rows]
        specs += [vmem] * len(rows)
    return pl.pallas_call(
        lambda *refs: unpack_kernel(count, parts, regions, kept, *refs),
        in_specs=[pl.BlockSpec(memory_space=pltpu.SMEM)] + [vmem] * len(inputs),
        out_specs=specs,
        out_shape=outs,
        scratch_shapes=[pltpu.VMEM(shape, F32) for shape in shapes]
        + [pltpu.SemaphoreType.DMA((len(regions[0]) + len(regions[1]),))],
        compiler_params=pltpu.CompilerParams(vmem_limit_bytes=VMEM_LIMIT),
        cost_estimate=cost(60 if kept else 0.1),
        name="unpack",
    )(places, *inputs)


def pieces_in(value, place):
    parts = [lax.dynamic_index_in_dim(value, place, 0, keepdims=True)]
    sent = []
    for mask in range(1, lax.axis_size("section")):
        sent.append(lax.dynamic_index_in_dim(value, place ^ mask, 0, keepdims=True))
        parts.append(swap_pairs(sent[-1], "section", mask))
    return in_rank_order(jnp.concatenate(parts, axis=0), place), sent, parts[1:]


def in_rank_order(pieces, place):
    count = pieces.shape[0]
    return jnp.stack(
        [lax.dynamic_index_in_dim(pieces, at ^ place, 0, keepdims=False) for at in range(count)]
    )


def sources_in(arrays, place):
    sections = lax.axis_size("section")
    sent = []
    for mask in range(1, sections):
        picked = [lax.dynamic_index_in_dim(a, place ^ mask, 0, keepdims=True) for a in arrays]
        sent.append(jnp.concatenate(picked, axis=1))
    sent = list(lax.optimization_barrier(tuple(sent)))
    pieces = [swap_pairs(value, "section", mask + 1) for mask, value in enumerate(sent)]
    own = len(arrays)

    def choose(at, here):
        yield (at ^ here) == 0, [(number, here) for number in range(own)]
        for other in range(1, sections):
            yield (at ^ here) == other, [(own + other - 1, 0)]

    return Sources(list(arrays) + pieces, choose), pieces, sent


def gathered_sources(arrays, chunks):
    rows = gathered_in(jnp.concatenate(arrays, axis=1), chunks)
    return Sources([rows], lambda at, here: [(at >= 0, [(0, at)])])


def gathered_in(value, chunks):
    place = lax.axis_index("section")
    gathered = lax.all_gather(value, "section")
    own = lax.dynamic_index_in_dim(gathered, place // chunks, 1, keepdims=False)
    count = gathered.shape[0] // chunks
    return lax.dynamic_slice_in_dim(own, (place % chunks) * count, count, 0)


def gathered_out(value, chunks):
    place = lax.axis_index("section")
    gathered = lax.all_gather(value, "section")
    sections = gathered.shape[0]
    by_stream = gathered.reshape((sections // chunks, chunks * value.shape[0]) + value.shape[1:])
    return lax.dynamic_index_in_dim(by_stream, place, 1, keepdims=False)


def tied(value, *others):
    return lax.optimization_barrier((value,) + others)[0]


def body(
    tokens,
    doc_ids,
    reset_flags,
    attn_gain,
    w_qkv,
    w_attn_out,
    ffn_gain,
    w_in,
    w_out,
    write_gain,
    w_write,
    w_write_out,
    init_memory,
    out_grad,
    memory_grad,
):
    streams, _, seg, width = tokens.shape
    slots = init_memory.shape[0]
    sections = lax.axis_size("section")
    chunks = sections // streams
    segs = sections // chunks
    place = lax.axis_index("section")

    spread = np.tile(np.eye(slots, dtype=np.float32), (1, HEADS))
    consts = dict(
        segs=segs,
        seg=seg,
        init=init_memory,
        gains=jnp.stack([attn_gain, ffn_gain, write_gain]).astype(F32),
        spread=jnp.asarray(spread, BF16),
        fold=jnp.asarray(spread.T, BF16),
    )
    w = dict(
        qkv=w_qkv,
        ao=w_attn_out,
        out=w_out,
        write=w_write,
        wo=w_write_out,
        qkv_t=w_qkv.T,
        ao_t=w_attn_out.T,
        in_t=w_in.T,
        write_t=w_write.T,
        wo_t=w_write_out.T,
    )
    w["in"] = w_in

    marks = jnp.concatenate(
        [doc_ids[:, 0], jnp.broadcast_to(reset_flags, (streams, seg))], axis=1
    ).reshape(streams, 2, seg)
    marks = jnp.pad(marks, ((0, 0), (0, 14), (0, 0))).astype(BF16)
    parts_in = [tokens[:, 0], marks]
    grads_in = [out_grad[:, 0], memory_grad[:, 0]]
    empty = jnp.zeros((width, slots), BF16)
    if chunks == 1:
        rows, pieces, _ = sources_in(parts_in, place)
        gout, _, sent = sources_in([tied(value, *pieces) for value in grads_in], place)
        xor = place
    else:
        rows = gathered_sources(parts_in, chunks)
        gout = gathered_sources(grads_in, chunks)
        sent = []
        xor = 0
    xor = jnp.full((1,), xor, jnp.int32)

    arriving = empty
    then = tied(xor, *sent)
    for turn in range(chunks):
        kept = forward_chain(rows, then, arriving, consts, w)
        if turn < chunks - 1:
            arriving = lax.ppermute(
                kept["last"], "section", [(i, i + 1) for i in range(sections - 1)]
            )
    if chunks == 1:
        done, sent, pieces = pieces_in(kept["enc"], place)
        then = tied(xor, *sent)
    else:
        done = gathered_out(kept["enc"], chunks)
        pieces = []
        then = xor

    returning = empty
    for turn in range(chunks):
        grads = backward_chain(kept, gout, then, returning, consts, w)
        if turn < chunks - 1:
            returning = lax.ppermute(
                grads["sent"], "section", [(i + 1, i) for i in range(sections - 1)]
            )

    ff = w_in.shape[1]
    folds = ff // width
    cores = sum_phases()[0]
    side = phase_bit(cores).reshape(1)
    grads = dict(grads, gu=tied(grads['gu'], *pieces))
    sent = early_weights(kept, grads, 1 - side)
    shares = [phase_swap(value, cores) for value in sent]
    halves = early_weights(kept, grads, tied(side, *sent))
    ffn = Sum(halves[0], shares[0], halve_all=True)
    write = Sum(halves[1], shares[1], dp_first=True)
    groups = [ffn, write]
    after, _ = advance(groups)
    turns = [[2], [0, 3], [1]] if segs == 4 else [[at] for at in range(segs)]
    gqkv = None
    gain_parts = []
    outgoing, incoming = {}, {}
    leaving, arriving = [], []
    for turn in turns:
        which = tied(jnp.concatenate([xor ^ at for at in turn]), *after, *arriving)
        gqkv, out, part = attention_back(kept, grads, which, consts, w, gqkv)
        gain_parts.append(part)
        after, (out,) = advance(groups, part, extra=[out])
        arriving, leaving = leaving, []
        for number, at in enumerate(turn):
            outgoing[at] = out[number : number + 1]
            if chunks == 1 and at:
                incoming[at] = swap_pairs(outgoing[at], "section", at)
                leaving.append(incoming[at])

    sent = late_weights(kept, grads, gqkv, gain_parts, tied(1 - side, *after, *arriving))
    after, (sent,) = advance(groups, sent, extra=[sent])
    share = phase_swap(sent, cores)
    mine = tied(side, sent, *after, *leaving)
    late = Sum(late_weights(kept, grads, gqkv, gain_parts, mine), share)

    half = ff // 2

    def paired(number, start, at):
        main = (start, start + width, at, 0, (1 + number) * width)
        other = (start + width, start + 2 * width, at + number, 0, 0)
        return [main, other]

    ffn_regions = [
        [(0, half, 0, 0, number * half)]
        + [
            (half + at * width, half + (at + 1) * width, 1, number * half + at * width, 0)
            for at in range(half // width)
        ]
        for number in range(2)
    ]
    write_regions = [paired(number, 0, 0) for number in range(2)]
    late_regions = [
        paired(number, 0, 0) + [(2 * width, 2 * width + 128, 2 + number, 0, 0)]
        for number in range(2)
    ]
    square, triple = (width, width), (width, 3 * width)
    advance([late])
    advance(groups, late.sent)
    if chunks == 1:
        incoming[0] = tied(outgoing[0], late.sent)
        back = in_rank_order(jnp.concatenate([incoming[at] for at in range(segs)]), place)
    else:
        back = gathered_out(jnp.concatenate([outgoing[at] for at in range(segs)]), chunks)
    (token_grads,) = late.finish(back.astype(F32))
    advance([late])
    advance(groups, late.sent)
    (done,) = late.finish(done)
    advance([late])
    advance([late])
    advance([ffn], late.sent)
    advance([late])
    advance([write], late.sent)
    advance([late])
    while ffn.steps or write.steps:
        advance(groups, late.sent)
    if late.steps:
        advance([late])
    advance(groups, late.sent)
    grad_write, grad_wo = unpacked(write, write_regions, [triple, square])
    grad_in, grad_out = unpacked(ffn, ffn_regions, [(width, ff), (ff, width)])
    grad_in, grad_write = late.finish(grad_in, grad_write)
    while late.steps:
        advance([late])
    if late.started is not None:
        late.finish()
    grad_qkv, grad_ao, grad_init, *gains = unpacked(
        late, late_regions, [triple, square, (width, 128), (width, 128)], slots, consts["gains"]
    )
    return (
        done[:, None, :seg],
        done[:, None, seg:],
        token_grads[:, None],
        gains[0].reshape(width),
        grad_qkv,
        grad_ao,
        gains[1].reshape(width),
        grad_in,
        grad_out,
        gains[2].reshape(width),
        grad_write,
        grad_wo,
        grad_init,
    )


def solution(mesh):
    local = P("dp", "section")
    return jax.shard_map(
        body,
        mesh=mesh,
        in_specs=(local,) * 3 + (P(),) * 10 + (local,) * 2,
        out_specs=(local,) * 3 + (P(),) * 10,
        check_vma=False,
    )
```
